32 devices in a mesh: section: 2 (over x), row: 4 (over z), col: 4 (over y, core).
Axes of the slice: x: 2, y: 2, z: 4, core: 2. Of those that a mesh axis runs over, the one named last changes fastest.
Arguments:
- x_in: bfloat16 [2, 4, 768, 1024], P(None, 'row', None, 'col'), may hold values from -6 to 6
- targets: bfloat16 [2, 4, 768, 1024], P(None, 'row', None, 'col'), may hold values from -6 to 6
- w_query: bfloat16 [2, 1024, 1024], P('section', 'row', 'col'), may hold values from -0.1875 to 0.1875
- w_key: bfloat16 [2, 1024, 512], P('section', 'row', 'col'), may hold values from -0.1875 to 0.1875
- w_value: bfloat16 [2, 1024, 512], P('section', 'row', 'col'), may hold values from -0.1875 to 0.1875
- w_out: bfloat16 [2, 1024, 1024], P('section', 'col', 'row'), may hold values from -0.75 to 0.75
- w_gate: bfloat16 [2, 32, 1024, 512], P('section', 'col', 'row'), may hold values from -0.1875 to 0.1875
- w_up: bfloat16 [2, 32, 1024, 512], P('section', 'col', 'row'), may hold values from -0.1875 to 0.1875
- w_down: bfloat16 [2, 32, 512, 1024], P('section', 'col', None, 'row'), may hold values from -0.75 to 0.75
- gain_attn: bfloat16 [2, 1024], P('section'), may hold values from 0.5 to 1.5
- gain_ffn: bfloat16 [2, 1024], P('section'), may hold values from 0.5 to 1.5
- expert_ids: int32 [2, 2, 4, 768, 8], P('section', None, 'row'), may hold values from 0 to 31, all different within a row; in each aligned block of 768 rows (0 to 767, 768 to 1535, ..., all dimensions but the last counted through in order) at most 384 rows name the same one
- gates: float32 [2, 2, 4, 768, 8], P('section', None, 'row'), may hold values from 0.06 to 0.2
- lengths: int32 [2, 4], replicated, may hold values from 1 to 512, 1536 in all within a row
Outputs:
- outputs: bfloat16 [2, 2, 4, 768, 1024], P('section', None, 'row', None, 'col')
- loss: float32 [], replicated
- input_grads: bfloat16 [2, 2, 4, 768, 1024], P('section', None, 'row', None, 'col')
- grad_query: float32 [2, 1024, 1024], P('section', 'row', 'col')
- grad_key: float32 [2, 1024, 512], P('section', 'row', 'col')
- grad_value: float32 [2, 1024, 512], P('section', 'row', 'col')
- grad_out: float32 [2, 1024, 1024], P('section', 'col', 'row')
- grad_gate: float32 [2, 32, 1024, 512], P('section', 'col', 'row')
- grad_up: float32 [2, 32, 1024, 512], P('section', 'col', 'row')
- grad_down: float32 [2, 32, 512, 1024], P('section', 'col', None, 'row')
- grad_gain_attn: float32 [2, 1024], P('section', 'col')
- grad_gain_ffn: float32 [2, 1024], P('section', 'col')
The draws below stay inside these ranges and needn't reach their ends.
Inputs may be any that keep to these rules, and one draw needn't show every extreme that they name: `expert_ids`: in each aligned block of 768 rows (one group of one micro-batch at one section) a row names 8 different experts, no expert is named by more than 384 rows, a bound that some block reaches. Each micro-batch's lengths sum to 1536, and its largest is exactly 512.
All inputs are finite; a program needn't handle non-finite values.
Results may differ from the reference program's by a relative error of at most 0.02.
Values may be sent and summed in bfloat16 or wider, within the bound.
No kernel may reach another device: no remote copies, remote signals or barrier semaphores. Data moves between devices by JAX's collectives and lax.ppermute only.
A program may use at most 384 MiB of HBM per device.

```python
import math
import jax
import jax.numpy as jnp
import numpy as np
from jax import lax

D = 1024
QHEADS = 16
KVHEADS = 8
HEAD = 64
HIDDEN_SIZE = 512
EXPERTS = 32
TOPK = 8
MICRO = 2
PROMPT_DEV = 256
CONT_LEN = 512
SECTIONS = 2
GROUPS = 4
PROMPT = 1024
TOK_DEV = 768
CAP = 384
QW = 1024
KW = 512


def level_of(stream_key, extent, pieces, low, high):
    loudness, own = 1.0, jax.random.fold_in(stream_key, 6)
    for position, blocks in pieces:
        draws = jnp.exp(jax.random.uniform(jax.random.fold_in(own, position), (blocks,), jnp.float32, low / len(pieces), high / len(pieces)))
        loudness = loudness * jnp.repeat(draws, extent[position] // blocks).reshape([-1 if axis == position else 1 for axis in range(len(extent))])
    return loudness


def split_up(count, total, reach, slope):
    portions = [(1 << 20) // math.isqrt(standing ** slope) + 1 for standing in range(2, count + 1)]
    spare, given = total - reach - (count - 1), [1] * (count - 1)
    while spare > 0:
        candidates = [i for i in range(count - 1) if given[i] < reach]
        pool, budget = sum([portions[i] for i in candidates]), spare
        for i in candidates:
            addition = min(reach - given[i], max(1, budget * portions[i] // pool), spare)
            given[i] = given[i] + addition
            spare = spare - addition
    return np.array([reach] + given)


def uneven(stream_key, count, total, limit, skew):
    if count == 2:
        one = jax.random.randint(stream_key, (), max(1, total - limit), min(limit, total - 1) + 1)
        return jnp.stack([one, total - one])
    sizes = jnp.asarray(split_up(count, total, limit, skew), jnp.int32)
    pairs = (count - 1) // 2
    donor, taker = sizes[1:1 + 2 * pairs:2], sizes[2:2 + 2 * pairs:2]
    margin = jnp.minimum(donor - 1, limit - taker)
    shifted = jax.random.randint(jax.random.fold_in(stream_key, 1), (pairs,), 0, 1 << 20) % (margin + 1)
    sizes = sizes.at[1:1 + 2 * pairs:2].set(donor - shifted).at[2:2 + 2 * pairs:2].set(taker + shifted)
    return sizes[jax.random.permutation(jax.random.fold_in(stream_key, 2), count)]


def shared_out(key, own, number, rows, count, top, bound, skew):
    order = jax.random.permutation(key, count)
    heavy_load, ordinary = portions_of(count, rows * top, bound, skew, True), portions_of(count, rows * top, bound, skew, False)
    places = jnp.arange(count)

    def named(tallies, rotation):
        used = int((tallies > 0).sum())
        fixed = max(1, used // 4)
        moved = fixed + (places - fixed + rotation * (used - fixed)) % max(1, count - fixed)
        return jnp.zeros((count,), jnp.int32).at[order[jnp.where(places < fixed, places, moved)]].set(jnp.asarray(tallies, jnp.int32))

    tallies = jnp.where(number % 4 == 0, named(heavy_load, number // 4), named(ordinary, number - number // 4 - 1))
    mixed = jax.random.permutation(jax.random.fold_in(own, 3), count)
    source_of, receiver = mixed[0:count // 2 * 2:2], mixed[1:count // 2 * 2:2]
    slack = jnp.minimum(tallies[source_of] - 1, bound - tallies[receiver]) // 2
    slack = jnp.where((source_of == order[0]) | (receiver == order[0]) | (tallies[receiver] == 0), 0, jnp.maximum(slack, 0))
    moved = jax.random.randint(jax.random.fold_in(own, 4), (count // 2,), 0, 1 << 20) % (slack + 1)
    tallies = tallies.at[source_of].add(-moved).at[receiver].add(moved)
    members = jnp.searchsorted(jnp.cumsum(tallies), jnp.arange(rows * top), side="right").astype(jnp.int32)
    listing = members.reshape(top, rows).T
    listing = listing[jax.random.permutation(jax.random.fold_in(own, 1), rows)]
    rotation = jax.random.randint(jax.random.fold_in(own, 2), (rows, 1), 0, top)
    return jnp.take_along_axis(listing, (jnp.arange(top)[None, :] + rotation) % top, axis=1)


def portions_of(count, total, limit, skew, full):
    loads = [(1 << 20) // math.isqrt(grade ** skew) + 1 for grade in range(1, count + 1)]
    largest = limit if full else min(limit, max(-(-total // count), total * loads[0] // sum(loads)))
    least = 1 if total - largest >= count - 1 else 0
    given, surplus = [largest] + [least] * (count - 1), total - largest - least * (count - 1)
    while surplus > 0:
        candidates = [i for i in range(1, count) if given[i] < largest] or [i for i in range(1, count) if given[i] < limit]
        mass, left = sum([loads[i] for i in candidates]), surplus
        for i in candidates:
            extra = min(limit - given[i], max(1, left * loads[i] // mass), surplus)
            given[i] = given[i] + extra
            surplus = surplus - extra
    return np.array(given)


def centred(key, shape, scale, most, split=(), kind=jnp.bfloat16):
    level = level_of(key, shape, split, -0.22, 0.18) if split else 1.0
    values = jax.random.normal(key, shape, jnp.float32) * scale * level
    return jnp.minimum(jnp.maximum(values, -most), most).astype(kind)


def setup_inputs(seed: int = 0) -> dict:
    key_of = jax.random.split(jax.random.key(seed), 15)
    x_in = centred(key_of[0], (MICRO, GROUPS, TOK_DEV, D), 1.0, 6.0, ((1, 4), (3, 4)))
    targets = centred(key_of[1], (MICRO, GROUPS, TOK_DEV, D), 1.0, 6.0, ((1, 4), (3, 4)))
    w_query = centred(key_of[2], (SECTIONS, D, QW), D ** -0.5, 0.1875, ((0, 2), (1, 4), (2, 4)))
    w_key = centred(key_of[3], (SECTIONS, D, KW), D ** -0.5, 0.1875, ((0, 2), (1, 4), (2, 4)))
    w_value = centred(key_of[4], (SECTIONS, D, KW), D ** -0.5, 0.1875, ((0, 2), (1, 4), (2, 4)))
    w_out = centred(key_of[5], (SECTIONS, QW, D), (QW // 16) ** -0.5, 0.75, ((0, 2), (1, 4), (2, 4)))
    w_gate = centred(key_of[6], (SECTIONS, EXPERTS, D, HIDDEN_SIZE), D ** -0.5, 0.1875, ((0, 2), (1, 4), (2, 4)))
    w_up = centred(key_of[7], (SECTIONS, EXPERTS, D, HIDDEN_SIZE), D ** -0.5, 0.1875, ((0, 2), (1, 4), (2, 4)))
    w_down = centred(key_of[8], (SECTIONS, EXPERTS, HIDDEN_SIZE, D), (HIDDEN_SIZE // 8) ** -0.5, 0.75, ((0, 2), (1, 4), (3, 4)))
    gain_attn = jnp.clip(1.0 + 0.1 * jax.random.normal(key_of[9], (SECTIONS, D), jnp.float32), 0.5, 1.5).astype(jnp.bfloat16)
    gain_ffn = jnp.clip(1.0 + 0.1 * jax.random.normal(key_of[10], (SECTIONS, D), jnp.float32), 0.5, 1.5).astype(jnp.bfloat16)
    expert_ids_keys = jax.random.split(jax.random.fold_in(key_of[11], 1), SECTIONS * MICRO * GROUPS * TOK_DEV // TOK_DEV)
    expert_ids_turns = jax.random.permutation(jax.random.fold_in(key_of[11], 3), SECTIONS * MICRO * GROUPS * TOK_DEV // TOK_DEV)
    expert_ids = jax.vmap(lambda own, number: shared_out(jax.random.fold_in(key_of[11], 2), own, number, TOK_DEV, EXPERTS, TOPK, CAP, 1))(expert_ids_keys, expert_ids_turns).reshape((SECTIONS, MICRO, GROUPS, TOK_DEV, TOPK))
    gates = jnp.clip(0.06 + 0.14 * jax.random.uniform(key_of[12], (SECTIONS, MICRO, GROUPS, TOK_DEV, TOPK), jnp.float32) ** level_of(key_of[12], (SECTIONS, MICRO, GROUPS, TOK_DEV, TOPK), ((0, 2), (2, 4)), -0.2, 0.2), 0.06, 0.2)
    lengths = jax.vmap(lambda own: uneven(own, GROUPS, GROUPS * CONT_LEN * 3 // 4, CONT_LEN, 2))(jax.random.split(key_of[13], MICRO)).reshape((MICRO, GROUPS)).astype(jnp.int32)
    return dict(x_in=x_in, targets=targets, w_query=w_query, w_key=w_key, w_value=w_value, w_out=w_out, w_gate=w_gate, w_up=w_up, w_down=w_down, gain_attn=gain_attn, gain_ffn=gain_ffn, expert_ids=expert_ids, gates=gates, lengths=lengths)


EPS = 1e-06
THETA = 10000.0
NEG = -1e+30

@jax.custom_vjp
def low(v):
    return lax.optimization_barrier(v.astype(jnp.bfloat16)).astype(jnp.float32)

@jax.custom_vjp
def low_back(v):
    return v

def low_keep(v):
    return (low(v), None)

def low_pass(kept, grad):
    return (grad,)

def back_keep(v):
    return (v, None)

def back_low(kept, grad):
    return (low(grad),)
low.defvjp(low_keep, low_pass)
low_back.defvjp(back_keep, back_low)

def matmul(left, right):
    return jnp.dot(left, right, precision=lax.Precision.HIGHEST)

def rms_norm(value, gain):
    scale = lax.rsqrt(lax.optimization_barrier(jnp.mean(value * value, axis=-1, keepdims=True)) + EPS)
    return value * scale * gain

def tables(positions):
    freqs = THETA ** (-(jnp.arange(HEAD // 2).astype(jnp.float32) * 2.0) / HEAD)
    angles = positions.astype(jnp.float32)[:, None] * freqs[None, :]
    return (jnp.cos(angles)[:, None, :], jnp.sin(angles)[:, None, :])

def rotate(value, cosine, sine):
    half = value.shape[-1] // 2
    first = value[..., :half]
    second = value[..., half:]
    return jnp.concatenate([first * cosine - second * sine, second * cosine + first * sine], axis=-1)

def row_positions():
    group = jnp.arange(GROUPS, dtype=jnp.int32)[:, None]
    inner = jnp.arange(TOK_DEV, dtype=jnp.int32)[None, :]
    return jnp.where(inner < PROMPT_DEV, group * PROMPT_DEV + inner, PROMPT + inner - PROMPT_DEV)

def experts(normed, w_gate, w_up, w_down, routes, weights_in):
    rows = normed.shape[0]
    slots = GROUPS * CAP
    match = routes[:, :, None] == jnp.arange(EXPERTS, dtype=jnp.int32)[None, None, :]
    member = jnp.any(match, axis=1)
    weight = lax.optimization_barrier(jnp.sum(jnp.where(match, weights_in[:, :, None], 0.0), axis=1))
    place = jnp.cumsum(member.astype(jnp.int32), axis=0) - 1
    slot = jnp.where(member, place, slots)
    index = jnp.zeros((EXPERTS, slots + 1), jnp.int32).at[jnp.arange(EXPERTS, dtype=jnp.int32)[None, :], slot].set(jnp.arange(rows, dtype=jnp.int32)[:, None])[:, :slots]
    counts = lax.optimization_barrier(jnp.sum(member.astype(jnp.int32), axis=0))
    live = jnp.arange(slots, dtype=jnp.int32)[None, :] < counts[:, None]
    slot_gate = jnp.where(live, jnp.take_along_axis(weight.T, index, axis=1), 0.0)

    def expert(operands):
        chosen_rows, gate_weight, up_weight, down_weight = operands
        chosen = normed[chosen_rows]
        gate = low_back(matmul(chosen, gate_weight))
        up = low_back(matmul(chosen, up_weight))
        hidden = low(jax.nn.silu(gate) * up)
        return low_back(matmul(hidden, down_weight))
    results = lax.map(jax.checkpoint(expert), (index, w_gate, w_up, w_down))
    weighted = (results * slot_gate[:, :, None]).reshape(-1, D)
    return jax.ops.segment_sum(weighted, index.reshape(-1), num_segments=rows)

def layer(x, w_query, w_key, w_value, w_out, w_gate, w_up, w_down, gain_first, gain_second, routes, weights_in):
    rows = GROUPS * TOK_DEV
    flat = x.reshape(rows, D)
    normed = low(rms_norm(flat, gain_first))
    query_raw = low_back(matmul(normed, w_query))
    key_raw = low_back(matmul(normed, w_key))
    value_raw = low_back(matmul(normed, w_value))
    positions = row_positions()
    cosine, sine = tables(positions.reshape(rows))
    queries = low(rotate(query_raw.reshape(rows, QHEADS, HEAD), cosine, sine)).reshape(GROUPS, TOK_DEV, QHEADS, HEAD)
    keys = low(rotate(key_raw.reshape(rows, KVHEADS, HEAD), cosine, sine)).reshape(GROUPS, TOK_DEV, KVHEADS, HEAD)
    values = low(value_raw).reshape(GROUPS, TOK_DEV, KVHEADS, HEAD)
    prompt_keys = keys[:, :PROMPT_DEV].reshape(PROMPT, KVHEADS, HEAD)
    prompt_values = values[:, :PROMPT_DEV].reshape(PROMPT, KVHEADS, HEAD)
    key_pos = jnp.concatenate([jnp.arange(PROMPT, dtype=jnp.int32), PROMPT + jnp.arange(CONT_LEN, dtype=jnp.int32)])
    repeat = QHEADS // KVHEADS

    def attend(operands):
        group_queries, group_keys, group_values, group_pos = operands
        all_keys = jnp.repeat(jnp.concatenate([prompt_keys, group_keys[PROMPT_DEV:]], axis=0), repeat, axis=1)
        all_values = jnp.repeat(jnp.concatenate([prompt_values, group_values[PROMPT_DEV:]], axis=0), repeat, axis=1)
        scores = low_back(jnp.einsum('qhd,khd->hqk', group_queries, all_keys, precision=lax.Precision.HIGHEST) * HEAD ** (-0.5))
        allowed = key_pos[None, :] <= group_pos[:, None]
        scores = jnp.where(allowed[None], scores, NEG)
        probs = low(jax.nn.softmax(scores, axis=-1))
        return jnp.einsum('hqk,khd->qhd', probs, all_values, precision=lax.Precision.HIGHEST)
    mixed = lax.map(jax.checkpoint(attend), (queries, keys, values, positions))
    mixed = low(low_back(mixed.reshape(rows, QW)))
    branch = low_back(matmul(mixed, w_out))
    second = flat + branch
    normed_second = low(rms_norm(low(second), gain_second))
    expert_sum = low_back(experts(normed_second, w_gate, w_up, w_down, routes.reshape(rows, TOPK), weights_in.reshape(rows, TOPK)))
    return (second + expert_sum).reshape(GROUPS, TOK_DEV, D)

def reference(x_in, targets, w_query, w_key, w_value, w_out, w_gate, w_up, w_down, gain_attn, gain_ffn, expert_ids, gates, lengths):
    weights = tuple((array.astype(jnp.float32) for array in (w_query, w_key, w_value, w_out, w_gate, w_up, w_down, gain_attn, gain_ffn)))
    inputs = x_in.astype(jnp.float32)
    goal = targets.astype(jnp.float32)
    cont_rows = jnp.arange(TOK_DEV, dtype=jnp.int32)[None, None, :] - PROMPT_DEV
    valid = (cont_rows < lengths[:, :, None]).astype(jnp.float32)
    count = (MICRO * PROMPT + jnp.sum(lengths)).astype(jnp.float32)
    zero_mid = jnp.zeros_like(inputs)

    def forward(inputs, zero_mid, wq_all, wk_all, wv_all, wo_all, wg_all, wu_all, wd_all, ga_all, gf_all):
        total = jnp.zeros((), jnp.float32)
        mids = []
        finals = []
        for micro in range(MICRO):
            first = layer(inputs[micro], wq_all[0], wk_all[0], wv_all[0], wo_all[0], wg_all[0], wu_all[0], wd_all[0], ga_all[0], gf_all[0], expert_ids[0, micro], gates[0, micro])
            middle = low(low_back(first)) + zero_mid[micro]
            final = layer(middle, wq_all[1], wk_all[1], wv_all[1], wo_all[1], wg_all[1], wu_all[1], wd_all[1], ga_all[1], gf_all[1], expert_ids[1, micro], gates[1, micro])
            diff = final - goal[micro]
            total = total + jnp.sum(valid[micro][:, :, None] * diff * diff) / count
            mids.append(middle)
            finals.append(final)
        return (total, (jnp.stack(mids), jnp.stack(finals)))
    loss, pull, (mids, finals) = jax.vjp(forward, inputs, zero_mid, *weights, has_aux=True)
    grads = pull(jnp.ones((), jnp.float32))
    outputs = jnp.stack([mids, finals]).astype(jnp.bfloat16)
    input_grads = jnp.stack([grads[0], grads[1]]).astype(jnp.bfloat16)
    return (outputs, loss, input_grads, grads[2], grads[3], grads[4], grads[5], grads[6], grads[7], grads[8], grads[9], grads[10])
```

```python
import jax
import jax.numpy as jnp
from jax import lax
from jax.sharding import PartitionSpec as P

HEAD = 64
HIDDEN_SIZE = 512
CONT_LEN = 512
CAP = 384


EPS = 1e-06
THETA = 10000.0
NEG = -1e30


def from_behind(value, axis, steps):
    count = lax.axis_size(axis)
    initial, last = (max(0, -steps), min(count, count - steps))
    return lax.ppermute(value, axis, [(source, source + steps) for source in range(initial, last)])


def tables(positions, head_size):
    freqs = THETA ** (-(jnp.arange(head_size // 2).astype(jnp.float32) * 2.0) / head_size)
    angles = positions.astype(jnp.float32)[:, None] * freqs[None, :]
    return (jnp.cos(angles)[:, None, :], jnp.sin(angles)[:, None, :])


def rotate(value, cosine, sine):
    half = value.shape[-1] // 2
    first = value[..., :half]
    second = value[..., half:]
    return jnp.concatenate(
        [first * cosine - second * sine, second * cosine + first * sine], axis=-1
    )


def spread(value):
    return lax.all_gather(value, "col", axis=1, tiled=True)


def collect(value):
    return lax.psum_scatter(
        value.astype(jnp.bfloat16), "col", scatter_dimension=1, tiled=True
    ).astype(jnp.float32)


def spread_grad(value):
    return lax.all_gather(value, "col", axis=1, tiled=True)


def collect_grad(value):
    return lax.psum_scatter(value, "col", scatter_dimension=1, tiled=True)


def norm_total(value):
    return lax.psum(value, "col")


def contract_last(left, right):
    return lax.dot_general(
        left, right, (((1,), (1,)), ((), ())), preferred_element_type=jnp.float32
    )


def contract_first(left, right):
    return lax.dot_general(
        left, right, (((0,), (0,)), ((), ())), preferred_element_type=jnp.float32
    )


def fetch(w_query, w_key, w_value, w_out, w_gate, w_up, w_down):
    full_query, full_key, full_value, full_out, full_gate, full_up, full_down = (
        lax.all_gather(w_query[0], "row", axis=0, tiled=True),
        lax.all_gather(w_key[0], "row", axis=0, tiled=True),
        lax.all_gather(w_value[0], "row", axis=0, tiled=True),
        lax.all_gather(w_out[0], "row", axis=1, tiled=True),
        lax.all_gather(w_gate[0], "row", axis=1, tiled=True),
        lax.all_gather(w_up[0], "row", axis=1, tiled=True),
        lax.all_gather(w_down[0], "row", axis=2, tiled=True),
    )
    return {
        "qkv": jnp.concatenate([full_query, full_key, full_value], axis=1),
        "out": full_out,
        "gate_up": jnp.concatenate([full_gate, full_up], axis=2),
        "down": full_down,
    }


def attention_scores(grouped, keys, allowed):
    scores = jnp.einsum(
        "tgrd,kgd->grtk", grouped, keys, preferred_element_type=jnp.float32
    ) * grouped.shape[-1] ** (-0.5)
    return jnp.where(allowed[None, None], scores, NEG)


def forward_layer(
    layer_in, fetched, gain_first, gain_second, routes, weights_in, row_rank, col_rank
):
    tokens = layer_in.shape[0]
    prompt_rows = tokens - CONT_LEN
    prompt_len = prompt_rows * lax.axis_size("row")
    width = fetched["qkv"].shape[0]
    query_cols = fetched["out"].shape[0]
    kv_cols = (fetched["qkv"].shape[1] - query_cols) // 2
    kv_heads = kv_cols // HEAD
    repeat = query_cols // kv_cols
    residual = layer_in.astype(jnp.float32)
    whole = spread(layer_in).astype(jnp.float32)
    scale_first = lax.rsqrt(jnp.mean(whole * whole, axis=1, keepdims=True) + EPS)
    normed = (whole * scale_first * gain_first).astype(jnp.bfloat16)
    projected = jnp.dot(normed, fetched["qkv"], preferred_element_type=jnp.float32)
    positions = jnp.concatenate(
        [
            row_rank * prompt_rows + jnp.arange(prompt_rows, dtype=jnp.int32),
            prompt_len + jnp.arange(CONT_LEN, dtype=jnp.int32),
        ]
    )
    cosine, sine = tables(positions, HEAD)
    queries = rotate(projected[:, :query_cols].reshape(tokens, -1, HEAD), cosine, sine).astype(
        jnp.bfloat16
    )
    keys_own = rotate(
        projected[:, query_cols : query_cols + kv_cols].reshape(tokens, kv_heads, HEAD),
        cosine,
        sine,
    ).astype(jnp.bfloat16)
    values_own = (
        projected[:, query_cols + kv_cols :].reshape(tokens, kv_heads, HEAD).astype(jnp.bfloat16)
    )
    prompt_keys, prompt_values = (
        lax.all_gather(keys_own[:prompt_rows], "row", axis=0, tiled=True),
        lax.all_gather(values_own[:prompt_rows], "row", axis=0, tiled=True),
    )
    keys = jnp.concatenate([prompt_keys, keys_own[prompt_rows:]], axis=0)
    values = jnp.concatenate([prompt_values, values_own[prompt_rows:]], axis=0)
    key_pos = jnp.concatenate(
        [
            jnp.arange(prompt_len, dtype=jnp.int32),
            prompt_len + jnp.arange(CONT_LEN, dtype=jnp.int32),
        ]
    )
    allowed = key_pos[None, :] <= positions[:, None]
    grouped = queries.reshape(tokens, kv_heads, repeat, HEAD)
    scores = attention_scores(grouped, keys, allowed)
    top = jnp.max(scores, axis=-1, keepdims=True)
    logsum = top + jnp.log(jnp.sum(jnp.exp(scores - top), axis=-1, keepdims=True))
    probs = jnp.exp(scores - logsum).astype(jnp.bfloat16)
    mixed = (
        jnp.einsum("grtk,kgd->tgrd", probs, values, preferred_element_type=jnp.float32)
        .reshape(tokens, query_cols)
        .astype(jnp.bfloat16)
    )
    second = residual + collect(jnp.dot(mixed, fetched["out"], preferred_element_type=jnp.float32))
    second_b = second.astype(jnp.bfloat16)
    whole_second = spread(second_b).astype(jnp.float32)
    scale_second = lax.rsqrt(jnp.mean(whole_second * whole_second, axis=1, keepdims=True) + EPS)
    normed_second = (whole_second * scale_second * gain_second).astype(jnp.bfloat16)
    local_experts = fetched["down"].shape[0]
    first_expert = col_rank * local_experts
    match = (
        routes[:, :, None]
        == (first_expert + jnp.arange(local_experts, dtype=jnp.int32))[None, None, :]
    )
    member = jnp.any(match, axis=1)
    weight = jnp.sum(jnp.where(match, weights_in[:, :, None], 0.0), axis=1)
    order = jnp.arange(tokens, dtype=jnp.int32)
    earlier = (order[:, None] >= order[None, :]).astype(jnp.bfloat16)
    place = (
        jnp.dot(earlier, member.astype(jnp.bfloat16), preferred_element_type=jnp.float32).astype(
            jnp.int32
        )
        - 1
    )
    slot = jnp.where(member, place, CAP)
    index = (
        jnp.zeros((local_experts, CAP + 1), jnp.int32)
        .at[jnp.arange(local_experts, dtype=jnp.int32)[None, :], slot]
        .set(jnp.arange(tokens, dtype=jnp.int32)[:, None])[:, :CAP]
    )
    counts = jnp.sum(member.astype(jnp.int32), axis=0)
    live = jnp.arange(CAP, dtype=jnp.int32)[None, :] < counts[:, None]
    slot_gate = jnp.where(live, jnp.take_along_axis(weight.T, index, axis=1), 0.0)
    chosen = normed_second[index]
    gate_up = jnp.einsum(
        "ecd,edh->ech", chosen, fetched["gate_up"], preferred_element_type=jnp.float32
    )
    gate = gate_up[..., :HIDDEN_SIZE]
    up_part = gate_up[..., HIDDEN_SIZE:]
    activated = (jax.nn.silu(gate) * up_part).astype(jnp.bfloat16)
    expert_out = jnp.einsum(
        "ech,ehd->ecd", activated, fetched["down"], preferred_element_type=jnp.float32
    )
    combined = jax.ops.segment_sum(
        (expert_out * slot_gate[..., None]).reshape(-1, width),
        index.reshape(-1),
        num_segments=tokens,
    )
    result = second + collect(combined)
    keep = {
        "layer_in": layer_in,
        "scale_first": scale_first,
        "normed": normed,
        "cosine": cosine,
        "sine": sine,
        "grouped": grouped,
        "keys": keys,
        "values": values,
        "allowed": allowed,
        "logsum": logsum,
        "mixed": mixed,
        "second_b": second_b,
        "scale_second": scale_second,
        "index": index,
        "slot_gate": slot_gate,
        "chosen": chosen,
        "gate": gate,
        "up_part": up_part,
        "activated": activated,
        "result": result,
    }
    return (result, keep)


def norm_backward(grad_local, value_local, scale, gain_local, width):
    scaled = grad_local * gain_local
    inner = norm_total(jnp.sum(scaled * value_local, axis=1))
    grad_value = scale * scaled - value_local * (scale * scale * scale) * inner[:, None] / width
    grad_gain = jnp.sum(grad_local * value_local * scale, axis=0)
    return (grad_value, grad_gain)


def backward_layer(grad_result, keep, fetched, gain_first, gain_second, col_rank):
    tokens, shard = grad_result.shape
    width = fetched["qkv"].shape[0]
    index = keep["index"]
    grad_whole = spread_grad(grad_result.astype(jnp.bfloat16))
    grad_expert = (grad_whole[index].astype(jnp.float32) * keep["slot_gate"][..., None]).astype(
        jnp.bfloat16
    )
    grad_act = jnp.einsum(
        "ecd,ehd->ech", grad_expert, fetched["down"], preferred_element_type=jnp.float32
    )
    grad_down = jnp.einsum(
        "ech,ecd->ehd", keep["activated"], grad_expert, preferred_element_type=jnp.float32
    )
    gate = keep["gate"]
    sigmoid = jax.nn.sigmoid(gate)
    grad_gate = grad_act * keep["up_part"] * sigmoid * (1.0 + gate * (1.0 - sigmoid))
    grad_up = grad_act * gate * sigmoid
    grad_gate_up = jnp.concatenate([grad_gate, grad_up], axis=2).astype(jnp.bfloat16)
    grad_chosen = jnp.einsum(
        "ech,edh->ecd", grad_gate_up, fetched["gate_up"], preferred_element_type=jnp.float32
    )
    grad_gate_up_weight = jnp.einsum(
        "ecd,ech->edh", keep["chosen"], grad_gate_up, preferred_element_type=jnp.float32
    )
    grad_normed_second = collect_grad(
        jax.ops.segment_sum(grad_chosen.reshape(-1, width), index.reshape(-1), num_segments=tokens)
    )
    second_local = keep["second_b"].astype(jnp.float32)
    gain_second_local = lax.dynamic_slice_in_dim(gain_second, col_rank * shard, shard)
    grad_norm_second, grad_gain_second = norm_backward(
        grad_normed_second, second_local, keep["scale_second"], gain_second_local, width
    )
    grad_second = grad_result + grad_norm_second
    grad_branch = spread_grad(grad_second.astype(jnp.bfloat16))
    grad_mixed = contract_last(grad_branch, fetched["out"])
    grad_out_weight = contract_first(keep["mixed"], grad_branch)
    grouped = keep["grouped"]
    keys = keep["keys"]
    values = keep["values"]
    grad_mixed_b = grad_mixed.astype(jnp.bfloat16).reshape(grouped.shape)
    scores = attention_scores(grouped, keys, keep["allowed"])
    probs = jnp.exp(scores - keep["logsum"])
    probs_b = probs.astype(jnp.bfloat16)
    grad_probs = jnp.einsum(
        "tgrd,kgd->grtk", grad_mixed_b, values, preferred_element_type=jnp.float32
    )
    delta = jnp.sum(probs * grad_probs, axis=-1, keepdims=True)
    grad_scores = (probs * (grad_probs - delta)).astype(jnp.bfloat16)
    factor = HEAD ** (-0.5)
    grad_queries = (
        jnp.einsum("grtk,kgd->tgrd", grad_scores, keys, preferred_element_type=jnp.float32) * factor
    )
    grad_keys = (
        jnp.einsum("grtk,tgrd->kgd", grad_scores, grouped, preferred_element_type=jnp.float32)
        * factor
    )
    grad_values = jnp.einsum(
        "grtk,tgrd->kgd", probs_b, grad_mixed_b, preferred_element_type=jnp.float32
    )
    prompt_len = keys.shape[0] - CONT_LEN
    prompt_key_grad, prompt_value_grad = (
        lax.psum_scatter(grad_keys[:prompt_len], "row", scatter_dimension=0, tiled=True),
        lax.psum_scatter(grad_values[:prompt_len], "row", scatter_dimension=0, tiled=True),
    )
    grad_keys_own = jnp.concatenate([prompt_key_grad, grad_keys[prompt_len:]], axis=0)
    grad_values_own = jnp.concatenate([prompt_value_grad, grad_values[prompt_len:]], axis=0)
    cosine = keep["cosine"]
    sine = keep["sine"]
    grad_query_raw = rotate(grad_queries.reshape(tokens, -1, HEAD), cosine, -sine)
    grad_key_raw = rotate(grad_keys_own, cosine, -sine)
    grad_projected = jnp.concatenate(
        [
            grad_query_raw.reshape(tokens, -1),
            grad_key_raw.reshape(tokens, -1),
            grad_values_own.reshape(tokens, -1),
        ],
        axis=1,
    ).astype(jnp.bfloat16)
    grad_normed = collect_grad(contract_last(grad_projected, fetched["qkv"]))
    grad_qkv_weight = contract_first(keep["normed"], grad_projected)
    input_local = keep["layer_in"].astype(jnp.float32)
    gain_first_local = lax.dynamic_slice_in_dim(gain_first, col_rank * shard, shard)
    grad_norm_first, grad_gain_first = norm_backward(
        grad_normed, input_local, keep["scale_first"], gain_first_local, width
    )
    grad_input = grad_second + grad_norm_first
    return (
        grad_input,
        {
            "qkv": grad_qkv_weight,
            "out": grad_out_weight,
            "gate_up": grad_gate_up_weight,
            "down": grad_down,
            "gain_first": grad_gain_first,
            "gain_second": grad_gain_second,
        },
    )


def on_device(
    x_in,
    targets,
    w_query,
    w_key,
    w_value,
    w_out,
    w_gate,
    w_up,
    w_down,
    gain_attn,
    gain_ffn,
    expert_ids,
    gates,
    lengths,
):
    section_rank = lax.axis_index("section")
    row_rank = lax.axis_index("row")
    col_rank = lax.axis_index("col")
    micro = x_in.shape[0]
    tokens = x_in.shape[2]
    shard = x_in.shape[3]
    prompt_rows = tokens - CONT_LEN
    prompt_len = prompt_rows * lax.axis_size("row")
    first_section = section_rank == 0
    gain_first = gain_attn[0].astype(jnp.float32)
    gain_second = gain_ffn[0].astype(jnp.float32)
    count = (micro * prompt_len + jnp.sum(lengths)).astype(jnp.float32)
    received = jnp.zeros((tokens, shard), jnp.bfloat16)
    kept = []
    for step in range(micro + 1):
        batch = jnp.clip(step - section_rank, 0, micro - 1)
        own_input = x_in[min(step, micro - 1), 0]
        layer_in = jnp.where(first_section, own_input, received)
        routes = lax.dynamic_index_in_dim(expert_ids[0], batch, 0, keepdims=False)[0]
        weights_in = lax.dynamic_index_in_dim(gates[0], batch, 0, keepdims=False)[0]
        fetched = fetch(w_query, w_key, w_value, w_out, w_gate, w_up, w_down)
        result, keep = forward_layer(
            layer_in, fetched, gain_first, gain_second, routes, weights_in, row_rank, col_rank
        )
        kept.append(keep)
        if step < micro:
            received = from_behind(result.astype(jnp.bfloat16), "section", 1)
    outputs = jnp.stack(
        [
            jnp.where(first_section, kept[index_m]["result"], kept[index_m + 1]["result"])
            for index_m in range(micro)
        ]
    )
    grad_received = jnp.zeros((tokens, shard), jnp.bfloat16)
    loss_part = jnp.zeros((), jnp.float32)
    totals = None
    input_list = []
    for step in range(micro + 1):
        picked = jax.tree.map(
            lambda early, later: jnp.where(first_section, early, later),
            kept[max(step - 1, 0)],
            kept[min(step + 1, micro)],
        )
        final_batch = min(step, micro - 1)
        final = kept[min(step + 1, micro)]["result"]
        goal = targets[final_batch, 0].astype(jnp.float32)
        length = lax.dynamic_index_in_dim(lengths[final_batch], row_rank, 0, keepdims=False)
        valid = (jnp.arange(tokens, dtype=jnp.int32) - prompt_rows < length).astype(jnp.float32)[
            :, None
        ]
        active = 1.0 if step < micro else 0.0
        diff = final - goal
        loss_part = loss_part + jnp.where(
            first_section, 0.0, active * jnp.sum(valid * diff * diff) / count
        )
        grad_loss = 2.0 * active / count * valid * diff
        grad_here = jnp.where(first_section, grad_received.astype(jnp.float32), grad_loss)
        fetched = fetch(w_query, w_key, w_value, w_out, w_gate, w_up, w_down)
        grad_input, layer_grads = backward_layer(
            grad_here, picked, fetched, gain_first, gain_second, col_rank
        )
        totals = (
            layer_grads
            if totals is None
            else jax.tree.map(lambda left, right: left + right, totals, layer_grads)
        )
        grad_b = grad_input.astype(jnp.bfloat16)
        input_list.append(grad_b)
        if step < micro:
            grad_received = from_behind(grad_b, "section", -1)
    input_grads = jnp.stack(
        [
            jnp.where(first_section, input_list[index_m + 1], input_list[index_m])
            for index_m in range(micro)
        ]
    )
    query_cols = w_query.shape[2]
    key_cols = w_key.shape[2]
    qkv_total = totals["qkv"]
    gate_up_total = totals["gate_up"]
    grad_query, grad_key, grad_value, grad_out, grad_gate, grad_up, grad_down = (
        lax.psum_scatter(qkv_total[:, :query_cols], "row", scatter_dimension=0, tiled=True),
        lax.psum_scatter(
            qkv_total[:, query_cols : query_cols + key_cols], "row", scatter_dimension=0, tiled=True
        ),
        lax.psum_scatter(
            qkv_total[:, query_cols + key_cols :], "row", scatter_dimension=0, tiled=True
        ),
        lax.psum_scatter(totals["out"], "row", scatter_dimension=1, tiled=True),
        lax.psum_scatter(gate_up_total[..., :HIDDEN_SIZE].astype(jnp.bfloat16), "row", scatter_dimension=1, tiled=True),
        lax.psum_scatter(gate_up_total[..., HIDDEN_SIZE:].astype(jnp.bfloat16), "row", scatter_dimension=1, tiled=True),
        lax.psum_scatter(totals["down"].astype(jnp.bfloat16), "row", scatter_dimension=2, tiled=True),
    )
    gain_grad_first, gain_grad_second = lax.psum(
        (totals["gain_first"], totals["gain_second"]), "row"
    )
    loss = lax.psum(loss_part, ("section", "row", "col"))
    return (
        outputs.astype(jnp.bfloat16)[None, :, None],
        loss,
        input_grads[None, :, None],
        grad_query[None],
        grad_key[None],
        grad_value[None],
        grad_out[None],
        grad_gate.astype(jnp.float32)[None],
        grad_up.astype(jnp.float32)[None],
        grad_down.astype(jnp.float32)[None],
        gain_grad_first[None],
        gain_grad_second[None],
    )


def solution(mesh):
    in_specs = (
        P(None, "row", None, "col"),
        P(None, "row", None, "col"),
        P("section", "row", "col"),
        P("section", "row", "col"),
        P("section", "row", "col"),
        P("section", "col", "row"),
        P("section", "col", "row", None),
        P("section", "col", "row", None),
        P("section", "col", None, "row"),
        P("section", None),
        P("section", None),
        P("section", None, "row", None, None),
        P("section", None, "row", None, None),
        P(),
    )
    out_specs = (
        P("section", None, "row", None, "col"),
        P(),
        P("section", None, "row", None, "col"),
        P("section", "row", "col"),
        P("section", "row", "col"),
        P("section", "row", "col"),
        P("section", "col", "row"),
        P("section", "col", "row", None),
        P("section", "col", "row", None),
        P("section", "col", None, "row"),
        P("section", "col"),
        P("section", "col"),
    )
    return jax.shard_map(
        on_device, mesh=mesh, in_specs=in_specs, out_specs=out_specs, check_vma=False
    )
```

```python
import functools

import jax
import jax.numpy as jnp
from jax import lax
from jax.experimental import pallas as pl
from jax.experimental.pallas import tpu as pltpu
from jax.sharding import PartitionSpec as P

HEAD = 64
HIDDEN_SIZE = 512
CONT_LEN = 512
CAP = 384
GROUP = 4

EPS = 1e-06
THETA = 10000.0
NEG = -1e30
BF16 = jnp.bfloat16
F32 = jnp.float32
VMEM_LIMIT = 60 * 1024 * 1024


def shift(value, axis, pairs):
    return lax.ppermute(value, axis, pairs)


def flip(value, bit):
    count = lax.axis_size("col")
    return shift(value, "col", [(i, i ^ bit) for i in range(count)])


def col_bits():
    count = lax.axis_size("col")
    bits = [1]
    while bits[-1] * 2 < count:
        bits.append(bits[-1] * 2)
    return bits


def gather_col(value):
    blocks = {0: value}
    for bit in reversed(col_bits()):
        for k in list(blocks):
            blocks[k ^ bit] = flip(blocks[k], bit)
    return [blocks[k] for k in range(lax.axis_size("col"))]


def scatter_col(blocks):
    blocks = dict(enumerate(blocks))
    total = None
    for bit in col_bits():
        keep = [k for k in blocks if not k & bit]
        total = {k: blocks[k].astype(F32) + flip(blocks[k ^ bit], bit).astype(F32) for k in keep}
        blocks = {k: total[k].astype(BF16) for k in keep}
    return total[0]


def ring(value):
    count = lax.axis_size("row")
    return shift(value, "row", [(i, (i + 1) % count) for i in range(count)])


def gather_row(value):
    pieces = [value]
    for _ in range(lax.axis_size("row") - 1):
        pieces.append(ring(pieces[-1]))
    return pieces


def scatter_row(parts):
    count = len(parts)
    if count == 1:
        return parts[0].astype(F32)
    running = parts[1]
    for k in range(2, count):
        running = (ring(running).astype(F32) + parts[k].astype(F32)).astype(BF16)
    return ring(running).astype(F32) + parts[0].astype(F32)


def dot_nn(left, right):
    return lax.dot_general(left, right, (((1,), (0,)), ((), ())), preferred_element_type=F32)


def dot_nt(left, right):
    return lax.dot_general(left, right, (((1,), (1,)), ((), ())), preferred_element_type=F32)


def dot_tn(left, right):
    return lax.dot_general(left, right, (((0,), (0,)), ((), ())), preferred_element_type=F32)


def swap_halves(value):
    lanes = value.shape[1]
    lane = lax.broadcasted_iota(jnp.int32, value.shape, 1)
    half = HEAD // 2
    ahead = pltpu.roll(value, lanes - half, 1)
    behind = pltpu.roll(value, half, 1)
    return jnp.where(lane % HEAD < half, ahead, behind)


def project_kernel(x_ref, gain_ref, w_ref, cos_ref, sin_ref, n_ref, out_ref):
    step = pl.program_id(0)
    turned = pl.num_programs(0) // 2

    @pl.when(step == 0)
    def _():
        x = x_ref[...].astype(F32)
        rho = lax.rsqrt(jnp.mean(x * x, axis=1, keepdims=True) + EPS)
        n_ref[...] = (x * rho * gain_ref[...]).astype(BF16)

    raw = dot_nn(n_ref[...], w_ref[...])
    cos, sin = cos_ref[...], sin_ref[...]
    left, right = raw[:, :128], raw[:, 128:]
    left = left * cos + swap_halves(left) * sin
    out_ref[:, :128] = left.astype(BF16)

    @pl.when(step < turned)
    def _():
        out_ref[:, 128:] = (right * cos + swap_halves(right) * sin).astype(BF16)

    @pl.when(step >= turned)
    def _():
        out_ref[:, 128:] = right.astype(BF16)


def project(x, gain, w, cos, sin):
    rows, width = x.shape
    columns = w.shape[1]
    whole = lambda i: (0, 0)
    return pl.pallas_call(
        project_kernel,
        grid=(columns // 256,),
        in_specs=[
            pl.BlockSpec((rows, width), whole),
            pl.BlockSpec((1, width), whole),
            pl.BlockSpec((width, 256), lambda i: (0, i)),
            pl.BlockSpec((rows, 128), whole),
            pl.BlockSpec((rows, 128), whole),
        ],
        out_specs=[
            pl.BlockSpec((rows, width), whole),
            pl.BlockSpec((rows, 256), lambda i: (0, i)),
        ],
        out_shape=[
            jax.ShapeDtypeStruct((rows, width), BF16),
            jax.ShapeDtypeStruct((rows, columns), BF16),
        ],
        compiler_params=pltpu.CompilerParams(vmem_limit_bytes=VMEM_LIMIT),
        cost_estimate=pl.CostEstimate(
            flops=2 * rows * width * columns,
            bytes_accessed=2 * (width * columns + rows * columns + 2 * rows * width),
            transcendentals=0,
        ),
    )(x, gain, w, cos, sin)


def stack_heads(value):
    low = (lax.broadcasted_iota(jnp.int32, (value.shape[0], 128), 1) < HEAD).astype(F32)
    first, second = value[:, :128].astype(F32), value[:, 128:].astype(F32)
    return jnp.concatenate(
        [first * low, second * low, first * (1.0 - low), second * (1.0 - low)], axis=0
    )


def unstack_heads(value):
    rows = value.shape[0] // 4
    low = lax.broadcasted_iota(jnp.int32, (rows, 128), 1) < HEAD
    first = jnp.where(low, value[:rows], value[2 * rows : 3 * rows])
    second = jnp.where(low, value[rows : 2 * rows], value[3 * rows :])
    return first, second


def attend_kernel(q_ref, k_ref, v_ref, bias_ref, o_ref, lse_ref):
    stacked = (stack_heads(q_ref[0]) * HEAD**-0.5).astype(BF16)
    scores = dot_nt(k_ref[0], stacked) + bias_ref[...]
    top = jnp.max(scores, axis=0, keepdims=True)
    weights = jnp.exp(scores - top)
    total = jnp.sum(weights, axis=0, keepdims=True)
    mixed = dot_tn(v_ref[0], weights.astype(BF16)) / total
    first, second = unstack_heads(mixed.T)
    o_ref[0, :, :128] = first
    o_ref[0, :, 128:] = second
    lse_ref[0, 0] = top + jnp.log(total)


def attend(qkv, kv, bias):
    micro, rows, _ = qkv.shape
    keys, width = kv.shape[1], kv.shape[2]
    groups = width // 256
    return pl.pallas_call(
        attend_kernel,
        grid=(micro, groups),
        in_specs=[
            pl.BlockSpec((1, rows, 256), lambda m, g: (m, 0, g)),
            pl.BlockSpec((1, keys, 128), lambda m, g: (m, 0, 2 * g)),
            pl.BlockSpec((1, keys, 128), lambda m, g: (m, 0, 2 * g + 1)),
            pl.BlockSpec((keys, 4 * rows), lambda m, g: (0, 0)),
        ],
        out_specs=[
            pl.BlockSpec((1, rows, 256), lambda m, g: (m, 0, g)),
            pl.BlockSpec((1, 1, 1, 4 * rows), lambda m, g: (m, g, 0, 0)),
        ],
        out_shape=[
            jax.ShapeDtypeStruct((micro, rows, groups * 256), F32),
            jax.ShapeDtypeStruct((micro, groups, 1, 4 * rows), F32),
        ],
        compiler_params=pltpu.CompilerParams(vmem_limit_bytes=VMEM_LIMIT),
        cost_estimate=pl.CostEstimate(
            flops=micro * groups * 4 * rows * keys * 128 * 4,
            bytes_accessed=2 * micro * keys * width + 4 * keys * 4 * rows,
            transcendentals=micro * groups * 4 * rows * keys,
        ),
    )(qkv, kv, kv, bias)


def attend_back_kernel(
    q_ref, k_ref, v_ref, bias_ref, do_ref, o_ref, lse_ref, cos_ref, sin_ref, kcos_ref, ksin_ref,
    dq_ref, dkv_ref,
):
    scale = HEAD**-0.5
    queries = (stack_heads(q_ref[0]) * scale).astype(BF16)
    grads_wide = stack_heads(do_ref[0])
    product = grads_wide * stack_heads(o_ref[0])
    delta = jnp.sum(product.T, axis=0, keepdims=True)
    grads = grads_wide.astype(BF16)
    keys, values = k_ref[0], v_ref[0]
    probs = jnp.exp(dot_nt(keys, queries) + bias_ref[...] - lse_ref[0, 0])
    dvalues = dot_nn(probs.astype(BF16), grads)
    dscores = (probs * (dot_nt(values, grads) - delta)).astype(BF16)
    dkeys = dot_nn(dscores, queries)
    dqueries = dot_tn(keys, dscores) * scale
    first, second = unstack_heads(dqueries.T)
    cos, sin = cos_ref[...], sin_ref[...]
    dq_ref[0, :, :128] = (first * cos - swap_halves(first) * sin).astype(BF16)
    dq_ref[0, :, 128:] = (second * cos - swap_halves(second) * sin).astype(BF16)
    dkv_ref[0, :, :128] = (dkeys * kcos_ref[...] - swap_halves(dkeys) * ksin_ref[...]).astype(BF16)
    dkv_ref[0, :, 128:] = dvalues.astype(BF16)


def attend_back(qkv, kv, bias, grad, o, lse, cos, sin, kcos, ksin):
    micro, rows, _ = qkv.shape
    keys, width = kv.shape[1], kv.shape[2]
    groups = width // 256
    mine = pl.BlockSpec((1, rows, 256), lambda m, g: (m, 0, g))
    return pl.pallas_call(
        attend_back_kernel,
        grid=(micro, groups),
        in_specs=[
            mine,
            pl.BlockSpec((1, keys, 128), lambda m, g: (m, 0, 2 * g)),
            pl.BlockSpec((1, keys, 128), lambda m, g: (m, 0, 2 * g + 1)),
            pl.BlockSpec((keys, 4 * rows), lambda m, g: (0, 0)),
            mine,
            mine,
            pl.BlockSpec((1, 1, 1, 4 * rows), lambda m, g: (m, g, 0, 0)),
            pl.BlockSpec((rows, 128), lambda m, g: (0, 0)),
            pl.BlockSpec((rows, 128), lambda m, g: (0, 0)),
            pl.BlockSpec((keys, 128), lambda m, g: (0, 0)),
            pl.BlockSpec((keys, 128), lambda m, g: (0, 0)),
        ],
        out_specs=[mine, pl.BlockSpec((1, keys, 256), lambda m, g: (m, 0, g))],
        out_shape=[
            jax.ShapeDtypeStruct((micro, rows, groups * 256), BF16),
            jax.ShapeDtypeStruct((micro, keys, width), BF16),
        ],
        compiler_params=pltpu.CompilerParams(vmem_limit_bytes=VMEM_LIMIT),
        cost_estimate=pl.CostEstimate(
            flops=micro * groups * 4 * rows * keys * 128 * 10,
            bytes_accessed=4 * micro * keys * width + 4 * keys * 4 * rows,
            transcendentals=micro * groups * 4 * rows * keys,
        ),
    )(qkv, kv, kv, bias, grad, o, lse, cos, sin, kcos, ksin)


def chosen_rows(place_ref, weight_ref, m, cap, tokens):
    slots = lax.broadcasted_iota(jnp.int32, (cap, tokens), 0)
    hit = slots == place_ref[0, m : m + 1, :]
    pick = jnp.where(hit, 1.0, 0.0)
    weight = jnp.sum(pick * weight_ref[0, m : m + 1, :], axis=1, keepdims=True)
    return pick.astype(BF16), weight


def load_tokens(meta_ref, pieces, scratch, cut):
    count = scratch.shape[2] // cut
    for at, piece in enumerate(pieces):
        rows = piece.shape[1]
        for k in range(count):
            start = pl.multiple_of(meta_ref[k], cut)
            scratch[:, at * rows : (at + 1) * rows, k * cut : (k + 1) * cut] = piece[
                :, :, pl.ds(start, cut)
            ]


def store_tokens(meta_ref, out_ref, total, cut):
    count = total.shape[2] // cut
    blocks, _, rows, _ = out_ref.shape
    for at in range(blocks):
        for k in range(count):
            start = pl.multiple_of(meta_ref[k], cut)
            out_ref[at, :, :, pl.ds(start, cut)] = total[
                :, at * rows : (at + 1) * rows, k * cut : (k + 1) * cut
            ].astype(BF16)


def by_load(meta_ref, nrow, body, empty=None):
    e = pl.program_id(0)
    most = jnp.maximum(meta_ref[nrow + 2 * e], meta_ref[nrow + 2 * e + 1])
    below = 0
    for cap in (CAP // 3, 2 * CAP // 3, CAP):
        pl.when((most > below) & (most <= cap))(functools.partial(body, cap))
        below = cap
    if empty is not None:
        pl.when(most == 0)(empty)


def experts_kernel(ncol, nrow, meta_ref, place_ref, weight_ref, *refs):
    pieces, refs = refs[:ncol], refs[ncol:]
    gates, refs = refs[:nrow], refs[nrow:]
    ups, refs = refs[:nrow], refs[nrow:]
    downs, refs = refs[:nrow], refs[nrow:]
    y_ref, chosen_ref, hidden_ref, tokens_ref, total_ref, rows_ref, out_ref = refs
    micro, tokens, width = tokens_ref.shape
    cut = width // nrow
    hidden = gates[0].shape[2]
    e = pl.program_id(0)

    @pl.when(e == 0)
    def _():
        load_tokens(meta_ref, pieces, tokens_ref, cut)
        total_ref[...] = jnp.zeros_like(total_ref)

    def body(cap):
        picks, weights = [], []
        for m in range(micro):
            pick, weight = chosen_rows(place_ref, weight_ref, m, cap, tokens)
            chosen = dot_nn(pick, tokens_ref[m]).astype(BF16)
            rows_ref[m * cap : (m + 1) * cap, :] = chosen
            chosen_ref[0, m, :cap, :] = chosen
            picks.append(pick)
            weights.append(weight)
        used = micro * cap
        gate = sum(
            dot_nn(rows_ref[:used, k * cut : (k + 1) * cut], gates[k][0]) for k in range(nrow)
        )
        up = sum(dot_nn(rows_ref[:used, k * cut : (k + 1) * cut], ups[k][0]) for k in range(nrow))
        for m in range(micro):
            hidden_ref[0, m, :cap, :hidden] = gate[m * cap : (m + 1) * cap].astype(BF16)
            hidden_ref[0, m, :cap, hidden:] = up[m * cap : (m + 1) * cap].astype(BF16)
        active = (gate * jax.nn.sigmoid(gate) * up).astype(BF16)
        scale = jnp.concatenate(weights, axis=0)
        for k in range(nrow):
            out_ref[:used, k * cut : (k + 1) * cut] = (
                dot_nn(active, downs[k][0]) * scale
            ).astype(BF16)
        for m in range(micro):
            total_ref[m] += dot_tn(picks[m], out_ref[m * cap : (m + 1) * cap, :])

    by_load(meta_ref, nrow, body)

    @pl.when(e == pl.num_programs(0) - 1)
    def _():
        store_tokens(meta_ref, y_ref, total_ref, cut)


def expert_specs(pieces, weights, slots):
    micro, rows, width = pieces[0].shape
    at_expert = lambda e: (e, 0, 0)
    specs = [
        pl.BlockSpec(memory_space=pltpu.SMEM),
        pl.BlockSpec((1, *slots.shape[1:]), at_expert),
        pl.BlockSpec((1, *slots.shape[1:]), at_expert),
    ]
    specs += [pl.BlockSpec((micro, rows, width), lambda e: (0, 0, 0)) for _ in pieces]
    specs += [pl.BlockSpec((1, *w.shape[1:]), at_expert) for w in weights]
    return specs


def experts(meta, place, weight, pieces, gates, ups, downs):
    micro, rows, width = pieces[0].shape
    local = place.shape[0]
    ncol, nrow, hidden = len(pieces), len(gates), gates[0].shape[2]
    tokens = ncol * rows
    weights = [*gates, *ups, *downs]
    fixed = lambda e: (0, 0, 0, 0)
    at_expert = lambda e: (e, 0, 0, 0)
    return pl.pallas_call(
        functools.partial(experts_kernel, ncol, nrow),
        grid=(local,),
        in_specs=expert_specs(pieces, weights, place),
        out_specs=[
            pl.BlockSpec((ncol, micro, rows, width), fixed),
            pl.BlockSpec((1, micro, CAP, width), at_expert),
            pl.BlockSpec((1, micro, CAP, 2 * hidden), at_expert),
        ],
        out_shape=[
            jax.ShapeDtypeStruct((ncol, micro, rows, width), BF16),
            jax.ShapeDtypeStruct((local, micro, CAP, width), BF16),
            jax.ShapeDtypeStruct((local, micro, CAP, 2 * hidden), BF16),
        ],
        scratch_shapes=[
            pltpu.VMEM((micro, tokens, width), BF16),
            pltpu.VMEM((micro, tokens, width), F32),
            pltpu.VMEM((micro * CAP, width), BF16),
            pltpu.VMEM((micro * CAP, width), BF16),
        ],
        compiler_params=pltpu.CompilerParams(vmem_limit_bytes=VMEM_LIMIT),
        cost_estimate=pl.CostEstimate(
            flops=local * micro * 256 * width * (6 * hidden + 4 * tokens),
            bytes_accessed=local * width * (6 * hidden + 4 * micro * CAP),
            transcendentals=local * micro * CAP * hidden,
        ),
    )(meta, place, weight, *pieces, *weights)


def experts_back_kernel(ncol, nrow, with_grads, meta_ref, place_ref, weight_ref, *refs):
    pieces, refs = refs[:ncol], refs[ncol:]
    gates, refs = refs[:nrow], refs[nrow:]
    ups, refs = refs[:nrow], refs[nrow:]
    downs, refs = refs[:nrow], refs[nrow:]
    chosen_ref, hidden_ref, dx_ref, refs = refs[0], refs[1], refs[2], refs[3:]
    if with_grads:
        dgates, refs = refs[:nrow], refs[nrow:]
        dups, refs = refs[:nrow], refs[nrow:]
        ddowns, refs = refs[:nrow], refs[nrow:]
    tokens_ref, total_ref, rows_ref, out_ref, dhid_ref = refs
    micro, tokens, width = tokens_ref.shape
    cut = width // nrow
    hidden = gates[0].shape[2]
    e = pl.program_id(0)

    @pl.when(e == 0)
    def _():
        load_tokens(meta_ref, pieces, tokens_ref, cut)
        total_ref[...] = jnp.zeros_like(total_ref)

    def body(cap):
        picks = []
        for m in range(micro):
            pick, weight = chosen_rows(place_ref, weight_ref, m, cap, tokens)
            picks.append(pick)
            rows_ref[m * cap : (m + 1) * cap, :] = (
                dot_nn(pick, tokens_ref[m]) * weight
            ).astype(BF16)
        used = micro * cap
        dactive = sum(
            dot_nt(rows_ref[:used, k * cut : (k + 1) * cut], downs[k][0]) for k in range(nrow)
        )
        gate = jnp.concatenate([hidden_ref[0, m, :cap, :hidden] for m in range(micro)], axis=0)
        up = jnp.concatenate([hidden_ref[0, m, :cap, hidden:] for m in range(micro)], axis=0)
        gate, up = gate.astype(F32), up.astype(F32)
        sigmoid = jax.nn.sigmoid(gate)
        silu = gate * sigmoid
        dhid_ref[:used, :hidden] = (dactive * up * sigmoid * (1.0 + gate * (1.0 - sigmoid))).astype(
            BF16
        )
        dhid_ref[:used, hidden:] = (dactive * silu).astype(BF16)
        dgate, dup = dhid_ref[:used, :hidden], dhid_ref[:used, hidden:]
        for k in range(nrow):
            out_ref[:used, k * cut : (k + 1) * cut] = (
                dot_nt(dgate, gates[k][0]) + dot_nt(dup, ups[k][0])
            ).astype(BF16)
        for m in range(micro):
            total_ref[m] += dot_tn(picks[m], out_ref[m * cap : (m + 1) * cap, :])
        if with_grads:
            active = (silu * up).astype(BF16)
            for m in range(micro):
                out_ref[m * cap : (m + 1) * cap, :] = chosen_ref[0, m, :cap, :]
            for k in range(nrow):
                lanes = slice(k * cut, (k + 1) * cut)
                dgates[k][0] = dot_tn(out_ref[:used, lanes], dgate).astype(BF16)
                dups[k][0] = dot_tn(out_ref[:used, lanes], dup).astype(BF16)
                ddowns[k][0] = dot_tn(active, rows_ref[:used, lanes]).astype(BF16)

    def empty():
        if with_grads:
            for ref in (*dgates, *dups, *ddowns):
                ref[...] = jnp.zeros_like(ref)

    by_load(meta_ref, nrow, body, empty)

    @pl.when(e == pl.num_programs(0) - 1)
    def _():
        store_tokens(meta_ref, dx_ref, total_ref, cut)


def experts_back(meta, place, weight, pieces, gates, ups, downs, chosen, hid, with_grads):
    micro, rows, width = pieces[0].shape
    local = place.shape[0]
    ncol, nrow, hidden = len(pieces), len(gates), gates[0].shape[2]
    tokens = ncol * rows
    weights = [*gates, *ups, *downs]
    at_expert = lambda e: (e, 0, 0, 0)
    out_specs = [pl.BlockSpec((ncol, micro, rows, width), lambda e: (0, 0, 0, 0))]
    out_shape = [jax.ShapeDtypeStruct((ncol, micro, rows, width), BF16)]
    if with_grads:
        out_specs += [pl.BlockSpec((1, *w.shape[1:]), lambda e: (e, 0, 0)) for w in weights]
        out_shape += [jax.ShapeDtypeStruct(w.shape, BF16) for w in weights]
    results = pl.pallas_call(
        functools.partial(experts_back_kernel, ncol, nrow, with_grads),
        grid=(local,),
        in_specs=[
            *expert_specs(pieces, weights, place),
            pl.BlockSpec((1, micro, CAP, width), at_expert),
            pl.BlockSpec((1, micro, CAP, 2 * hidden), at_expert),
        ],
        out_specs=out_specs,
        out_shape=out_shape,
        scratch_shapes=[
            pltpu.VMEM((micro, tokens, width), BF16),
            pltpu.VMEM((micro, tokens, width), F32),
            pltpu.VMEM((micro * CAP, width), BF16),
            pltpu.VMEM((micro * CAP, width), BF16),
            pltpu.VMEM((micro * CAP, 2 * hidden), BF16),
        ],
        compiler_params=pltpu.CompilerParams(vmem_limit_bytes=VMEM_LIMIT),
        cost_estimate=pl.CostEstimate(
            flops=local * micro * 256 * width * (12 * hidden + 4 * tokens),
            bytes_accessed=local * width * (12 * hidden + 4 * micro * CAP),
            transcendentals=local * micro * CAP * hidden,
        ),
    )(meta, place, weight, *pieces, *weights, chosen, hid)
    if not with_grads:
        return results[0], None
    return results[0], (
        results[1 : 1 + nrow],
        results[1 + nrow : 1 + 2 * nrow],
        results[1 + 2 * nrow :],
    )


def forward_layer(layer_in, env, weights):
    micro, rows, width = layer_in.shape
    flat = micro * rows
    prompt = env["prompt"]
    normed, qkv = project(
        layer_in.reshape(flat, width), env["gain_first"], weights["qkv"], env["cos2"], env["sin2"]
    )
    qkv = qkv.reshape(micro, rows, 2 * width)
    own = qkv[:, :, width:]
    blocks = gather_col(own)
    for piece in gather_row(own[:, :prompt])[1:]:
        blocks += gather_col(piece)
    kv = jnp.concatenate(blocks, axis=1)
    mixed, lse = attend(qkv, kv, env["bias"])
    mixed_b = mixed.astype(BF16).reshape(flat, width)
    second = layer_in.reshape(flat, width).astype(F32) + dot_nn(mixed_b, weights["out"])
    second_b = second.astype(BF16)
    wide = second_b.astype(F32)
    rho = lax.rsqrt(jnp.mean(wide * wide, axis=1, keepdims=True) + EPS)
    normed_second = (wide * rho * env["gain_second"]).astype(BF16)
    pieces = gather_col(normed_second.reshape(micro, rows, width))
    partial, chosen, hid = experts(
        env["meta"], env["place"], env["weight"], pieces, *weights["experts"]
    )
    summed = scatter_col([partial[k] for k in range(partial.shape[0])])
    result = second.reshape(micro, rows, width) + summed
    keep = {
        "layer_in": layer_in,
        "normed": normed,
        "qkv": qkv,
        "kv": kv,
        "mixed": mixed,
        "lse": lse,
        "second_b": second_b,
        "chosen": chosen,
        "hid": hid,
    }
    return result, keep


def norm_back(grad, value, gain):
    width = value.shape[1]
    wide = value.astype(F32)
    rho = lax.rsqrt(jnp.mean(wide * wide, axis=1, keepdims=True) + EPS)
    scaled = grad * gain
    inner = jnp.sum(scaled * wide, axis=1, keepdims=True)
    out = rho * scaled - wide * (rho * rho * rho) * (inner / width)
    return out, jnp.sum(grad * wide * rho, axis=0)


def backward_layer(grad_result, keep, env, weights, with_grads):
    micro, rows, width = grad_result.shape
    flat = micro * rows
    prompt = env["prompt"]
    ncol, nrow = lax.axis_size("col"), lax.axis_size("row")
    pieces = gather_col(grad_result.astype(BF16))
    partial, expert_grads = experts_back(
        env["meta"], env["place"], env["weight"], pieces, *weights["experts"],
        keep["chosen"], keep["hid"], with_grads,
    )
    dn2 = scatter_col([partial[k] for k in range(ncol)]).reshape(flat, width)
    dnorm, gain_second = norm_back(dn2, keep["second_b"], env["gain_second"])
    dsecond = grad_result.reshape(flat, width) + dnorm
    dbranch = dsecond.astype(BF16)
    dmixed = dot_nt(dbranch, weights["out"]).astype(BF16)
    dq, dkv = attend_back(
        keep["qkv"], keep["kv"], env["bias"], dmixed.reshape(micro, rows, width), keep["mixed"],
        keep["lse"], env["cos"], env["sin"], env["kcos"], env["ksin"],
    )
    own = scatter_col([dkv[:, k * rows : (k + 1) * rows] for k in range(ncol)])
    parts = [own[:, :prompt]]
    at = ncol * rows
    for _ in range(1, nrow):
        cut = [dkv[:, at + k * prompt : at + (k + 1) * prompt] for k in range(ncol)]
        parts.append(scatter_col(cut).astype(BF16))
        at += ncol * prompt
    own = jnp.concatenate([scatter_row(parts), own[:, prompt:]], axis=1).astype(BF16)
    dqkv = jnp.concatenate([dq, own], axis=2).reshape(flat, 2 * width)
    dn1 = dot_nt(dqkv, weights["qkv"])
    dnorm, gain_first = norm_back(dn1, keep["layer_in"].reshape(flat, width), env["gain_first"])
    grad_in = (dsecond + dnorm).reshape(micro, rows, width)
    if not with_grads:
        return grad_in, None
    return grad_in, {
        "qkv": dot_tn(keep["normed"], dqkv),
        "out": dot_tn(keep["mixed"].astype(BF16).reshape(flat, width), dbranch),
        "experts": expert_grads,
        "gain_first": gain_first,
        "gain_second": gain_second,
    }


def own_rows(value, prompt_rows):
    micro, _, shard = value.shape
    ncol = lax.axis_size("col")
    return jnp.concatenate(
        [
            value[:, :prompt_rows].reshape(micro, ncol, -1, shard),
            value[:, prompt_rows:].reshape(micro, ncol, -1, shard),
        ],
        axis=2,
    )


def to_rows(value, prompt_rows):
    split = own_rows(value, prompt_rows)
    return lax.all_to_all(split, "col", 1, 3, tiled=True)[:, 0]


def to_columns(value, prompt):
    micro, _, width = value.shape
    ncol = lax.axis_size("col")
    split = lax.all_to_all(value[:, None], "col", 3, 1, tiled=True)
    shard = width // ncol
    return jnp.concatenate(
        [
            split[:, :, :prompt].reshape(micro, -1, shard),
            split[:, :, prompt:].reshape(micro, -1, shard),
        ],
        axis=1,
    )


def turn_tables(positions):
    half = HEAD // 2
    freqs = THETA ** (-(jnp.arange(half).astype(F32) * 2.0) / HEAD)
    angles = positions.astype(F32)[:, None] * freqs[None, :]
    cos, sin = jnp.cos(angles), jnp.sin(angles)
    return (
        jnp.concatenate([cos, cos, cos, cos], axis=1),
        jnp.concatenate([-sin, sin, -sin, sin], axis=1),
    )


def small_weights(w_query, w_key, w_value, w_out):
    nrow, ncol = lax.axis_size("row"), lax.axis_size("col")
    cut, columns = w_query.shape
    packed = jnp.concatenate([w_query, w_key, w_value], axis=1)
    whole = lax.all_gather(packed, ("row", "col"), axis=0)
    whole = whole.reshape(nrow, ncol, cut, -1)
    pick = lambda a, b: whole[..., a:b].transpose(0, 2, 1, 3).reshape(nrow * cut, -1)
    kcols = w_key.shape[1]
    query = pick(0, columns)
    key, value = pick(columns, columns + kcols), pick(columns + kcols, columns + 2 * kcols)
    width = nrow * cut
    query = query.reshape(width, -1, 2, 2, HEAD).transpose(0, 1, 3, 2, 4).reshape(width, -1)
    both = jnp.stack([key.reshape(width, -1, 128), value.reshape(width, -1, 128)], axis=2)
    out = lax.all_gather(w_out, ("row", "col"), axis=0)
    out = out.reshape(nrow, ncol, *w_out.shape).transpose(1, 2, 0, 3).reshape(-1, width)
    out = out.reshape(-1, 2, 2, HEAD, width).transpose(0, 2, 1, 3, 4).reshape(-1, width)
    return jnp.concatenate([query, both.reshape(width, -1)], axis=1), out


def small_gradients(grad_qkv, grad_out, cut, columns, kcols):
    nrow, ncol = lax.axis_size("row"), lax.axis_size("col")
    width = grad_out.shape[1]
    heads = nrow * cut
    query = grad_qkv[:, :width].astype(BF16)
    query = query.reshape(heads, -1, 2, 2, HEAD).transpose(0, 1, 3, 2, 4).reshape(heads, -1)
    both = grad_qkv[:, width:].astype(BF16).reshape(heads, -1, 2, 128)
    key, value = both[:, :, 0].reshape(heads, -1), both[:, :, 1].reshape(heads, -1)
    split = lambda g: g.reshape(nrow, cut, ncol, -1).transpose(0, 2, 1, 3)
    packed = jnp.concatenate([split(query), split(key), split(value)], axis=3)
    packed = packed.reshape(nrow * ncol * cut, -1)
    packed = lax.psum_scatter(packed, ("row", "col"), scatter_dimension=0, tiled=True).astype(F32)
    out = grad_out.astype(BF16)
    out = out.reshape(-1, 2, 2, HEAD, width).transpose(0, 2, 1, 3, 4).reshape(ncol, -1, nrow, width // nrow)
    out = out.transpose(2, 0, 1, 3).reshape(-1, width // nrow)
    out = lax.psum_scatter(out, ("row", "col"), scatter_dimension=0, tiled=True).astype(F32)
    return (
        packed[:, :columns],
        packed[:, columns : columns + kcols],
        packed[:, columns + kcols :],
        out,
    )


def routing(expert_ids, gates, prompt_rows, local):
    ncol, col = lax.axis_size("col"), lax.axis_index("col")

    def mine(value):
        blocks = own_rows(value, prompt_rows)
        order = [lax.dynamic_index_in_dim(blocks, col ^ k, 1, False) for k in range(ncol)]
        return jnp.concatenate(order, axis=1).transpose(0, 2, 1)

    ids, scale = mine(expert_ids), mine(gates)
    names = col * local + jnp.arange(local, dtype=jnp.int32)
    match = ids[None] == names[:, None, None, None]
    member = jnp.any(match, axis=2)
    weight = jnp.sum(jnp.where(match, scale[None], 0.0), axis=2)
    tokens = member.shape[2]
    order = jnp.arange(tokens, dtype=jnp.int32)
    earlier = (order[:, None] <= order[None, :]).astype(BF16)
    seen = dot_nn(member.astype(BF16).reshape(-1, tokens), earlier).astype(jnp.int32)
    seen = seen.reshape(member.shape)
    return jnp.where(member, seen - 1, -1), weight, seen[:, :, -1]


def on_device(
    x_in,
    targets,
    w_query,
    w_key,
    w_value,
    w_out,
    w_gate,
    w_up,
    w_down,
    gain_attn,
    gain_ffn,
    expert_ids,
    gates,
    lengths,
):
    section, row, col = (lax.axis_index(name) for name in ("section", "row", "col"))
    nrow, ncol = lax.axis_size("row"), lax.axis_size("col")
    micro, _, tokens, shard = x_in.shape
    width = shard * ncol
    prompt_rows = tokens - CONT_LEN
    prompt_len = prompt_rows * nrow
    prompt, cont = prompt_rows // ncol, CONT_LEN // ncol
    rows = prompt + cont
    local, cut = w_gate.shape[1], w_gate.shape[2]
    first_section = section == 0

    gathered = tuple(gather_row(w[0]) for w in (w_gate, w_up, w_down))
    qkv_weight, out_weight = small_weights(w_query[0], w_key[0], w_value[0], w_out[0])
    weights = {"experts": gathered, "qkv": qkv_weight, "out": out_weight}

    def positions_of(row_index, col_index):
        return row_index * prompt_rows + col_index * prompt + jnp.arange(prompt, dtype=jnp.int32)

    def cont_positions(col_index):
        return prompt_len + col_index * cont + jnp.arange(cont, dtype=jnp.int32)

    positions = jnp.concatenate([positions_of(row, col), cont_positions(col)])
    key_positions = []
    for k in range(ncol):
        key_positions += [positions_of(row, col ^ k), cont_positions(col ^ k)]
    for j in range(1, nrow):
        key_positions += [positions_of((row - j) % nrow, col ^ k) for k in range(ncol)]
    key_positions = jnp.concatenate(key_positions)
    bias = jnp.where(key_positions[:, None] <= jnp.tile(positions, GROUP)[None, :], 0.0, NEG)
    cos, sin = turn_tables(positions)
    kcos, ksin = turn_tables(key_positions)
    place, weight, counts = routing(expert_ids[0, :, 0], gates[0, :, 0], prompt_rows, local)
    starts = ((row - jnp.arange(nrow, dtype=jnp.int32)) % nrow) * cut
    env = {
        "prompt": prompt,
        "gain_first": gain_attn.astype(F32),
        "gain_second": gain_ffn.astype(F32),
        "cos": cos,
        "sin": sin,
        "cos2": jnp.concatenate([cos] * micro, axis=0),
        "sin2": jnp.concatenate([sin] * micro, axis=0),
        "kcos": kcos,
        "ksin": ksin,
        "bias": bias,
        "place": place,
        "weight": weight,
        "meta": jnp.concatenate([starts, counts.reshape(-1)]),
    }

    first_in = to_rows(x_in[:, 0], prompt_rows)
    goal = to_rows(targets[:, 0], prompt_rows).astype(F32)

    mid, _ = forward_layer(first_in, env, weights)
    received = shift(mid.astype(BF16), "section", [(0, 1)])
    layer_in = jnp.where(first_section, first_in, received)
    final, keep = forward_layer(layer_in, env, weights)

    count = (micro * prompt_len + jnp.sum(lengths)).astype(F32)
    length = lax.dynamic_index_in_dim(lengths, row, 1, keepdims=False)
    valid = (positions[None, :] - prompt_len < length[:, None]).astype(F32)[:, :, None]
    diff = (final - goal) * valid
    loss = jnp.where(first_section, 0.0, jnp.sum(diff * diff) / count)
    dfinal = (2.0 / count) * diff

    dmid, _ = backward_layer(dfinal, keep, env, weights, False)
    received = shift(dmid.astype(BF16), "section", [(1, 0)])
    grad_result = jnp.where(first_section, received.astype(F32), dfinal)
    grad_in, grads = backward_layer(grad_result, keep, env, weights, True)

    grad_gate, grad_up, grad_down = (scatter_row(list(g)) for g in grads["experts"])
    grad_query, grad_key, grad_value, grad_out = small_gradients(
        grads["qkv"], grads["out"], w_query.shape[1], w_query.shape[2], w_key.shape[2]
    )
    gains = lax.psum(jnp.stack([grads["gain_first"], grads["gain_second"]]), ("row", "col"))
    gains = lax.dynamic_slice_in_dim(gains, col * shard, shard, 1)
    loss = lax.psum(loss, ("section", "row", "col"))
    outputs = to_columns(final.astype(BF16), prompt)
    input_grads = to_columns(grad_in.astype(BF16), prompt)
    return (
        outputs[None, :, None],
        loss,
        input_grads[None, :, None],
        grad_query[None],
        grad_key[None],
        grad_value[None],
        grad_out[None],
        grad_gate[None],
        grad_up[None],
        grad_down[None],
        gains[:1],
        gains[1:],
    )


def solution(mesh):
    in_specs = (
        P(None, "row", None, "col"),
        P(None, "row", None, "col"),
        P("section", "row", "col"),
        P("section", "row", "col"),
        P("section", "row", "col"),
        P("section", "col", "row"),
        P("section", "col", "row", None),
        P("section", "col", "row", None),
        P("section", "col", None, "row"),
        P("section", None),
        P("section", None),
        P("section", None, "row", None, None),
        P("section", None, "row", None, None),
        P(),
    )
    out_specs = (
        P("section", None, "row", None, "col"),
        P(),
        P("section", None, "row", None, "col"),
        P("section", "row", "col"),
        P("section", "row", "col"),
        P("section", "row", "col"),
        P("section", "col", "row"),
        P("section", "col", "row", None),
        P("section", "col", "row", None),
        P("section", "col", None, "row"),
        P("section", "col"),
        P("section", "col"),
    )
    return jax.shard_map(
        on_device, mesh=mesh, in_specs=in_specs, out_specs=out_specs, check_vma=False
    )
```

```python
import functools

import jax
import jax.numpy as jnp
from jax import lax
from jax.experimental import pallas as pl
from jax.experimental.pallas import tpu as pltpu
from jax.sharding import PartitionSpec as P

HEAD = 64
HIDDEN_SIZE = 512
CONT_LEN = 512
CAP = 384
GROUP = 4

EPS = 1e-06
THETA = 10000.0
NEG = -1e30
BF16 = jnp.bfloat16
F32 = jnp.float32
VMEM_LIMIT = 60 * 1024 * 1024


def shift(value, axis, pairs):
    return lax.ppermute(value, axis, pairs)


def flip(value, bit):
    count = lax.axis_size("col")
    return shift(value, "col", [(i, i ^ bit) for i in range(count)])


def col_bits():
    count = lax.axis_size("col")
    bits = [1]
    while bits[-1] * 2 < count:
        bits.append(bits[-1] * 2)
    return bits


def gather_col(value):
    blocks = {0: value}
    for bit in reversed(col_bits()):
        for k in list(blocks):
            blocks[k ^ bit] = flip(blocks[k], bit)
    return [blocks[k] for k in range(lax.axis_size("col"))]


def scatter_col(blocks):
    blocks = dict(enumerate(blocks))
    total = None
    for bit in col_bits():
        keep = [k for k in blocks if not k & bit]
        total = {k: blocks[k].astype(F32) + flip(blocks[k ^ bit], bit).astype(F32) for k in keep}
        blocks = {k: total[k].astype(BF16) for k in keep}
    return total[0]


def exchange(value):
    return shift(value, "section", [(0, 1), (1, 0)])


def ring(value):
    count = lax.axis_size("row")
    return shift(value, "row", [(i, (i + 1) % count) for i in range(count)])


def gather_row(value):
    count = lax.axis_size("row")
    pieces = [value]
    for k in range(1, count):
        pieces.append(shift(value, "row", [(i, (i + k) % count) for i in range(count)]))
    return pieces


def scatter_row(parts):
    count = len(parts)
    total = parts[0].astype(F32)
    for k in range(1, count):
        pairs = [(i, (i - k) % count) for i in range(count)]
        total = total + shift(parts[k], "row", pairs).astype(F32)
    return total


def total_everywhere(value):
    for bit in col_bits():
        value = value + flip(value, bit)
    count, bit = lax.axis_size("row"), 1
    while bit < count:
        value = value + shift(value, "row", [(i, i ^ bit) for i in range(count)])
        bit *= 2
    return value + exchange(value)


def after(value, *others):
    return lax.optimization_barrier((value, *others))[0]


def dot_nn(left, right):
    return lax.dot_general(left, right, (((1,), (0,)), ((), ())), preferred_element_type=F32)


def dot_nt(left, right):
    return lax.dot_general(left, right, (((1,), (1,)), ((), ())), preferred_element_type=F32)


def dot_tn(left, right):
    return lax.dot_general(left, right, (((0,), (0,)), ((), ())), preferred_element_type=F32)


def swap_halves(value):
    lanes = value.shape[1]
    lane = lax.broadcasted_iota(jnp.int32, value.shape, 1)
    half = HEAD // 2
    ahead = pltpu.roll(value, lanes - half, 1)
    behind = pltpu.roll(value, half, 1)
    return jnp.where(lane % HEAD < half, ahead, behind)


def ordered(value, starts_ref, first, count, cut):
    picks = []
    for k in range(count):
        start = pl.multiple_of(starts_ref[first + k], cut)
        picks.append(value[:, pl.ds(start, cut)])
    return jnp.concatenate(picks, axis=1)


def flat(ref):
    return ref[...].reshape(ref.shape[0] * ref.shape[1], ref.shape[2])


def normalised(value):
    return lax.rsqrt(jnp.mean(value * value, axis=1, keepdims=True) + EPS)


def project_kernel(nblocks, starts_ref, x_ref, gain_ref, cos_ref, sin_ref, *refs):
    blocks, (n_ref, out_ref) = refs[:nblocks], refs[nblocks:]
    nrow, cut = blocks[0].shape[0], blocks[0].shape[1]
    width = x_ref.shape[1]
    x = x_ref[...].astype(F32)
    n_ref[...] = (x * normalised(x) * gain_ref[...]).astype(BF16)
    normed = ordered(n_ref, starts_ref, 0, nrow, cut)
    cos, sin = cos_ref[...], sin_ref[...]
    turn = lambda v: (v * cos + swap_halves(v) * sin).astype(BF16)
    for k, block in enumerate(blocks):
        raw = dot_nn(normed, flat(block))
        start = pl.multiple_of(starts_ref[nrow + k], 256)
        out_ref[:, pl.ds(start, 256)] = jnp.concatenate(
            [turn(raw[:, :128]), turn(raw[:, 128:256])], axis=1
        )
        start = pl.multiple_of(starts_ref[nrow + k] + width, 256)
        out_ref[:, pl.ds(start, 256)] = jnp.concatenate(
            [turn(raw[:, 256:384]), raw[:, 384:].astype(BF16)], axis=1
        )


def close_kernel(nblocks, starts_ref, x_ref, mixed_ref, gain_ref, *refs):
    blocks, (second_ref, n_ref, wide_ref) = refs[:nblocks], refs[nblocks:]
    nrow, cut = blocks[0].shape[0], blocks[0].shape[2]
    wide_ref[...] = mixed_ref[...].astype(BF16)
    mixed = ordered(wide_ref, starts_ref, nrow, nblocks, 256)
    for j in range(nrow):
        weight = jnp.concatenate([block[j] for block in blocks], axis=0)
        lanes = pl.ds(pl.multiple_of(starts_ref[j], cut), cut)
        second_ref[:, lanes] = x_ref[:, lanes].astype(F32) + dot_nn(mixed, weight)
    second = second_ref[...].astype(BF16).astype(F32)
    n_ref[...] = (second * normalised(second) * gain_ref[...]).astype(BF16)


def norm_back(grad, value, gain):
    rho = normalised(value)
    scaled = grad * gain
    inner = jnp.sum(scaled * value, axis=1, keepdims=True)
    out = rho * scaled - value * (rho * rho * rho) * (inner / value.shape[1])
    return out, jnp.sum(grad * value * rho, axis=0, keepdims=True)


def open_back_kernel(nblocks, starts_ref, grad_ref, dn_ref, second_ref, gain_ref, *refs):
    blocks, (dsecond_ref, dbranch_ref, dmixed_ref, dgain_ref) = refs[:nblocks], refs[nblocks:]
    nrow, cut = blocks[0].shape[0], blocks[0].shape[2]
    second = second_ref[...].astype(BF16).astype(F32)
    dnorm, dgain_ref[...] = norm_back(dn_ref[...], second, gain_ref[...])
    dsecond = grad_ref[...].astype(F32) + dnorm
    dsecond_ref[...] = dsecond
    dbranch_ref[...] = dsecond.astype(BF16)
    for k, block in enumerate(blocks):
        total = None
        for j in range(nrow):
            lanes = pl.ds(pl.multiple_of(starts_ref[j], cut), cut)
            term = dot_nt(dbranch_ref[:, lanes], block[j])
            total = term if total is None else total + term
        start = pl.multiple_of(starts_ref[nrow + k], 256)
        dmixed_ref[:, pl.ds(start, 256)] = total.astype(BF16)


def project_back_kernel(nblocks, starts_ref, dq_ref, dkv_ref, x_ref, gain_ref, dsecond_ref, *refs):
    blocks, (dx_ref, dgain_ref, wide_ref) = refs[:nblocks], refs[nblocks:]
    nrow, cut = blocks[0].shape[0], blocks[0].shape[1]
    total = None
    for k, block in enumerate(blocks):
        lanes = pl.ds(pl.multiple_of(starts_ref[nrow + k], 256), 256)
        grad = jnp.concatenate([dq_ref[:, lanes], dkv_ref[:, lanes]], axis=1)
        term = dot_nt(grad, flat(block))
        total = term if total is None else total + term
    for j in range(nrow):
        lanes = pl.ds(pl.multiple_of(starts_ref[j], cut), cut)
        wide_ref[:, lanes] = total[:, j * cut : (j + 1) * cut]
    dnorm, dgain_ref[...] = norm_back(wide_ref[...], x_ref[...].astype(F32), gain_ref[...])
    dx_ref[...] = (dsecond_ref[...] + dnorm).astype(BF16)


def weight_back_kernel(nblocks, starts_ref, n_ref, dq_ref, dkv_ref, mixed_ref, dbranch_ref, *refs):
    qkvs, outs = refs[:nblocks], refs[nblocks : 2 * nblocks]
    nrow, cut = qkvs[0].shape[0], qkvs[0].shape[1]
    normed = ordered(n_ref, starts_ref, 0, nrow, cut)
    for k in range(nblocks):
        lanes = pl.ds(pl.multiple_of(starts_ref[nrow + k], 256), 256)
        grad = jnp.concatenate([dq_ref[:, lanes], dkv_ref[:, lanes]], axis=1)
        qkvs[k][...] = dot_tn(normed, grad).astype(BF16).reshape(qkvs[k].shape)
        mixed = mixed_ref[:, lanes].astype(BF16)
        for j in range(nrow):
            there = pl.ds(pl.multiple_of(starts_ref[j], cut), cut)
            outs[k][j] = dot_tn(mixed, dbranch_ref[:, there]).astype(BF16)


def whole_call(kernel, out_shape, starts, operands, blocks, lanes, scratch=(), flops=0):
    start, count = lanes
    specs = [pl.BlockSpec(memory_space=pltpu.SMEM)]
    specs += [pl.BlockSpec(memory_space=pltpu.VMEM) for _ in operands]
    specs += [
        pl.BlockSpec((*b.shape[:2], count), lambda i: (0, 0, start // count)) for b in blocks
    ]
    specs[1 : 1 + len(operands)] = [
        pl.BlockSpec(o.shape, lambda i, n=o.ndim: (0,) * n) for o in operands
    ]
    return pl.pallas_call(
        functools.partial(kernel, len(blocks)),
        grid=(1,),
        in_specs=specs,
        out_specs=[pl.BlockSpec(o.shape, lambda i, n=len(o.shape): (0,) * n) for o in out_shape],
        out_shape=out_shape,
        scratch_shapes=scratch,
        compiler_params=pltpu.CompilerParams(vmem_limit_bytes=VMEM_LIMIT),
        cost_estimate=pl.CostEstimate(
            flops=flops,
            bytes_accessed=8 * 1024 * 1024,
            transcendentals=0,
        ),
    )(starts, *operands, *blocks)


def project(x, gain, cos, sin, part):
    rows, width = x.shape
    shapes = [
        jax.ShapeDtypeStruct((rows, width), BF16),
        jax.ShapeDtypeStruct((rows, 2 * width), BF16),
    ]
    return whole_call(
        project_kernel, shapes, part["starts"], (x, gain, cos, sin), part["qkv"], (0, 512),
        flops=4 * rows * width * width,
    )


def close_attention(x, mixed, gain, part):
    rows, width = x.shape
    shapes = [jax.ShapeDtypeStruct((rows, width), F32), jax.ShapeDtypeStruct((rows, width), BF16)]
    return whole_call(
        close_kernel, shapes, part["starts"], (x, mixed, gain), part["out"], part["out_lanes"],
        [pltpu.VMEM((rows, width), BF16)], 2 * rows * width * width,
    )


def open_back(grad, dn, second, gain, part):
    rows, width = grad.shape
    shapes = [
        jax.ShapeDtypeStruct((rows, width), F32),
        jax.ShapeDtypeStruct((rows, width), BF16),
        jax.ShapeDtypeStruct((rows, width), BF16),
        jax.ShapeDtypeStruct((1, width), F32),
    ]
    return whole_call(
        open_back_kernel, shapes, part["starts"], (grad, dn, second, gain), part["out"],
        part["out_lanes"], flops=2 * rows * width * width,
    )


def project_back(dq, dkv, x, gain, dsecond, part):
    rows, width = x.shape
    shapes = [jax.ShapeDtypeStruct((rows, width), BF16), jax.ShapeDtypeStruct((1, width), F32)]
    return whole_call(
        project_back_kernel, shapes, part["starts"], (dq, dkv, x, gain, dsecond), part["qkv"],
        (0, 512), [pltpu.VMEM((rows, width), F32)], 4 * rows * width * width,
    )


def weight_back(normed, dq, dkv, mixed, dbranch, part):
    rows, width = normed.shape
    nblocks = len(part["qkv"])
    nrow, cut = part["qkv"][0].shape[:2]
    shapes = [jax.ShapeDtypeStruct((nrow, cut, 512), BF16)] * nblocks
    shapes += [jax.ShapeDtypeStruct((nrow, 256, width // nrow), BF16)] * nblocks
    operands = (normed, dq, dkv, mixed, dbranch)
    grads = pl.pallas_call(
        functools.partial(weight_back_kernel, nblocks),
        in_specs=[pl.BlockSpec(memory_space=pltpu.SMEM)]
        + [pl.BlockSpec(memory_space=pltpu.VMEM)] * len(operands),
        out_specs=[pl.BlockSpec(memory_space=pltpu.VMEM)] * len(shapes),
        out_shape=shapes,
        compiler_params=pltpu.CompilerParams(vmem_limit_bytes=VMEM_LIMIT),
        cost_estimate=pl.CostEstimate(
            flops=6 * rows * width * width, bytes_accessed=8 * 1024 * 1024, transcendentals=0
        ),
    )(part["starts"], *operands)
    return grads[:nblocks], grads[nblocks:]


def stack_heads(value):
    low = (lax.broadcasted_iota(jnp.int32, (value.shape[0], 128), 1) < HEAD).astype(F32)
    first, second = value[:, :128].astype(F32), value[:, 128:].astype(F32)
    return jnp.concatenate(
        [first * low, second * low, first * (1.0 - low), second * (1.0 - low)], axis=0
    )


def unstack_heads(value):
    rows = value.shape[0] // 4
    low = lax.broadcasted_iota(jnp.int32, (rows, 128), 1) < HEAD
    first = jnp.where(low, value[:rows], value[2 * rows : 3 * rows])
    second = jnp.where(low, value[rows : 2 * rows], value[3 * rows :])
    return first, second


def attend_kernel(q_ref, k_ref, v_ref, bias_ref, o_ref, lse_ref):
    stacked = (stack_heads(q_ref[0]) * HEAD**-0.5).astype(BF16)
    scores = dot_nt(k_ref[0], stacked) + bias_ref[...]
    top = jnp.max(scores, axis=0, keepdims=True)
    weights = jnp.exp(scores - top)
    total = jnp.sum(weights, axis=0, keepdims=True)
    mixed = dot_tn(v_ref[0], weights.astype(BF16)) / total
    first, second = unstack_heads(mixed.T)
    o_ref[0, :, :128] = first
    o_ref[0, :, 128:] = second
    lse_ref[0, 0] = top + jnp.log(total)


def attend(qkv, kv, bias):
    micro, rows, _ = qkv.shape
    keys, width = kv.shape[1], kv.shape[2]
    groups = width // 256
    return pl.pallas_call(
        attend_kernel,
        grid=(micro, groups),
        in_specs=[
            pl.BlockSpec((1, rows, 256), lambda m, g: (m, 0, g)),
            pl.BlockSpec((1, keys, 128), lambda m, g: (m, 0, 2 * g)),
            pl.BlockSpec((1, keys, 128), lambda m, g: (m, 0, 2 * g + 1)),
            pl.BlockSpec((keys, 4 * rows), lambda m, g: (0, 0)),
        ],
        out_specs=[
            pl.BlockSpec((1, rows, 256), lambda m, g: (m, 0, g)),
            pl.BlockSpec((1, 1, 1, 4 * rows), lambda m, g: (m, g, 0, 0)),
        ],
        out_shape=[
            jax.ShapeDtypeStruct((micro, rows, groups * 256), F32),
            jax.ShapeDtypeStruct((micro, groups, 1, 4 * rows), F32),
        ],
        compiler_params=pltpu.CompilerParams(vmem_limit_bytes=VMEM_LIMIT),
        cost_estimate=pl.CostEstimate(
            flops=micro * groups * 4 * rows * keys * 128 * 4,
            bytes_accessed=2 * micro * keys * width + 4 * keys * 4 * rows,
            transcendentals=micro * groups * 4 * rows * keys,
        ),
    )(qkv, kv, kv, bias)


def attend_back_kernel(
    q_ref, k_ref, v_ref, bias_ref, do_ref, o_ref, lse_ref, cos_ref, sin_ref, kcos_ref, ksin_ref,
    dq_ref, dkv_ref,
):
    scale = HEAD**-0.5
    queries = (stack_heads(q_ref[0]) * scale).astype(BF16)
    grads_wide = stack_heads(do_ref[0])
    product = grads_wide * stack_heads(o_ref[0])
    delta = jnp.sum(product.T, axis=0, keepdims=True)
    grads = grads_wide.astype(BF16)
    keys, values = k_ref[0], v_ref[0]
    probs = jnp.exp(dot_nt(keys, queries) + bias_ref[...] - lse_ref[0, 0])
    dvalues = dot_nn(probs.astype(BF16), grads)
    dscores = (probs * (dot_nt(values, grads) - delta)).astype(BF16)
    dkeys = dot_nn(dscores, queries)
    dqueries = dot_tn(keys, dscores) * scale
    first, second = unstack_heads(dqueries.T)
    cos, sin = cos_ref[...], sin_ref[...]
    dq_ref[0, :, :128] = (first * cos - swap_halves(first) * sin).astype(BF16)
    dq_ref[0, :, 128:] = (second * cos - swap_halves(second) * sin).astype(BF16)
    dkv_ref[0, :, :128] = (dkeys * kcos_ref[...] - swap_halves(dkeys) * ksin_ref[...]).astype(BF16)
    dkv_ref[0, :, 128:] = dvalues.astype(BF16)


def attend_back(qkv, kv, bias, grad, o, lse, cos, sin, kcos, ksin):
    micro, rows, _ = qkv.shape
    keys, width = kv.shape[1], kv.shape[2]
    groups = width // 256
    mine = pl.BlockSpec((1, rows, 256), lambda m, g: (m, 0, g))
    return pl.pallas_call(
        attend_back_kernel,
        grid=(micro, groups),
        in_specs=[
            mine,
            pl.BlockSpec((1, keys, 128), lambda m, g: (m, 0, 2 * g)),
            pl.BlockSpec((1, keys, 128), lambda m, g: (m, 0, 2 * g + 1)),
            pl.BlockSpec((keys, 4 * rows), lambda m, g: (0, 0)),
            mine,
            mine,
            pl.BlockSpec((1, 1, 1, 4 * rows), lambda m, g: (m, g, 0, 0)),
            pl.BlockSpec((rows, 128), lambda m, g: (0, 0)),
            pl.BlockSpec((rows, 128), lambda m, g: (0, 0)),
            pl.BlockSpec((keys, 128), lambda m, g: (0, 0)),
            pl.BlockSpec((keys, 128), lambda m, g: (0, 0)),
        ],
        out_specs=[mine, pl.BlockSpec((1, keys, 256), lambda m, g: (m, 0, g))],
        out_shape=[
            jax.ShapeDtypeStruct((micro, rows, groups * 256), BF16),
            jax.ShapeDtypeStruct((micro, keys, width), BF16),
        ],
        compiler_params=pltpu.CompilerParams(vmem_limit_bytes=VMEM_LIMIT),
        cost_estimate=pl.CostEstimate(
            flops=micro * groups * 4 * rows * keys * 128 * 10,
            bytes_accessed=4 * micro * keys * width + 4 * keys * 4 * rows,
            transcendentals=micro * groups * 4 * rows * keys,
        ),
    )(qkv, kv, kv, bias, grad, o, lse, cos, sin, kcos, ksin)


def chosen_rows(place_ref, weight_ref, m, cap, tokens):
    slots = lax.broadcasted_iota(jnp.int32, (cap, tokens), 0)
    hit = slots == place_ref[0, m : m + 1, :]
    pick = jnp.where(hit, 1.0, 0.0)
    weight = jnp.sum(pick * weight_ref[0, m : m + 1, :], axis=1, keepdims=True)
    return pick.astype(BF16), weight


def load_tokens(pieces, scratch):
    for at, piece in enumerate(pieces):
        rows = piece.shape[1]
        scratch[:, at * rows : (at + 1) * rows, :] = piece[...]


def store_tokens(out_ref, total):
    blocks, _, rows, _ = out_ref.shape
    for at in range(blocks):
        out_ref[at] = total[:, at * rows : (at + 1) * rows, :].astype(BF16)


def by_load(counts_ref, body, empty=None):
    e = pl.program_id(0)
    most = jnp.maximum(counts_ref[2 * e], counts_ref[2 * e + 1])
    below = 0
    for cap in (CAP // 3, 2 * CAP // 3, CAP):
        pl.when((most > below) & (most <= cap))(functools.partial(body, cap))
        below = cap
    if empty is not None:
        pl.when(most == 0)(empty)


def experts_kernel(ncol, counts_ref, place_ref, weight_ref, *refs):
    pieces, refs = refs[:ncol], refs[ncol:]
    gate_ref, up_ref, down_ref, y_ref, chosen_ref, hidden_ref, tokens_ref, total_ref, rows_ref, out_ref = refs
    micro, tokens, _ = tokens_ref.shape
    hidden = gate_ref.shape[2]
    e = pl.program_id(0)

    @pl.when(e == 0)
    def _():
        load_tokens(pieces, tokens_ref)
        total_ref[...] = jnp.zeros_like(total_ref)

    def body(cap):
        picks, weights = [], []
        for m in range(micro):
            pick, weight = chosen_rows(place_ref, weight_ref, m, cap, tokens)
            chosen = dot_nn(pick, tokens_ref[m]).astype(BF16)
            rows_ref[m * cap : (m + 1) * cap, :] = chosen
            chosen_ref[0, m, :cap, :] = chosen
            picks.append(pick)
            weights.append(weight)
        used = micro * cap
        gate = dot_nn(rows_ref[:used, :], gate_ref[0])
        up = dot_nn(rows_ref[:used, :], up_ref[0])
        for m in range(micro):
            hidden_ref[0, m, :cap, :hidden] = gate[m * cap : (m + 1) * cap].astype(BF16)
            hidden_ref[0, m, :cap, hidden:] = up[m * cap : (m + 1) * cap].astype(BF16)
        active = (gate * jax.nn.sigmoid(gate) * up).astype(BF16)
        scale = jnp.concatenate(weights, axis=0)
        out_ref[:used, :] = (dot_nn(active, down_ref[0]) * scale).astype(BF16)
        for m in range(micro):
            total_ref[m] += dot_tn(picks[m], out_ref[m * cap : (m + 1) * cap, :])

    by_load(counts_ref, body)

    @pl.when(e == pl.num_programs(0) - 1)
    def _():
        store_tokens(y_ref, total_ref)


def expert_specs(pieces, weights, slots):
    micro, rows, width = pieces[0].shape
    at_expert = lambda e: (e, 0, 0)
    specs = [
        pl.BlockSpec(memory_space=pltpu.SMEM),
        pl.BlockSpec((1, *slots.shape[1:]), at_expert),
        pl.BlockSpec((1, *slots.shape[1:]), at_expert),
    ]
    specs += [pl.BlockSpec((micro, rows, width), lambda e: (0, 0, 0)) for _ in pieces]
    specs += [pl.BlockSpec((1, *w.shape[1:]), at_expert) for w in weights]
    return specs


def experts(counts, place, weight, pieces, weights):
    micro, rows, width = pieces[0].shape
    local, hidden = weights[0].shape[0], weights[0].shape[2]
    ncol = len(pieces)
    tokens = ncol * rows
    at_expert = lambda e: (e, 0, 0, 0)
    return pl.pallas_call(
        functools.partial(experts_kernel, ncol),
        grid=(local,),
        in_specs=expert_specs(pieces, weights, place),
        out_specs=[
            pl.BlockSpec((ncol, micro, rows, width), lambda e: (0, 0, 0, 0)),
            pl.BlockSpec((1, micro, CAP, width), at_expert),
            pl.BlockSpec((1, micro, CAP, 2 * hidden), at_expert),
        ],
        out_shape=[
            jax.ShapeDtypeStruct((ncol, micro, rows, width), BF16),
            jax.ShapeDtypeStruct((local, micro, CAP, width), BF16),
            jax.ShapeDtypeStruct((local, micro, CAP, 2 * hidden), BF16),
        ],
        scratch_shapes=[
            pltpu.VMEM((micro, tokens, width), BF16),
            pltpu.VMEM((micro, tokens, width), F32),
            pltpu.VMEM((micro * CAP, width), BF16),
            pltpu.VMEM((micro * CAP, width), BF16),
        ],
        compiler_params=pltpu.CompilerParams(vmem_limit_bytes=VMEM_LIMIT),
        cost_estimate=pl.CostEstimate(
            flops=local * micro * 256 * width * (6 * hidden + 4 * tokens),
            bytes_accessed=local * width * (6 * hidden + 4 * micro * CAP),
            transcendentals=local * micro * CAP * hidden,
        ),
    )(counts, place, weight, *pieces, *weights)


def experts_back_kernel(ncol, counts_ref, place_ref, weight_ref, *refs):
    pieces, refs = refs[:ncol], refs[ncol:]
    gate_ref, up_ref, down_ref, chosen_ref, hidden_ref, dx_ref, dgate_ref, dup_ref, ddown_ref, *refs = refs
    tokens_ref, total_ref, rows_ref, out_ref, dhid_ref = refs
    micro, tokens, _ = tokens_ref.shape
    hidden = gate_ref.shape[2]
    e = pl.program_id(0)

    @pl.when(e == 0)
    def _():
        load_tokens(pieces, tokens_ref)
        total_ref[...] = jnp.zeros_like(total_ref)

    def body(cap):
        picks = []
        for m in range(micro):
            pick, weight = chosen_rows(place_ref, weight_ref, m, cap, tokens)
            picks.append(pick)
            rows_ref[m * cap : (m + 1) * cap, :] = (
                dot_nn(pick, tokens_ref[m]) * weight
            ).astype(BF16)
        used = micro * cap
        dactive = dot_nt(rows_ref[:used, :], down_ref[0])
        gate = jnp.concatenate([hidden_ref[0, m, :cap, :hidden] for m in range(micro)], axis=0)
        up = jnp.concatenate([hidden_ref[0, m, :cap, hidden:] for m in range(micro)], axis=0)
        gate, up = gate.astype(F32), up.astype(F32)
        sigmoid = jax.nn.sigmoid(gate)
        silu = gate * sigmoid
        dhid_ref[:used, :hidden] = (dactive * up * sigmoid * (1.0 + gate * (1.0 - sigmoid))).astype(
            BF16
        )
        dhid_ref[:used, hidden:] = (dactive * silu).astype(BF16)
        dgate, dup = dhid_ref[:used, :hidden], dhid_ref[:used, hidden:]
        out_ref[:used, :] = (dot_nt(dgate, gate_ref[0]) + dot_nt(dup, up_ref[0])).astype(BF16)
        for m in range(micro):
            total_ref[m] += dot_tn(picks[m], out_ref[m * cap : (m + 1) * cap, :])
        active = (silu * up).astype(BF16)
        for m in range(micro):
            out_ref[m * cap : (m + 1) * cap, :] = chosen_ref[0, m, :cap, :]
        dgate_ref[0] = dot_tn(out_ref[:used, :], dgate).astype(BF16)
        dup_ref[0] = dot_tn(out_ref[:used, :], dup).astype(BF16)
        ddown_ref[0] = dot_tn(active, rows_ref[:used, :]).astype(BF16)

    def empty():
        for ref in (dgate_ref, dup_ref, ddown_ref):
            ref[...] = jnp.zeros_like(ref)

    by_load(counts_ref, body, empty)

    @pl.when(e == pl.num_programs(0) - 1)
    def _():
        store_tokens(dx_ref, total_ref)


def experts_back(counts, place, weight, pieces, weights, chosen, hid):
    micro, rows, width = pieces[0].shape
    local, hidden = weights[0].shape[0], weights[0].shape[2]
    ncol = len(pieces)
    tokens = ncol * rows
    at_expert = lambda e: (e, 0, 0, 0)
    return pl.pallas_call(
        functools.partial(experts_back_kernel, ncol),
        grid=(local,),
        in_specs=[
            *expert_specs(pieces, weights, place),
            pl.BlockSpec((1, micro, CAP, width), at_expert),
            pl.BlockSpec((1, micro, CAP, 2 * hidden), at_expert),
        ],
        out_specs=[
            pl.BlockSpec((ncol, micro, rows, width), lambda e: (0, 0, 0, 0)),
            *[pl.BlockSpec((1, *w.shape[1:]), lambda e: (e, 0, 0)) for w in weights],
        ],
        out_shape=[
            jax.ShapeDtypeStruct((ncol, micro, rows, width), BF16),
            *[jax.ShapeDtypeStruct(w.shape, BF16) for w in weights],
        ],
        scratch_shapes=[
            pltpu.VMEM((micro, tokens, width), BF16),
            pltpu.VMEM((micro, tokens, width), F32),
            pltpu.VMEM((micro * CAP, width), BF16),
            pltpu.VMEM((micro * CAP, width), BF16),
            pltpu.VMEM((micro * CAP, 2 * hidden), BF16),
        ],
        compiler_params=pltpu.CompilerParams(vmem_limit_bytes=VMEM_LIMIT),
        cost_estimate=pl.CostEstimate(
            flops=local * micro * 256 * width * (12 * hidden + 4 * tokens),
            bytes_accessed=local * width * (12 * hidden + 4 * micro * CAP),
            transcendentals=local * micro * CAP * hidden,
        ),
    )(counts, place, weight, *pieces, *weights, chosen, hid)


def spread_rows(value):
    both = jnp.stack([value, exchange(value)])
    return gather_col(both)


def collect_rows(partial):
    blocks = [partial[k] for k in range(partial.shape[0])]
    theirs = exchange(scatter_col([b[1] for b in blocks]).astype(BF16))
    return scatter_col([b[0] for b in blocks]) + theirs.astype(F32)


def forward_layer(layer_in, env, part):
    rows, width = layer_in.shape
    prompt = env["prompt"]
    normed, qkv = project(layer_in, part["gain_first"], env["cos"], env["sin"], part)
    own = qkv[:, width:]
    near = gather_col(own)
    far = gather_col(jnp.concatenate(gather_row(own[:prompt])[1:], axis=0))
    kv = jnp.concatenate([b for pair in zip(near, far) for b in pair], axis=0)
    mixed, lse = attend(qkv[None], kv[None], env["bias"])
    second, normed_second = close_attention(layer_in, mixed[0], part["gain_second"], part)
    pieces = spread_rows(normed_second)
    partial, chosen, hid = experts(*part["slots"], pieces, part["experts"])
    result = second + collect_rows(partial)
    keep = {
        "layer_in": layer_in,
        "normed": normed,
        "qkv": qkv,
        "kv": kv,
        "mixed": mixed,
        "lse": lse,
        "second": second,
        "pieces": pieces[-1],
        "chosen": chosen,
        "hid": hid,
    }
    return result, keep


def backward_layer(grad_result, keep, env, part):
    rows, _ = grad_result.shape
    prompt = env["prompt"]
    ncol, nrow = lax.axis_size("col"), lax.axis_size("row")
    pieces = spread_rows(grad_result.astype(BF16))
    partial, *expert_grads = experts_back(
        *part["slots"], pieces, part["experts"], keep["chosen"], keep["hid"]
    )
    dn2 = collect_rows(partial)
    dsecond, dbranch, dmixed, gain_second = open_back(
        grad_result, dn2, keep["second"], part["gain_second"], part
    )
    dq, dkv = attend_back(
        keep["qkv"][None], keep["kv"][None], env["bias"], dmixed[None], keep["mixed"],
        keep["lse"], env["cos"], env["sin"], env["kcos"], env["ksin"],
    )
    span = dkv.shape[1] // ncol
    own = scatter_col([dkv[0, k * span : (k + 1) * span] for k in range(ncol)])
    parts = [own[:prompt]]
    for j in range(1, nrow):
        at = rows + (j - 1) * prompt
        parts.append(own[at : at + prompt].astype(BF16))
    own = jnp.concatenate([scatter_row(parts), own[prompt:rows]], axis=0).astype(BF16)
    grad_in, gain_first = project_back(
        dq[0], own, keep["layer_in"], part["gain_first"], dsecond, part
    )
    small = weight_back(keep["normed"], dq[0], own, keep["mixed"][0], dbranch, part)
    return grad_in, {
        "small": small,
        "experts": expert_grads,
        "gain_first": gain_first[0],
        "gain_second": gain_second[0],
    }


def own_rows(value, prompt_rows):
    micro, _, shard = value.shape
    ncol = lax.axis_size("col")
    return jnp.concatenate(
        [
            value[:, :prompt_rows].reshape(micro, ncol, -1, shard),
            value[:, prompt_rows:].reshape(micro, ncol, -1, shard),
        ],
        axis=2,
    )


def to_rows(value, prompt_rows):
    split = own_rows(value, prompt_rows)
    return lax.all_to_all(split, "col", 1, 3, tiled=True)[:, 0]


def to_columns(value, prompt):
    micro, _, width = value.shape
    ncol = lax.axis_size("col")
    split = lax.all_to_all(value[:, None], "col", 3, 1, tiled=True)
    shard = width // ncol
    return jnp.concatenate(
        [
            split[:, :, :prompt].reshape(micro, -1, shard),
            split[:, :, prompt:].reshape(micro, -1, shard),
        ],
        axis=1,
    )


def turn_tables(positions):
    half = HEAD // 2
    freqs = THETA ** (-(jnp.arange(half).astype(F32) * 2.0) / HEAD)
    angles = positions.astype(F32)[:, None] * freqs[None, :]
    cos, sin = jnp.cos(angles), jnp.sin(angles)
    return (
        jnp.concatenate([cos, cos, cos, cos], axis=1),
        jnp.concatenate([-sin, sin, -sin, sin], axis=1),
    )


def small_weights(packed, w_rows, early):
    nrow, ncol = lax.axis_size("row"), lax.axis_size("col")
    row, col = lax.axis_index("row"), lax.axis_index("col")
    cut = packed.shape[0]
    starts = ((row - jnp.arange(nrow, dtype=jnp.int32)) % nrow) * cut
    if early:
        pieces = [packed]
        for _ in range(nrow - 1):
            pieces.append(ring(pieces[-1]))
    else:
        pieces = gather_row(packed)
    blocks = gather_col(jnp.stack(pieces))
    if w_rows == 256:
        order = (col ^ jnp.arange(ncol, dtype=jnp.int32)) * 256
        lanes = (512, 256)
        return {"starts": jnp.concatenate([starts, order]), "qkv": blocks, "out": blocks, "out_lanes": lanes}
    blocks = jnp.stack(blocks)
    whole = [lax.dynamic_index_in_dim(blocks, col ^ c, 0, False) for c in range(ncol)]
    qkv, out = [], []
    for a, b in zip(whole[::2], whole[1::2]):
        heads = [a[..., :64], b[..., :64], a[..., 64:128], b[..., 64:128]]
        others = [a[..., 128:192], b[..., 128:192], a[..., 192:256], b[..., 192:256]]
        qkv.append(jnp.concatenate(heads + others, axis=2))
        a, b = a[..., 256:], b[..., 256:]
        out.append(jnp.concatenate([a[:, :64], b[:, :64], a[:, 64:], b[:, 64:]], axis=1))
    order = jnp.arange(len(qkv), dtype=jnp.int32) * 256
    return {"starts": jnp.concatenate([starts, order]), "qkv": qkv, "out": out, "out_lanes": (0, cut)}


def pack_weights(w_query, w_key, w_value, w_out):
    if w_out.shape[0] == 256:
        heads = lambda v: [v[..., :64], v[..., 128:192], v[..., 64:128], v[..., 192:]]
        rows = [w_out[:64], w_out[128:192], w_out[64:128], w_out[192:]]
        w_out = jnp.concatenate(rows, axis=0)
        w_query = jnp.concatenate(heads(w_query), axis=1)
    return jnp.concatenate([w_query, w_key, w_value, w_out], axis=1)


def small_gradients(qkv, out, w_rows):
    nrow, ncol = lax.axis_size("row"), lax.axis_size("col")
    col = lax.axis_index("col")
    if w_rows == 256:
        blocks = [jnp.concatenate([a, b], axis=2) for a, b in zip(qkv, out)]
    else:
        whole = []
        for a, b in zip(qkv, out):
            for c in (0, 1):
                at = lambda i: a[..., 64 * i : 64 * i + 64]
                heads = [at(c), at(2 + c), at(4 + c), at(6 + c)]
                rows = jnp.concatenate(
                    [b[:, 64 * c : 64 * c + 64], b[:, 128 + 64 * c : 192 + 64 * c]], axis=1
                )
                whole.append(jnp.concatenate([*heads, rows], axis=2))
        whole = jnp.stack(whole)
        blocks = [lax.dynamic_index_in_dim(whole, col ^ k, 0, False) for k in range(ncol)]
    mine = scatter_col(blocks).astype(BF16)
    return scatter_row([mine[j] for j in range(nrow)]).astype(BF16)


def routing(ids, scale, prompt_rows, first, local):
    ncol, col = lax.axis_size("col"), lax.axis_index("col")

    def mine(value):
        blocks = own_rows(value, prompt_rows)
        order = [lax.dynamic_index_in_dim(blocks, col ^ k, 1, False) for k in range(ncol)]
        return jnp.concatenate(order, axis=1).transpose(0, 2, 1)

    ids, scale = mine(ids), mine(scale)
    names = first + jnp.arange(local, dtype=jnp.int32)
    match = ids[None] == names[:, None, None, None]
    member = jnp.any(match, axis=2)
    weight = jnp.sum(jnp.where(match, scale[None], 0.0), axis=2)
    tokens = member.shape[2]
    order = jnp.arange(tokens, dtype=jnp.int32)
    earlier = (order[:, None] <= order[None, :]).astype(BF16)
    seen = dot_nn(member.astype(BF16).reshape(-1, tokens), earlier).astype(jnp.int32)
    seen = seen.reshape(member.shape)
    return seen[:, :, -1].reshape(-1), jnp.where(member, seen - 1, -1), weight


def on_device(
    x_in,
    targets,
    w_query,
    w_key,
    w_value,
    w_out,
    w_gate,
    w_up,
    w_down,
    gain_attn,
    gain_ffn,
    expert_ids,
    gates,
    lengths,
):
    section, row, col = (lax.axis_index(name) for name in ("section", "row", "col"))
    nrow, ncol = lax.axis_size("row"), lax.axis_size("col")
    micro, _, tokens, shard = x_in.shape
    width = shard * ncol
    prompt_rows = tokens - CONT_LEN
    prompt_len = prompt_rows * nrow
    prompt, cont = prompt_rows // ncol, CONT_LEN // ncol
    local = w_gate.shape[1]
    half = local // 2
    columns, kcols = w_query.shape[2], w_key.shape[2]
    home = [section == 0, section == 1]

    def by_layer(value):
        other = exchange(value)
        return [jnp.where(is_home, value, other) for is_home in home]

    w_rows = w_out.shape[1]
    packed = by_layer(pack_weights(w_query[0], w_key[0], w_value[0], w_out[0]))
    big = [w[0] for w in (w_gate, w_up, w_down)]
    crossed = [exchange(after(w[half:], packed[0])) for w in big]
    shards = [
        [jnp.where(is_home, w[:half], c) for w, c in zip(big, crossed)] for is_home in home
    ]
    ids_layer, gates_layer = by_layer(expert_ids[0, :, 0]), by_layer(gates[0, :, 0])
    gains = by_layer(jnp.concatenate([gain_attn, gain_ffn]).astype(F32))

    def whole(pieces):
        return [
            lax.all_gather(w, "row", axis=axis, tiled=True) for w, axis in zip(pieces, (1, 1, 2))
        ]

    def layer_part(layer, held):
        own_first = lambda v: jnp.where(home[0], v, v[::-1])
        first = col * local + jnp.where(home[layer], 0, half)
        ids, scale = own_first(ids_layer[layer]), own_first(gates_layer[layer])
        return {
            "experts": held,
            "gain_first": gains[layer][:1],
            "gain_second": gains[layer][1:],
            "slots": routing(ids, scale, prompt_rows, first, half),
        }

    parts = [layer_part(0, whole(shards[0]))]
    parts[0].update(small_weights(packed[0], w_rows, True))
    later = lax.optimization_barrier((shards[1], parts[0]["experts"][0]))[0]
    parts.append(layer_part(1, whole(later)))

    def prompt_positions(row_index, col_index):
        return row_index * prompt_rows + col_index * prompt + jnp.arange(prompt, dtype=jnp.int32)

    def cont_positions(col_index):
        return prompt_len + col_index * cont + jnp.arange(cont, dtype=jnp.int32)

    positions = jnp.concatenate([prompt_positions(row, col), cont_positions(col)])
    key_positions = []
    for k in range(ncol):
        key_positions += [prompt_positions(row, col ^ k), cont_positions(col ^ k)]
        key_positions += [prompt_positions((row - j) % nrow, col ^ k) for j in range(1, nrow)]
    key_positions = jnp.concatenate(key_positions)
    bias = jnp.where(key_positions[:, None] <= jnp.tile(positions, GROUP)[None, :], 0.0, NEG)
    cos, sin = turn_tables(positions)
    kcos, ksin = turn_tables(key_positions)
    env = {"prompt": prompt, "cos": cos, "sin": sin, "kcos": kcos, "ksin": ksin, "bias": bias}

    mine = lambda v: lax.dynamic_index_in_dim(v, section, 0, keepdims=True)
    first_in = to_rows(mine(x_in[:, 0]), prompt_rows)[0]
    goal = to_rows(mine(targets[:, 0]), prompt_rows)[0].astype(F32)

    result, keep_first = forward_layer(first_in, env, parts[0])
    mid = result.astype(BF16)
    parts[1].update(small_weights(after(packed[1], keep_first["pieces"]), w_rows, False))
    final, keep_last = forward_layer(mid, env, parts[1])

    count = (micro * prompt_len + jnp.sum(lengths)).astype(F32)
    length = lengths[section, row]
    valid = (positions - prompt_len < length).astype(F32)[:, None]
    diff = (final - goal) * valid
    loss = jnp.sum(diff * diff) / count
    dfinal = (2.0 / count) * diff

    dmid, last_grads = backward_layer(dfinal, keep_last, env, parts[1])
    dx, first_grads = backward_layer(dmid, keep_first, env, parts[0])

    layer_grads = [first_grads, last_grads]

    def over_rows(j, layer, *earlier):
        grad = after(layer_grads[layer]["experts"][j], *earlier)
        return lax.psum_scatter(grad, "row", scatter_dimension=(1, 1, 2)[j], tiled=True)

    returned = []

    def expert_gradient(j):
        last = over_rows(j, 1)
        back = shift(last, "section", [(0, 1)])
        first = over_rows(j, 0, back)
        returned.append(shift(first, "section", [(1, 0)]))
        own = jnp.where(home[0], first, last)
        other = jnp.where(home[0], returned[-1], back)
        return jnp.concatenate([own, other], axis=0).astype(F32)

    grad_gate, grad_up, grad_down = (expert_gradient(j) for j in range(3))
    small = [small_gradients(*grads["small"], w_rows) for grads in layer_grads]

    def at_home(first, last):
        received = exchange(jnp.where(home[0], last, first))
        return jnp.where(home[0], first, last).astype(F32) + received.astype(F32)

    small = at_home(*small)
    grad_query, grad_out = small[:, :columns], small[:, columns + 2 * kcols :]
    if w_rows == 256:
        heads = lambda v: [v[:, :64], v[:, 128:192], v[:, 64:128], v[:, 192:]]
        grad_query = jnp.concatenate(heads(grad_query), axis=1)
        grad_out = jnp.concatenate(
            [grad_out[:64], grad_out[128:192], grad_out[64:128], grad_out[192:]], axis=0
        )
    tally = jnp.concatenate(
        [g[name] for g in layer_grads for name in ("gain_first", "gain_second")]
        + [jnp.broadcast_to(loss, (128,))]
    )
    tally = total_everywhere(after(tally, returned[0]))
    loss = tally[4 * width]
    gains = tally[: 4 * width].reshape(2, 2, width)
    gains = jnp.where(home[0], gains[0], gains[1])
    gains = lax.dynamic_slice_in_dim(gains, col * shard, shard, 1)

    def both_micros(first, last):
        received = exchange(jnp.where(home[0], last, first))
        pair = jnp.where(home[0], jnp.stack([first, received]), jnp.stack([received, last]))
        return to_columns(pair, prompt)

    outputs = both_micros(mid, final.astype(BF16))
    input_grads = both_micros(after(dx, returned[1]), dmid)
    return (
        outputs[None, :, None],
        loss,
        input_grads[None, :, None],
        grad_query[None],
        small[None, :, columns : columns + kcols],
        small[None, :, columns + kcols : columns + 2 * kcols],
        grad_out[None],
        grad_gate[None],
        grad_up[None],
        grad_down[None],
        gains[:1],
        gains[1:],
    )


def solution(mesh):
    in_specs = (
        P(None, "row", None, "col"),
        P(None, "row", None, "col"),
        P("section", "row", "col"),
        P("section", "row", "col"),
        P("section", "row", "col"),
        P("section", "col", "row"),
        P("section", "col", "row", None),
        P("section", "col", "row", None),
        P("section", "col", None, "row"),
        P("section", None),
        P("section", None),
        P("section", None, "row", None, None),
        P("section", None, "row", None, None),
        P(),
    )
    out_specs = (
        P("section", None, "row", None, "col"),
        P(),
        P("section", None, "row", None, "col"),
        P("section", "row", "col"),
        P("section", "row", "col"),
        P("section", "row", "col"),
        P("section", "col", "row"),
        P("section", "col", "row", None),
        P("section", "col", "row", None),
        P("section", "col", None, "row"),
        P("section", "col"),
        P("section", "col"),
    )
    return jax.shard_map(
        on_device, mesh=mesh, in_specs=in_specs, out_specs=out_specs, check_vma=False
    )
```

```python
import functools

import jax
import jax.numpy as jnp
from jax import lax
from jax.experimental import pallas as pl
from jax.experimental.pallas import tpu as pltpu
from jax.sharding import PartitionSpec as P

HEAD = 64
HIDDEN_SIZE = 512
CONT_LEN = 512
CAP = 384
GROUP = 4

EPS = 1e-06
THETA = 10000.0
NEG = -1e30
BF16 = jnp.bfloat16
F32 = jnp.float32
VMEM_LIMIT = 60 * 1024 * 1024


def shift(value, axis, pairs):
    return lax.ppermute(value, axis, pairs)


def flip(value, bit):
    count = lax.axis_size("col")
    return shift(value, "col", [(i, i ^ bit) for i in range(count)])


def col_bits():
    count = lax.axis_size("col")
    bits = [1]
    while bits[-1] * 2 < count:
        bits.append(bits[-1] * 2)
    return bits


def gather_col(value):
    blocks = {0: value}
    for bit in reversed(col_bits()):
        for k in list(blocks):
            blocks[k ^ bit] = flip(blocks[k], bit)
    return [blocks[k] for k in range(lax.axis_size("col"))]


def scatter_col(blocks, begun=None):
    blocks = dict(enumerate(blocks))
    total = None
    for bit in col_bits():
        keep = [k for k in blocks if not k & bit]
        total = {k: blocks[k].astype(F32) + flip(blocks[k ^ bit], bit).astype(F32) for k in keep}
        blocks = {k: total[k].astype(BF16) for k in keep}
        if begun is not None and bit == 1:
            begun.append(blocks[0])
    return total[0]


def exchange(value):
    return shift(value, "section", [(0, 1), (1, 0)])


def ring(value):
    count = lax.axis_size("row")
    return shift(value, "row", [(i, (i + 1) % count) for i in range(count)])


def gather_row(value):
    count = lax.axis_size("row")
    pieces = [value]
    for k in range(1, count):
        pieces.append(shift(value, "row", [(i, (i + k) % count) for i in range(count)]))
    return pieces


def scatter_row(parts):
    count = len(parts)
    total = parts[0].astype(F32)
    for k in range(1, count):
        pairs = [(i, (i - k) % count) for i in range(count)]
        total = total + shift(parts[k], "row", pairs).astype(F32)
    return total


def total_everywhere(value):
    for bit in col_bits():
        value = value + flip(value, bit)
    count, bit = lax.axis_size("row"), 1
    while bit < count:
        value = value + shift(value, "row", [(i, i ^ bit) for i in range(count)])
        bit *= 2
    return value + exchange(value)


def after(value, *others):
    return lax.optimization_barrier((value, *others))[0]


def needing(value, other):
    return value + (other.reshape(-1)[0] * 0.0).astype(value.dtype)


def behind(kernel, count):
    return lambda *refs: kernel(*refs[count:])


def dot_nn(left, right):
    return lax.dot_general(left, right, (((1,), (0,)), ((), ())), preferred_element_type=F32)


def dot_nt(left, right):
    return lax.dot_general(left, right, (((1,), (1,)), ((), ())), preferred_element_type=F32)


def dot_tn(left, right):
    return lax.dot_general(left, right, (((0,), (0,)), ((), ())), preferred_element_type=F32)


def swap_halves(value):
    lanes = value.shape[1]
    lane = lax.broadcasted_iota(jnp.int32, value.shape, 1)
    half = HEAD // 2
    ahead = pltpu.roll(value, lanes - half, 1)
    behind = pltpu.roll(value, half, 1)
    return jnp.where(lane % HEAD < half, ahead, behind)


def ordered(value, starts_ref, first, count, cut):
    picks = []
    for k in range(count):
        start = pl.multiple_of(starts_ref[first + k], cut)
        picks.append(value[:, pl.ds(start, cut)])
    return jnp.concatenate(picks, axis=1)


def flat(ref):
    return ref[...].reshape(ref.shape[0] * ref.shape[1], ref.shape[2])


def normalised(value):
    return lax.rsqrt(jnp.mean(value * value, axis=1, keepdims=True) + EPS)


def project_kernel(nblocks, starts_ref, x_ref, gain_ref, cos_ref, sin_ref, *refs):
    blocks, (n_ref, out_ref) = refs[:nblocks], refs[nblocks:]
    nrow, cut = blocks[0].shape[0], blocks[0].shape[1]
    width = x_ref.shape[1]
    x = x_ref[...].astype(F32)
    n_ref[...] = (x * normalised(x) * gain_ref[...]).astype(BF16)
    normed = ordered(n_ref, starts_ref, 0, nrow, cut)
    cos, sin = cos_ref[...], sin_ref[...]
    turn = lambda v: (v * cos + swap_halves(v) * sin).astype(BF16)
    for k, block in enumerate(blocks):
        raw = dot_nn(normed, flat(block))
        start = pl.multiple_of(starts_ref[nrow + k], 256)
        out_ref[:, pl.ds(start, 256)] = jnp.concatenate(
            [turn(raw[:, :128]), turn(raw[:, 128:256])], axis=1
        )
        start = pl.multiple_of(starts_ref[nrow + k] + width, 256)
        out_ref[:, pl.ds(start, 256)] = jnp.concatenate(
            [turn(raw[:, 256:384]), raw[:, 384:].astype(BF16)], axis=1
        )


def close_kernel(nblocks, starts_ref, x_ref, mixed_ref, gain_ref, *refs):
    blocks, (second_ref, n_ref, wide_ref) = refs[:nblocks], refs[nblocks:]
    nrow, cut = blocks[0].shape[0], blocks[0].shape[2]
    wide_ref[...] = mixed_ref[...].astype(BF16)
    mixed = ordered(wide_ref, starts_ref, nrow, nblocks, 256)
    for j in range(nrow):
        weight = jnp.concatenate([block[j] for block in blocks], axis=0)
        lanes = pl.ds(pl.multiple_of(starts_ref[j], cut), cut)
        second_ref[:, lanes] = x_ref[:, lanes].astype(F32) + dot_nn(mixed, weight)
    second = second_ref[...].astype(BF16).astype(F32)
    n_ref[...] = (second * normalised(second) * gain_ref[...]).astype(BF16)


def norm_back(grad, value, gain):
    rho = normalised(value)
    scaled = grad * gain
    inner = jnp.sum(scaled * value, axis=1, keepdims=True)
    out = rho * scaled - value * (rho * rho * rho) * (inner / value.shape[1])
    return out, jnp.sum(grad * value * rho, axis=0, keepdims=True)


def open_back_kernel(nblocks, starts_ref, grad_ref, dn_ref, second_ref, gain_ref, *refs):
    blocks, (dsecond_ref, dbranch_ref, dmixed_ref, dgain_ref) = refs[:nblocks], refs[nblocks:]
    nrow, cut = blocks[0].shape[0], blocks[0].shape[2]
    second = second_ref[...].astype(BF16).astype(F32)
    dnorm, dgain_ref[...] = norm_back(dn_ref[...], second, gain_ref[...])
    dsecond = grad_ref[...].astype(F32) + dnorm
    dsecond_ref[...] = dsecond
    dbranch_ref[...] = dsecond.astype(BF16)
    for k, block in enumerate(blocks):
        total = None
        for j in range(nrow):
            lanes = pl.ds(pl.multiple_of(starts_ref[j], cut), cut)
            term = dot_nt(dbranch_ref[:, lanes], block[j])
            total = term if total is None else total + term
        start = pl.multiple_of(starts_ref[nrow + k], 256)
        dmixed_ref[:, pl.ds(start, 256)] = total.astype(BF16)


def project_back_kernel(nblocks, starts_ref, dq_ref, dkv_ref, x_ref, gain_ref, dsecond_ref, *refs):
    blocks, (dx_ref, dgain_ref, wide_ref) = refs[:nblocks], refs[nblocks:]
    nrow, cut = blocks[0].shape[0], blocks[0].shape[1]
    total = None
    for k, block in enumerate(blocks):
        lanes = pl.ds(pl.multiple_of(starts_ref[nrow + k], 256), 256)
        grad = jnp.concatenate([dq_ref[:, lanes], dkv_ref[:, lanes]], axis=1)
        term = dot_nt(grad, flat(block))
        total = term if total is None else total + term
    for j in range(nrow):
        lanes = pl.ds(pl.multiple_of(starts_ref[j], cut), cut)
        wide_ref[:, lanes] = total[:, j * cut : (j + 1) * cut]
    dnorm, dgain_ref[...] = norm_back(wide_ref[...], x_ref[...].astype(F32), gain_ref[...])
    dx_ref[...] = (dsecond_ref[...] + dnorm).astype(BF16)


def weight_back_kernel(nblocks, starts_ref, n_ref, dq_ref, dkv_ref, mixed_ref, dbranch_ref, *refs):
    qkvs, outs = refs[:nblocks], refs[nblocks : 2 * nblocks]
    nrow, cut = qkvs[0].shape[0], qkvs[0].shape[1]
    normed = ordered(n_ref, starts_ref, 0, nrow, cut)
    for k in range(nblocks):
        lanes = pl.ds(pl.multiple_of(starts_ref[nrow + k], 256), 256)
        grad = jnp.concatenate([dq_ref[:, lanes], dkv_ref[:, lanes]], axis=1)
        qkvs[k][...] = dot_tn(normed, grad).astype(BF16).reshape(qkvs[k].shape)
        mixed = mixed_ref[:, lanes].astype(BF16)
        for j in range(nrow):
            there = pl.ds(pl.multiple_of(starts_ref[j], cut), cut)
            outs[k][j] = dot_tn(mixed, dbranch_ref[:, there]).astype(BF16)


def whole_call(kernel, out_shape, starts, operands, blocks, lanes, scratch=(), flops=0, ready=()):
    start, count = lanes
    specs = [pl.BlockSpec(memory_space=pltpu.SMEM)]
    specs += [pl.BlockSpec(memory_space=pltpu.VMEM) for _ in operands]
    specs += [
        pl.BlockSpec((*b.shape[:2], count), lambda i: (0, 0, start // count)) for b in blocks
    ]
    specs[1 : 1 + len(operands)] = [
        pl.BlockSpec(o.shape, lambda i, n=o.ndim: (0,) * n) for o in operands
    ]
    specs = [pl.BlockSpec(memory_space=pl.ANY) for _ in ready] + specs
    return pl.pallas_call(
        behind(functools.partial(kernel, len(blocks)), len(ready)),
        grid=(1,),
        in_specs=specs,
        out_specs=[pl.BlockSpec(o.shape, lambda i, n=len(o.shape): (0,) * n) for o in out_shape],
        out_shape=out_shape,
        scratch_shapes=scratch,
        compiler_params=pltpu.CompilerParams(vmem_limit_bytes=VMEM_LIMIT),
        cost_estimate=pl.CostEstimate(
            flops=flops,
            bytes_accessed=8 * 1024 * 1024,
            transcendentals=0,
        ),
    )(*ready, starts, *operands, *blocks)


def project(x, gain, cos, sin, part):
    rows, width = x.shape
    shapes = [
        jax.ShapeDtypeStruct((rows, width), BF16),
        jax.ShapeDtypeStruct((rows, 2 * width), BF16),
    ]
    return whole_call(
        project_kernel, shapes, part["starts"], (x, gain, cos, sin), part["qkv"], (0, 512),
        flops=4 * rows * width * width,
    )


def close_attention(x, mixed, gain, part):
    rows, width = x.shape
    shapes = [jax.ShapeDtypeStruct((rows, width), F32), jax.ShapeDtypeStruct((rows, width), BF16)]
    return whole_call(
        close_kernel, shapes, part["starts"], (x, mixed, gain), part["out"], part["out_lanes"],
        [pltpu.VMEM((rows, width), BF16)], 2 * rows * width * width,
    )


def open_back(grad, dn, second, gain, part):
    rows, width = grad.shape
    shapes = [
        jax.ShapeDtypeStruct((rows, width), F32),
        jax.ShapeDtypeStruct((rows, width), BF16),
        jax.ShapeDtypeStruct((rows, width), BF16),
        jax.ShapeDtypeStruct((1, width), F32),
    ]
    return whole_call(
        open_back_kernel, shapes, part["starts"], (grad, dn, second, gain), part["out"],
        part["out_lanes"], flops=2 * rows * width * width,
    )


def project_back(dq, dkv, x, gain, dsecond, part, ready):
    rows, width = x.shape
    shapes = [jax.ShapeDtypeStruct((rows, width), BF16), jax.ShapeDtypeStruct((1, width), F32)]
    return whole_call(
        project_back_kernel, shapes, part["starts"], (dq, dkv, x, gain, dsecond), part["qkv"],
        (0, 512), [pltpu.VMEM((rows, width), F32)], 4 * rows * width * width, ready,
    )


def weight_back(normed, dq, dkv, mixed, dbranch, part, ready=()):
    rows, width = normed.shape
    nblocks = len(part["qkv"])
    nrow, cut = part["qkv"][0].shape[:2]
    shapes = [jax.ShapeDtypeStruct((nrow, cut, 512), BF16)] * nblocks
    shapes += [jax.ShapeDtypeStruct((nrow, 256, width // nrow), BF16)] * nblocks
    operands = (normed, dq, dkv, mixed, dbranch)
    grads = pl.pallas_call(
        behind(functools.partial(weight_back_kernel, nblocks), len(ready)),
        in_specs=[pl.BlockSpec(memory_space=pl.ANY)] * len(ready)
        + [pl.BlockSpec(memory_space=pltpu.SMEM)]
        + [pl.BlockSpec(memory_space=pltpu.VMEM)] * len(operands),
        out_specs=[pl.BlockSpec(memory_space=pltpu.VMEM)] * len(shapes),
        out_shape=shapes,
        compiler_params=pltpu.CompilerParams(vmem_limit_bytes=VMEM_LIMIT),
        cost_estimate=pl.CostEstimate(
            flops=6 * rows * width * width, bytes_accessed=8 * 1024 * 1024, transcendentals=0
        ),
    )(*ready, part["starts_back"], *operands)
    return grads[:nblocks], grads[nblocks:]


def stack_heads(value):
    low = (lax.broadcasted_iota(jnp.int32, (value.shape[0], 128), 1) < HEAD).astype(F32)
    first, second = value[:, :128].astype(F32), value[:, 128:].astype(F32)
    return jnp.concatenate(
        [first * low, second * low, first * (1.0 - low), second * (1.0 - low)], axis=0
    )


def unstack_heads(value):
    rows = value.shape[0] // 4
    low = lax.broadcasted_iota(jnp.int32, (rows, 128), 1) < HEAD
    first = jnp.where(low, value[:rows], value[2 * rows : 3 * rows])
    second = jnp.where(low, value[rows : 2 * rows], value[3 * rows :])
    return first, second


def attend_kernel(q_ref, k_ref, v_ref, bias_ref, o_ref, lse_ref):
    stacked = (stack_heads(q_ref[0]) * HEAD**-0.5).astype(BF16)
    scores = dot_nt(k_ref[0], stacked) + bias_ref[...]
    top = jnp.max(scores, axis=0, keepdims=True)
    weights = jnp.exp(scores - top)
    total = jnp.sum(weights, axis=0, keepdims=True)
    mixed = dot_tn(v_ref[0], weights.astype(BF16)) / total
    first, second = unstack_heads(mixed.T)
    o_ref[0, :, :128] = first
    o_ref[0, :, 128:] = second
    lse_ref[0, 0] = top + jnp.log(total)


def attend(qkv, kv, bias):
    micro, rows, _ = qkv.shape
    keys, width = kv.shape[1], kv.shape[2]
    groups = width // 256
    return pl.pallas_call(
        attend_kernel,
        grid=(micro, groups),
        in_specs=[
            pl.BlockSpec((1, rows, 256), lambda m, g: (m, 0, g)),
            pl.BlockSpec((1, keys, 128), lambda m, g: (m, 0, 2 * g)),
            pl.BlockSpec((1, keys, 128), lambda m, g: (m, 0, 2 * g + 1)),
            pl.BlockSpec((keys, 4 * rows), lambda m, g: (0, 0)),
        ],
        out_specs=[
            pl.BlockSpec((1, rows, 256), lambda m, g: (m, 0, g)),
            pl.BlockSpec((1, 1, 1, 4 * rows), lambda m, g: (m, g, 0, 0)),
        ],
        out_shape=[
            jax.ShapeDtypeStruct((micro, rows, groups * 256), F32),
            jax.ShapeDtypeStruct((micro, groups, 1, 4 * rows), F32),
        ],
        compiler_params=pltpu.CompilerParams(vmem_limit_bytes=VMEM_LIMIT),
        cost_estimate=pl.CostEstimate(
            flops=micro * groups * 4 * rows * keys * 128 * 4,
            bytes_accessed=2 * micro * keys * width + 4 * keys * 4 * rows,
            transcendentals=micro * groups * 4 * rows * keys,
        ),
    )(qkv, kv, kv, bias)


def attend_back_kernel(
    q_ref, k_ref, v_ref, bias_ref, do_ref, o_ref, lse_ref, cos_ref, sin_ref, kcos_ref, ksin_ref,
    dq_ref, dkv_ref,
):
    scale = HEAD**-0.5
    queries = (stack_heads(q_ref[0]) * scale).astype(BF16)
    grads_wide = stack_heads(do_ref[0])
    product = grads_wide * stack_heads(o_ref[0])
    delta = jnp.sum(product.T, axis=0, keepdims=True)
    grads = grads_wide.astype(BF16)
    keys, values = k_ref[0], v_ref[0]
    probs = jnp.exp(dot_nt(keys, queries) + bias_ref[...] - lse_ref[0, 0])
    dvalues = dot_nn(probs.astype(BF16), grads)
    dscores = (probs * (dot_nt(values, grads) - delta)).astype(BF16)
    dkeys = dot_nn(dscores, queries)
    dqueries = dot_tn(keys, dscores) * scale
    first, second = unstack_heads(dqueries.T)
    cos, sin = cos_ref[...], sin_ref[...]
    dq_ref[0, :, :128] = (first * cos - swap_halves(first) * sin).astype(BF16)
    dq_ref[0, :, 128:] = (second * cos - swap_halves(second) * sin).astype(BF16)
    dkv_ref[0, :, :128] = (dkeys * kcos_ref[...] - swap_halves(dkeys) * ksin_ref[...]).astype(BF16)
    dkv_ref[0, :, 128:] = dvalues.astype(BF16)


def attend_back(qkv, kv, bias, grad, o, lse, cos, sin, kcos, ksin):
    micro, rows, _ = qkv.shape
    keys, width = kv.shape[1], kv.shape[2]
    groups = width // 256
    mine = pl.BlockSpec((1, rows, 256), lambda m, g: (m, 0, g))
    return pl.pallas_call(
        attend_back_kernel,
        grid=(micro, groups),
        in_specs=[
            mine,
            pl.BlockSpec((1, keys, 128), lambda m, g: (m, 0, 2 * g)),
            pl.BlockSpec((1, keys, 128), lambda m, g: (m, 0, 2 * g + 1)),
            pl.BlockSpec((keys, 4 * rows), lambda m, g: (0, 0)),
            mine,
            mine,
            pl.BlockSpec((1, 1, 1, 4 * rows), lambda m, g: (m, g, 0, 0)),
            pl.BlockSpec((rows, 128), lambda m, g: (0, 0)),
            pl.BlockSpec((rows, 128), lambda m, g: (0, 0)),
            pl.BlockSpec((keys, 128), lambda m, g: (0, 0)),
            pl.BlockSpec((keys, 128), lambda m, g: (0, 0)),
        ],
        out_specs=[mine, pl.BlockSpec((1, keys, 256), lambda m, g: (m, 0, g))],
        out_shape=[
            jax.ShapeDtypeStruct((micro, rows, groups * 256), BF16),
            jax.ShapeDtypeStruct((micro, keys, width), BF16),
        ],
        compiler_params=pltpu.CompilerParams(vmem_limit_bytes=VMEM_LIMIT),
        cost_estimate=pl.CostEstimate(
            flops=micro * groups * 4 * rows * keys * 128 * 10,
            bytes_accessed=4 * micro * keys * width + 4 * keys * 4 * rows,
            transcendentals=micro * groups * 4 * rows * keys,
        ),
    )(qkv, kv, kv, bias, grad, o, lse, cos, sin, kcos, ksin)


def chosen_rows(place_ref, m, cap, tokens):
    slots = lax.broadcasted_iota(jnp.int32, (cap, tokens), 0)
    return jnp.where(slots == place_ref[0, m : m + 1, :], 1.0, 0.0).astype(BF16)


def slot_weights(pick, weight_ref, m):
    return jnp.sum(pick.astype(F32) * weight_ref[0, m : m + 1, :], axis=1, keepdims=True)


def load_tokens(pieces, scratch):
    for at, piece in enumerate(pieces):
        rows = piece.shape[1]
        scratch[:, at * rows : (at + 1) * rows, :] = piece[...]


def store_tokens(out_ref, total):
    blocks, _, rows, _ = out_ref.shape
    for at in range(blocks):
        out_ref[at] = total[:, at * rows : (at + 1) * rows, :].astype(BF16)


def by_load(counts_ref, body, empty=None):
    e = pl.program_id(0)
    most = jnp.maximum(counts_ref[2 * e], counts_ref[2 * e + 1])
    below = 0
    for cap in (CAP // 3, 2 * CAP // 3, CAP):
        pl.when((most > below) & (most <= cap))(functools.partial(body, cap))
        below = cap
    if empty is not None:
        pl.when(most == 0)(empty)


def expert_call(kernel, local, operands, specs, outs, scratch, flops, moved, ready=()):
    def spec(shape, own):
        zeros = (0,) * (len(shape) - 1)
        if own:
            return pl.BlockSpec((1, *shape[1:]), lambda e: (e, *zeros))
        return pl.BlockSpec(shape, lambda e: (0, *zeros))

    return pl.pallas_call(
        behind(kernel, len(ready)),
        grid=(local,),
        in_specs=[pl.BlockSpec(memory_space=pl.ANY) for _ in ready]
        + [
            pl.BlockSpec(memory_space=pltpu.SMEM) if own is None else spec(o.shape, own)
            for o, own in zip(operands, specs)
        ],
        out_specs=[spec(shape, own) for shape, own in outs],
        out_shape=[jax.ShapeDtypeStruct(shape, BF16) for shape, _ in outs],
        scratch_shapes=scratch,
        compiler_params=pltpu.CompilerParams(vmem_limit_bytes=VMEM_LIMIT),
        cost_estimate=pl.CostEstimate(flops=flops, bytes_accessed=moved, transcendentals=0),
    )(*ready, *operands)


def expert_hidden_kernel(ncol, counts_ref, place_ref, *refs):
    pieces, refs = refs[:ncol], refs[ncol:]
    gate_ref, up_ref, chosen_ref, hidden_ref, active_ref, tokens_ref, rows_ref = refs
    micro, tokens, _ = tokens_ref.shape
    hidden = gate_ref.shape[2]

    @pl.when(pl.program_id(0) == 0)
    def _():
        load_tokens(pieces, tokens_ref)

    def body(cap):
        for m in range(micro):
            chosen = dot_nn(chosen_rows(place_ref, m, cap, tokens), tokens_ref[m]).astype(BF16)
            rows_ref[m * cap : (m + 1) * cap, :] = chosen
            chosen_ref[0, m, :cap, :] = chosen
        gate = dot_nn(rows_ref[: micro * cap, :], gate_ref[0])
        up = dot_nn(rows_ref[: micro * cap, :], up_ref[0])
        active = (gate * jax.nn.sigmoid(gate) * up).astype(BF16)
        for m in range(micro):
            slots = slice(m * cap, (m + 1) * cap)
            hidden_ref[0, m, :cap, :hidden] = gate[slots].astype(BF16)
            hidden_ref[0, m, :cap, hidden:] = up[slots].astype(BF16)
            active_ref[0, m, :cap, :] = active[slots]

    by_load(counts_ref, body)


def expert_out_kernel(counts_ref, place_ref, weight_ref, active_ref, down_ref, y_ref, total_ref):
    micro, tokens, _ = total_ref.shape

    @pl.when(pl.program_id(0) == 0)
    def _():
        total_ref[...] = jnp.zeros_like(total_ref)

    def body(cap):
        active = jnp.concatenate([active_ref[0, m, :cap, :] for m in range(micro)], axis=0)
        out = dot_nn(active, down_ref[0])
        for m in range(micro):
            pick = chosen_rows(place_ref, m, cap, tokens)
            scaled = (out[m * cap : (m + 1) * cap] * slot_weights(pick, weight_ref, m)).astype(BF16)
            total_ref[m] += dot_tn(pick, scaled)

    by_load(counts_ref, body)

    @pl.when(pl.program_id(0) == pl.num_programs(0) - 1)
    def _():
        store_tokens(y_ref, total_ref)


def experts(counts, place, weight, pieces, weights):
    micro, rows, width = pieces[0].shape
    gate, up, down = weights
    local, hidden = gate.shape[0], gate.shape[2]
    ncol = len(pieces)
    tokens = ncol * rows
    slots = local * micro * 256
    chosen, hid, active = expert_call(
        functools.partial(expert_hidden_kernel, ncol),
        local,
        (counts, place, *pieces, gate, up),
        (None, True, *[False] * ncol, True, True),
        [
            ((local, micro, CAP, width), True),
            ((local, micro, CAP, 2 * hidden), True),
            ((local, micro, CAP, hidden), True),
        ],
        [pltpu.VMEM((micro, tokens, width), BF16), pltpu.VMEM((micro * CAP, width), BF16)],
        slots * width * (4 * hidden + 2 * tokens),
        local * width * (4 * hidden + 4 * micro * CAP),
    )
    (y,) = expert_call(
        expert_out_kernel,
        local,
        (counts, place, weight, active, down),
        (None, True, True, True, True),
        [((ncol, micro, rows, width), False)],
        [pltpu.VMEM((micro, tokens, width), F32)],
        slots * width * (2 * hidden + 2 * tokens),
        local * width * 2 * hidden + 4 * micro * tokens * width,
    )
    return y, chosen, hid


def expert_back_kernel(ncol, counts_ref, place_ref, weight_ref, *refs):
    pieces, refs = refs[:ncol], refs[ncol:]
    gate_ref, up_ref, down_ref, hidden_ref, dx_ref, dhidden_ref, ddown_ref, *refs = refs
    tokens_ref, total_ref, rows_ref = refs
    micro, tokens, _ = tokens_ref.shape
    hidden = down_ref.shape[1]

    @pl.when(pl.program_id(0) == 0)
    def _():
        load_tokens(pieces, tokens_ref)
        total_ref[...] = jnp.zeros_like(total_ref)

    def body(cap):
        picks = [chosen_rows(place_ref, m, cap, tokens) for m in range(micro)]
        for m in range(micro):
            grads = dot_nn(picks[m], tokens_ref[m]) * slot_weights(picks[m], weight_ref, m)
            rows_ref[m * cap : (m + 1) * cap, :] = grads.astype(BF16)
        used = micro * cap
        dactive = dot_nt(rows_ref[:used, :], down_ref[0])
        both = jnp.concatenate([hidden_ref[0, m, :cap, :] for m in range(micro)], axis=0)
        gate, up = both[:, :hidden].astype(F32), both[:, hidden:].astype(F32)
        sigmoid = jax.nn.sigmoid(gate)
        silu = gate * sigmoid
        dgate = (dactive * up * sigmoid * (1.0 + gate * (1.0 - sigmoid))).astype(BF16)
        dup = (dactive * silu).astype(BF16)
        for m in range(micro):
            dhidden_ref[0, m, :cap, :hidden] = dgate[m * cap : (m + 1) * cap]
            dhidden_ref[0, m, :cap, hidden:] = dup[m * cap : (m + 1) * cap]
        ddown_ref[0] = dot_tn((silu * up).astype(BF16), rows_ref[:used, :]).astype(BF16)
        out = (dot_nt(dgate, gate_ref[0]) + dot_nt(dup, up_ref[0])).astype(BF16)
        for m in range(micro):
            total_ref[m] += dot_tn(picks[m], out[m * cap : (m + 1) * cap])

    def empty():
        ddown_ref[...] = jnp.zeros_like(ddown_ref)

    by_load(counts_ref, body, empty)

    @pl.when(pl.program_id(0) == pl.num_programs(0) - 1)
    def _():
        store_tokens(dx_ref, total_ref)


def expert_weight_back_kernel(counts_ref, chosen_ref, dhidden_ref, dgate_ref, dup_ref):
    micro = chosen_ref.shape[1]
    hidden = dgate_ref.shape[2]

    def body(cap):
        rows = jnp.concatenate([chosen_ref[0, m, :cap, :] for m in range(micro)], axis=0)
        both = jnp.concatenate([dhidden_ref[0, m, :cap, :] for m in range(micro)], axis=0)
        grads = dot_tn(rows, both).astype(BF16)
        dgate_ref[0] = grads[:, :hidden]
        dup_ref[0] = grads[:, hidden:]

    def empty():
        dgate_ref[...] = jnp.zeros_like(dgate_ref)
        dup_ref[...] = jnp.zeros_like(dup_ref)

    by_load(counts_ref, body, empty)


def experts_back(counts, place, weight, pieces, weights, hid):
    micro, rows, width = pieces[0].shape
    gate, up, down = weights
    local, hidden = gate.shape[0], gate.shape[2]
    ncol = len(pieces)
    tokens = ncol * rows
    slots = local * micro * 256
    dx, dhid, ddown = expert_call(
        functools.partial(expert_back_kernel, ncol),
        local,
        (counts, place, weight, *pieces, gate, up, down, hid),
        (None, True, True, *[False] * ncol, True, True, True, True),
        [
            ((ncol, micro, rows, width), False),
            ((local, micro, CAP, 2 * hidden), True),
            (down.shape, True),
        ],
        [
            pltpu.VMEM((micro, tokens, width), BF16),
            pltpu.VMEM((micro, tokens, width), F32),
            pltpu.VMEM((micro * CAP, width), BF16),
        ],
        slots * width * (8 * hidden + 4 * tokens),
        local * width * (8 * hidden + 2 * micro * CAP),
    )
    return dx, dhid, ddown


def expert_weights_back(counts, chosen, dhid, weights, ready):
    gate, up, _ = weights
    local, width, hidden = gate.shape
    micro = chosen.shape[1]
    return expert_call(
        expert_weight_back_kernel,
        local,
        (counts, chosen, dhid),
        (None, True, True),
        [(gate.shape, True), (up.shape, True)],
        [],
        local * micro * 256 * width * 4 * hidden,
        local * width * (4 * hidden + 4 * micro * CAP),
        ready,
    )


def spread_rows(value):
    both = jnp.stack([value, exchange(value)])
    return gather_col(both)


def collect_rows(partial, begun=None):
    blocks = [partial[k] for k in range(partial.shape[0])]
    theirs = exchange(scatter_col([b[1] for b in blocks], begun).astype(BF16))
    return scatter_col([b[0] for b in blocks]) + theirs.astype(F32)


def forward_layer(layer_in, env, part):
    rows, width = layer_in.shape
    prompt = env["prompt"]
    normed, qkv = project(layer_in, part["gain_first"], env["cos"], env["sin"], part)
    own = qkv[:, width:]
    near = gather_col(own)
    far = gather_col(jnp.concatenate(gather_row(own[:prompt])[1:], axis=0))
    kv = jnp.concatenate([b for pair in zip(near, far) for b in pair], axis=0)
    mixed, lse = attend(qkv[None], kv[None], env["bias"])
    second, normed_second = close_attention(layer_in, mixed[0], part["gain_second"], part)
    pieces = spread_rows(normed_second)
    partial, chosen, hid = experts(*part["slots"], pieces, part["experts"])
    result = second + collect_rows(partial)
    keep = {
        "layer_in": layer_in,
        "normed": normed,
        "qkv": qkv,
        "kv": kv,
        "mixed": mixed,
        "lse": lse,
        "second": second,
        "chosen": chosen,
        "hid": hid,
    }
    return result, keep


def backward_layer(grad_result, pieces, keep, env, part, before_projections=()):
    rows, _ = grad_result.shape
    prompt = env["prompt"]
    ncol, nrow = lax.axis_size("col"), lax.axis_size("row")
    partial, dhid, ddown = experts_back(*part["slots"], pieces, part["experts"], keep["hid"])
    begun = []
    dn2 = collect_rows(partial, begun)
    dgate, dup = expert_weights_back(part["slots"][0], keep["chosen"], dhid, part["experts"], begun)
    dsecond, dbranch, dmixed, gain_second = open_back(
        grad_result, dn2, keep["second"], part["gain_second"], part
    )
    dq, dkv = attend_back(
        keep["qkv"][None], keep["kv"][None], env["bias"], dmixed[None], keep["mixed"],
        keep["lse"], env["cos"], env["sin"], env["kcos"], env["ksin"],
    )
    span = dkv.shape[1] // ncol
    own = scatter_col([dkv[0, k * span : (k + 1) * span] for k in range(ncol)])
    parts = [own[:prompt]]
    for j in range(1, nrow):
        at = rows + (j - 1) * prompt
        parts.append(own[at : at + prompt].astype(BF16))
    own = jnp.concatenate([scatter_row(parts), own[prompt:rows]], axis=0).astype(BF16)
    grad_in, gain_first = project_back(
        dq[0], own, keep["layer_in"], part["gain_first"], dsecond, part, before_projections
    )
    return grad_in, {
        "small": (keep["normed"], dq[0], own, keep["mixed"][0], dbranch, part),
        "experts": (dgate, dup, ddown),
        "gain_first": gain_first[0],
        "gain_second": gain_second[0],
    }


def own_rows(value, prompt_rows):
    micro, _, shard = value.shape
    ncol = lax.axis_size("col")
    return jnp.concatenate(
        [
            value[:, :prompt_rows].reshape(micro, ncol, -1, shard),
            value[:, prompt_rows:].reshape(micro, ncol, -1, shard),
        ],
        axis=2,
    )


def to_rows(value, prompt_rows):
    split = own_rows(value, prompt_rows)
    return lax.all_to_all(split, "col", 1, 3, tiled=True)[:, 0]


def to_columns(value, prompt):
    micro, _, width = value.shape
    ncol, col = lax.axis_size("col"), lax.axis_index("col")
    shard = width // ncol
    blocks = []
    for k in range(ncol):
        block = lax.dynamic_slice_in_dim(value, (col ^ k) * shard, shard, 2)
        blocks.append(flip(block, k) if k else block)
    blocks = jnp.stack(blocks)
    blocks = [lax.dynamic_index_in_dim(blocks, col ^ c, 0, False) for c in range(ncol)]
    parts = [b[:, :prompt] for b in blocks] + [b[:, prompt:] for b in blocks]
    return jnp.concatenate(parts, axis=1)


def turn_tables(positions):
    half = HEAD // 2
    freqs = THETA ** (-(jnp.arange(half).astype(F32) * 2.0) / HEAD)
    angles = positions.astype(F32)[:, None] * freqs[None, :]
    cos, sin = jnp.cos(angles), jnp.sin(angles)
    return (
        jnp.concatenate([cos, cos, cos, cos], axis=1),
        jnp.concatenate([-sin, sin, -sin, sin], axis=1),
    )


def small_weights(rows, w_rows):
    nrow, cut = rows.shape[:2]
    ncol, row, col = lax.axis_size("col"), lax.axis_index("row"), lax.axis_index("col")
    index = jnp.arange(nrow, dtype=jnp.int32)
    blocks = gather_col(rows)

    def result(qkv, out, lanes, order):
        return {
            "starts": jnp.concatenate([index * cut, order]),
            "starts_back": jnp.concatenate([((row - index) % nrow) * cut, order]),
            "qkv": qkv,
            "out": out,
            "out_lanes": lanes,
        }

    if w_rows == 256:
        order = (col ^ jnp.arange(ncol, dtype=jnp.int32)) * 256
        return result(blocks, blocks, (512, 256), order)
    blocks = jnp.stack(blocks)
    whole = [lax.dynamic_index_in_dim(blocks, col ^ c, 0, False) for c in range(ncol)]
    qkv, out = [], []
    for a, b in zip(whole[::2], whole[1::2]):
        heads = [a[..., :64], b[..., :64], a[..., 64:128], b[..., 64:128]]
        others = [a[..., 128:192], b[..., 128:192], a[..., 192:256], b[..., 192:256]]
        qkv.append(jnp.concatenate(heads + others, axis=2))
        a, b = a[..., 256:], b[..., 256:]
        out.append(jnp.concatenate([a[:, :64], b[:, :64], a[:, 64:], b[:, 64:]], axis=1))
    return result(qkv, out, (0, cut), jnp.arange(len(qkv), dtype=jnp.int32) * 256)


def pack_weights(w_query, w_key, w_value, w_out):
    if w_out.shape[0] == 256:
        heads = lambda v: [v[..., :64], v[..., 128:192], v[..., 64:128], v[..., 192:]]
        rows = [w_out[:64], w_out[128:192], w_out[64:128], w_out[192:]]
        w_out = jnp.concatenate(rows, axis=0)
        w_query = jnp.concatenate(heads(w_query), axis=1)
    return jnp.concatenate([w_query, w_key, w_value, w_out], axis=1)


def col_gradients(qkv, out, w_rows, begun=None):
    ncol, col = lax.axis_size("col"), lax.axis_index("col")
    if w_rows == 256:
        blocks = [jnp.concatenate([a, b], axis=2) for a, b in zip(qkv, out)]
    else:
        whole = []
        for a, b in zip(qkv, out):
            for c in (0, 1):
                at = lambda i: a[..., 64 * i : 64 * i + 64]
                heads = [at(c), at(2 + c), at(4 + c), at(6 + c)]
                rows = jnp.concatenate(
                    [b[:, 64 * c : 64 * c + 64], b[:, 128 + 64 * c : 192 + 64 * c]], axis=1
                )
                whole.append(jnp.concatenate([*heads, rows], axis=2))
        whole = jnp.stack(whole)
        blocks = [lax.dynamic_index_in_dim(whole, col ^ k, 0, False) for k in range(ncol)]
    return scatter_col(blocks, begun).astype(BF16)


def routing(ids, scale, prompt_rows, first, local):
    ncol, col = lax.axis_size("col"), lax.axis_index("col")

    def mine(value):
        blocks = own_rows(value, prompt_rows)
        order = [lax.dynamic_index_in_dim(blocks, col ^ k, 1, False) for k in range(ncol)]
        return jnp.concatenate(order, axis=1).transpose(0, 2, 1)

    ids, scale = mine(ids), mine(scale)
    names = first + jnp.arange(local, dtype=jnp.int32)
    match = ids[None] == names[:, None, None, None]
    member = jnp.any(match, axis=2)
    weight = jnp.sum(jnp.where(match, scale[None], 0.0), axis=2)
    tokens = member.shape[2]
    order = jnp.arange(tokens, dtype=jnp.int32)
    earlier = (order[:, None] <= order[None, :]).astype(BF16)
    seen = dot_nn(member.astype(BF16).reshape(-1, tokens), earlier).astype(jnp.int32)
    seen = seen.reshape(member.shape)
    return seen[:, :, -1].reshape(-1), jnp.where(member, seen - 1, -1), weight


def on_device(
    x_in,
    targets,
    w_query,
    w_key,
    w_value,
    w_out,
    w_gate,
    w_up,
    w_down,
    gain_attn,
    gain_ffn,
    expert_ids,
    gates,
    lengths,
):
    section, row, col = (lax.axis_index(name) for name in ("section", "row", "col"))
    nrow, ncol = lax.axis_size("row"), lax.axis_size("col")
    micro, _, tokens, shard = x_in.shape
    width = shard * ncol
    prompt_rows = tokens - CONT_LEN
    prompt_len = prompt_rows * nrow
    prompt, cont = prompt_rows // ncol, CONT_LEN // ncol
    local = w_gate.shape[1]
    half = local // 2
    columns, kcols = w_query.shape[2], w_key.shape[2]
    home = [section == 0, section == 1]

    def by_layer(value):
        other = exchange(value)
        return [jnp.where(is_home, value, other) for is_home in home]

    w_rows = w_out.shape[1]
    packed = by_layer(pack_weights(w_query[0], w_key[0], w_value[0], w_out[0]))
    big = [w[0] for w in (w_gate, w_up, w_down)]
    over_row = lambda v: lax.all_gather(v, "row", axis=0)
    small_first = over_row(packed[0])
    crossed = [exchange(after(big[0][half:], packed[0]))]
    for w in big[1:]:
        crossed.append(exchange(after(w[half:], crossed[-1])))
    shards = [
        [jnp.where(is_home, w[:half], c) for w, c in zip(big, crossed)] for is_home in home
    ]
    ids_layer, gates_layer = by_layer(expert_ids[0, :, 0]), by_layer(gates[0, :, 0])
    gains = by_layer(jnp.concatenate([gain_attn, gain_ffn]).astype(F32))

    def whole(pieces):
        return [
            lax.all_gather(w, "row", axis=axis, tiled=True) for w, axis in zip(pieces, (1, 1, 2))
        ]

    def layer_part(layer, held):
        own_first = lambda v: jnp.where(home[0], v, v[::-1])
        first = col * local + jnp.where(home[layer], 0, half)
        ids, scale = own_first(ids_layer[layer]), own_first(gates_layer[layer])
        return {
            "experts": held,
            "gain_first": gains[layer][:1],
            "gain_second": gains[layer][1:],
            "slots": routing(ids, scale, prompt_rows, first, half),
        }

    shards[0] = [after(w, small_first) for w in shards[0]]
    parts = [layer_part(0, whole(shards[0]))]
    parts[0].update(small_weights(small_first, w_rows))
    held = parts[0]["experts"]
    small_later = over_row(after(packed[1], held[0]))
    parts.append(layer_part(1, whole(lax.optimization_barrier((shards[1], held[2]))[0])))
    parts[1].update(small_weights(small_later, w_rows))

    def prompt_positions(row_index, col_index):
        return row_index * prompt_rows + col_index * prompt + jnp.arange(prompt, dtype=jnp.int32)

    def cont_positions(col_index):
        return prompt_len + col_index * cont + jnp.arange(cont, dtype=jnp.int32)

    positions = jnp.concatenate([prompt_positions(row, col), cont_positions(col)])
    key_positions = []
    for k in range(ncol):
        key_positions += [prompt_positions(row, col ^ k), cont_positions(col ^ k)]
        key_positions += [prompt_positions((row - j) % nrow, col ^ k) for j in range(1, nrow)]
    key_positions = jnp.concatenate(key_positions)
    bias = jnp.where(key_positions[:, None] <= jnp.tile(positions, GROUP)[None, :], 0.0, NEG)
    cos, sin = turn_tables(positions)
    kcos, ksin = turn_tables(key_positions)
    env = {"prompt": prompt, "cos": cos, "sin": sin, "kcos": kcos, "ksin": ksin, "bias": bias}

    mine = lambda v: lax.dynamic_index_in_dim(v, section, 0, keepdims=True)
    first_in = to_rows(mine(x_in[:, 0]), prompt_rows)[0]
    goal = to_rows(mine(targets[:, 0]), prompt_rows)[0].astype(F32)

    result, keep_first = forward_layer(first_in, env, parts[0])
    mid = result.astype(BF16)
    final, keep_last = forward_layer(mid, env, parts[1])

    count = (micro * prompt_len + jnp.sum(lengths)).astype(F32)
    length = lengths[section, row]
    valid = (positions - prompt_len < length).astype(F32)[:, None]
    diff = (final - goal) * valid
    loss = jnp.sum(diff * diff) / count
    dfinal = (2.0 / count) * diff

    def both_micros(first, last):
        received = exchange(jnp.where(home[0], last, first))
        pair = jnp.where(home[0], jnp.stack([first, received]), jnp.stack([received, last]))
        return to_columns(pair, prompt)

    outputs = both_micros(mid, final.astype(BF16))
    dfinal_pieces = spread_rows(dfinal.astype(BF16))
    dmid, last_grads = backward_layer(dfinal, dfinal_pieces, keep_last, env, parts[1])
    dmid_pieces = spread_rows(dmid)
    small_last = col_gradients(*weight_back(*last_grads["small"], dmid_pieces[-1:]), w_rows)
    small_last = small_last, shift(small_last, "section", [(0, 1)])
    dx, first_grads = backward_layer(dmid, dmid_pieces, keep_first, env, parts[0], small_last)

    layer_grads = [first_grads, last_grads]

    def over_rows(j, layer, *earlier):
        grad = after(layer_grads[layer]["experts"][j], *earlier)
        return lax.psum_scatter(grad, "row", scatter_dimension=(1, 1, 2)[j], tiled=True)

    order = (2, 0, 1)
    sums_last = [over_rows(j, 1) for j in order]
    back_last = [shift(g, "section", [(0, 1)]) for g in sums_last]
    sums_first = [over_rows(j, 0, back) for j, back in zip(order, back_last)]
    back_first = [shift(g, "section", [(1, 0)]) for g in sums_first]

    def expert_gradient(j):
        at = order.index(j)
        own = jnp.where(home[0], sums_first[at], sums_last[at])
        other = jnp.where(home[0], back_first[at], back_last[at])
        return jnp.concatenate([own, other], axis=0).astype(F32)

    grad_gate, grad_up, grad_down = (expert_gradient(j) for j in range(3))
    small_first = col_gradients(*weight_back(*first_grads["small"], back_first[:1]), w_rows)
    small_first = small_first, shift(small_first, "section", [(1, 0)])
    small = [a.astype(F32) + b.astype(F32) for a, b in (small_first, small_last)]
    small = jnp.where(home[0], *small).astype(BF16)
    small = scatter_row([small[j] for j in range(nrow)])
    grad_query, grad_out = small[:, :columns], small[:, columns + 2 * kcols :]
    if w_rows == 256:
        heads = lambda v: [v[:, :64], v[:, 128:192], v[:, 64:128], v[:, 192:]]
        grad_query = jnp.concatenate(heads(grad_query), axis=1)
        grad_out = jnp.concatenate(
            [grad_out[:64], grad_out[128:192], grad_out[64:128], grad_out[192:]], axis=0
        )
    tally = jnp.concatenate(
        [g[name] for g in layer_grads for name in ("gain_first", "gain_second")]
        + [jnp.broadcast_to(loss, (128,))]
    )
    tally = total_everywhere(tally)
    loss = tally[4 * width]
    gains = tally[: 4 * width].reshape(2, 2, width)
    gains = jnp.where(home[0], gains[0], gains[1])
    gains = lax.dynamic_slice_in_dim(gains, col * shard, shard, 1)

    input_grads = both_micros(dx, dmid)
    return (
        outputs[None, :, None],
        loss,
        input_grads[None, :, None],
        grad_query[None],
        small[None, :, columns : columns + kcols],
        small[None, :, columns + kcols : columns + 2 * kcols],
        grad_out[None],
        grad_gate[None],
        grad_up[None],
        grad_down[None],
        gains[:1],
        gains[1:],
    )


def solution(mesh):
    in_specs = (
        P(None, "row", None, "col"),
        P(None, "row", None, "col"),
        P("section", "row", "col"),
        P("section", "row", "col"),
        P("section", "row", "col"),
        P("section", "col", "row"),
        P("section", "col", "row", None),
        P("section", "col", "row", None),
        P("section", "col", None, "row"),
        P("section", None),
        P("section", None),
        P("section", None, "row", None, None),
        P("section", None, "row", None, None),
        P(),
    )
    out_specs = (
        P("section", None, "row", None, "col"),
        P(),
        P("section", None, "row", None, "col"),
        P("section", "row", "col"),
        P("section", "row", "col"),
        P("section", "row", "col"),
        P("section", "col", "row"),
        P("section", "col", "row", None),
        P("section", "col", "row", None),
        P("section", "col", None, "row"),
        P("section", "col"),
        P("section", "col"),
    )
    return jax.shard_map(
        on_device, mesh=mesh, in_specs=in_specs, out_specs=out_specs, check_vma=False
    )
```

```python
import functools

import jax
import jax.numpy as jnp
from jax import lax
from jax.experimental import pallas as pl
from jax.experimental.pallas import tpu as pltpu
from jax.sharding import PartitionSpec as P

HEAD = 64
HIDDEN_SIZE = 512
CONT_LEN = 512
CAP = 384
GROUP = 4

EPS = 1e-06
THETA = 10000.0
NEG = -1e30
BF16 = jnp.bfloat16
F32 = jnp.float32
VMEM_LIMIT = 60 * 1024 * 1024


def shift(value, axis, pairs):
    return lax.ppermute(value, axis, pairs)


def flip(value, bit):
    count = lax.axis_size("col")
    return shift(value, "col", [(i, i ^ bit) for i in range(count)])


def col_bits():
    count = lax.axis_size("col")
    bits = [1]
    while bits[-1] * 2 < count:
        bits.append(bits[-1] * 2)
    return bits


def gather_col(value):
    blocks = {0: value}
    for bit in reversed(col_bits()):
        for k in list(blocks):
            blocks[k ^ bit] = flip(blocks[k], bit)
    return [blocks[k] for k in range(lax.axis_size("col"))]


def scatter_col(blocks, begun=None):
    blocks = dict(enumerate(blocks))
    total = None
    for bit in col_bits():
        keep = [k for k in blocks if not k & bit]
        total = {k: blocks[k].astype(F32) + flip(blocks[k ^ bit], bit).astype(F32) for k in keep}
        blocks = {k: total[k].astype(BF16) for k in keep}
        if begun is not None and bit == 1:
            begun.append(blocks[0])
    return total[0]


def exchange(value):
    return shift(value, "section", [(0, 1), (1, 0)])


def ring(value):
    count = lax.axis_size("row")
    return shift(value, "row", [(i, (i + 1) % count) for i in range(count)])


def gather_row(value):
    count = lax.axis_size("row")
    pieces = [value]
    for k in range(1, count):
        pieces.append(shift(value, "row", [(i, (i + k) % count) for i in range(count)]))
    return pieces


def scatter_row(parts):
    count = len(parts)
    total = parts[0].astype(F32)
    for k in range(1, count):
        pairs = [(i, (i - k) % count) for i in range(count)]
        total = total + shift(parts[k], "row", pairs).astype(F32)
    return total


def total_everywhere(value):
    for bit in col_bits():
        value = value + flip(value, bit)
    count, bit = lax.axis_size("row"), 1
    while bit < count:
        value = value + shift(value, "row", [(i, i ^ bit) for i in range(count)])
        bit *= 2
    return value + exchange(value)


def after(value, *others):
    return lax.optimization_barrier((value, *others))[0]


def needing(value, other):
    return value + (other.reshape(-1)[0] * 0.0).astype(value.dtype)


def behind(kernel, count):
    return lambda *refs: kernel(*refs[count:])


def dot_nn(left, right):
    return lax.dot_general(left, right, (((1,), (0,)), ((), ())), preferred_element_type=F32)


def dot_nt(left, right):
    return lax.dot_general(left, right, (((1,), (1,)), ((), ())), preferred_element_type=F32)


def dot_tn(left, right):
    return lax.dot_general(left, right, (((0,), (0,)), ((), ())), preferred_element_type=F32)


def swap_halves(value):
    lanes = value.shape[1]
    lane = lax.broadcasted_iota(jnp.int32, value.shape, 1)
    half = HEAD // 2
    ahead = pltpu.roll(value, lanes - half, 1)
    behind = pltpu.roll(value, half, 1)
    return jnp.where(lane % HEAD < half, ahead, behind)


def ordered(value, starts_ref, first, count, cut):
    picks = []
    for k in range(count):
        start = pl.multiple_of(starts_ref[first + k], cut)
        picks.append(value[:, pl.ds(start, cut)])
    return jnp.concatenate(picks, axis=1)


def flat(ref):
    return ref[...].reshape(ref.shape[0] * ref.shape[1], ref.shape[2])


def normalised(value):
    return lax.rsqrt(jnp.mean(value * value, axis=1, keepdims=True) + EPS)


def project_kernel(nblocks, starts_ref, x_ref, gain_ref, cos_ref, sin_ref, *refs):
    blocks, (n_ref, out_ref) = refs[:nblocks], refs[nblocks:]
    nrow, cut = blocks[0].shape[0], blocks[0].shape[1]
    width = x_ref.shape[1]
    x = x_ref[...].astype(F32)
    n_ref[...] = (x * normalised(x) * gain_ref[...]).astype(BF16)
    normed = ordered(n_ref, starts_ref, 0, nrow, cut)
    cos, sin = cos_ref[...], sin_ref[...]
    turn = lambda v: (v * cos + swap_halves(v) * sin).astype(BF16)
    for k, block in enumerate(blocks):
        raw = dot_nn(normed, flat(block))
        start = pl.multiple_of(starts_ref[nrow + k], 256)
        out_ref[:, pl.ds(start, 256)] = jnp.concatenate(
            [turn(raw[:, :128]), turn(raw[:, 128:256])], axis=1
        )
        start = pl.multiple_of(starts_ref[nrow + k] + width, 256)
        out_ref[:, pl.ds(start, 256)] = jnp.concatenate(
            [turn(raw[:, 256:384]), raw[:, 384:].astype(BF16)], axis=1
        )


def close_kernel(nblocks, starts_ref, x_ref, mixed_ref, gain_ref, *refs):
    blocks, (second_ref, n_ref, wide_ref) = refs[:nblocks], refs[nblocks:]
    nrow, cut = blocks[0].shape[0], blocks[0].shape[2]
    wide_ref[...] = mixed_ref[...].astype(BF16)
    mixed = ordered(wide_ref, starts_ref, nrow, nblocks, 256)
    for j in range(nrow):
        weight = jnp.concatenate([block[j] for block in blocks], axis=0)
        lanes = pl.ds(pl.multiple_of(starts_ref[j], cut), cut)
        second_ref[:, lanes] = x_ref[:, lanes].astype(F32) + dot_nn(mixed, weight)
    second = second_ref[...].astype(BF16).astype(F32)
    n_ref[...] = (second * normalised(second) * gain_ref[...]).astype(BF16)


def norm_back(grad, value, gain):
    rho = normalised(value)
    scaled = grad * gain
    inner = jnp.sum(scaled * value, axis=1, keepdims=True)
    out = rho * scaled - value * (rho * rho * rho) * (inner / value.shape[1])
    return out, jnp.sum(grad * value * rho, axis=0, keepdims=True)


def open_back_kernel(nblocks, starts_ref, grad_ref, dn_ref, second_ref, gain_ref, *refs):
    blocks, (dsecond_ref, dbranch_ref, dmixed_ref, dgain_ref) = refs[:nblocks], refs[nblocks:]
    nrow, cut = blocks[0].shape[0], blocks[0].shape[2]
    second = second_ref[...].astype(BF16).astype(F32)
    dnorm, dgain_ref[...] = norm_back(dn_ref[...], second, gain_ref[...])
    dsecond = grad_ref[...].astype(F32) + dnorm
    dsecond_ref[...] = dsecond
    dbranch_ref[...] = dsecond.astype(BF16)
    for k, block in enumerate(blocks):
        total = None
        for j in range(nrow):
            lanes = pl.ds(pl.multiple_of(starts_ref[j], cut), cut)
            term = dot_nt(dbranch_ref[:, lanes], block[j])
            total = term if total is None else total + term
        start = pl.multiple_of(starts_ref[nrow + k], 256)
        dmixed_ref[:, pl.ds(start, 256)] = total.astype(BF16)


def project_back_kernel(nblocks, starts_ref, dq_ref, dkv_ref, x_ref, gain_ref, dsecond_ref, *refs):
    blocks, (dx_ref, dgain_ref, wide_ref) = refs[:nblocks], refs[nblocks:]
    nrow, cut = blocks[0].shape[0], blocks[0].shape[1]
    total = None
    for k, block in enumerate(blocks):
        lanes = pl.ds(pl.multiple_of(starts_ref[nrow + k], 256), 256)
        grad = jnp.concatenate([dq_ref[:, lanes], dkv_ref[:, lanes]], axis=1)
        term = dot_nt(grad, flat(block))
        total = term if total is None else total + term
    for j in range(nrow):
        lanes = pl.ds(pl.multiple_of(starts_ref[j], cut), cut)
        wide_ref[:, lanes] = total[:, j * cut : (j + 1) * cut]
    dnorm, dgain_ref[...] = norm_back(wide_ref[...], x_ref[...].astype(F32), gain_ref[...])
    dx_ref[...] = (dsecond_ref[...] + dnorm).astype(BF16)


def weight_back_kernel(nblocks, starts_ref, n_ref, dq_ref, dkv_ref, mixed_ref, dbranch_ref, *refs):
    qkvs, outs = refs[:nblocks], refs[nblocks : 2 * nblocks]
    nrow, cut = qkvs[0].shape[0], qkvs[0].shape[1]
    normed = ordered(n_ref, starts_ref, 0, nrow, cut)
    for k in range(nblocks):
        lanes = pl.ds(pl.multiple_of(starts_ref[nrow + k], 256), 256)
        grad = jnp.concatenate([dq_ref[:, lanes], dkv_ref[:, lanes]], axis=1)
        qkvs[k][...] = dot_tn(normed, grad).astype(BF16).reshape(qkvs[k].shape)
        mixed = mixed_ref[:, lanes].astype(BF16)
        for j in range(nrow):
            there = pl.ds(pl.multiple_of(starts_ref[j], cut), cut)
            outs[k][j] = dot_tn(mixed, dbranch_ref[:, there]).astype(BF16)


def whole_call(kernel, out_shape, starts, operands, blocks, lanes, scratch=(), flops=0, ready=()):
    start, count = lanes
    specs = [pl.BlockSpec(memory_space=pltpu.SMEM)]
    specs += [pl.BlockSpec(memory_space=pltpu.VMEM) for _ in operands]
    specs += [
        pl.BlockSpec((*b.shape[:2], count), lambda i: (0, 0, start // count)) for b in blocks
    ]
    specs[1 : 1 + len(operands)] = [
        pl.BlockSpec(o.shape, lambda i, n=o.ndim: (0,) * n) for o in operands
    ]
    specs = [pl.BlockSpec(memory_space=pl.ANY) for _ in ready] + specs
    return pl.pallas_call(
        behind(functools.partial(kernel, len(blocks)), len(ready)),
        grid=(1,),
        in_specs=specs,
        out_specs=[pl.BlockSpec(o.shape, lambda i, n=len(o.shape): (0,) * n) for o in out_shape],
        out_shape=out_shape,
        scratch_shapes=scratch,
        compiler_params=pltpu.CompilerParams(vmem_limit_bytes=VMEM_LIMIT),
        cost_estimate=pl.CostEstimate(
            flops=flops,
            bytes_accessed=8 * 1024 * 1024,
            transcendentals=0,
        ),
    )(*ready, starts, *operands, *blocks)


def project(x, gain, cos, sin, part):
    rows, width = x.shape
    shapes = [
        jax.ShapeDtypeStruct((rows, width), BF16),
        jax.ShapeDtypeStruct((rows, 2 * width), BF16),
    ]
    return whole_call(
        project_kernel, shapes, part["starts"], (x, gain, cos, sin), part["qkv"], (0, 512),
        flops=4 * rows * width * width,
    )


def close_attention(x, mixed, gain, part):
    rows, width = x.shape
    shapes = [jax.ShapeDtypeStruct((rows, width), F32), jax.ShapeDtypeStruct((rows, width), BF16)]
    return whole_call(
        close_kernel, shapes, part["starts"], (x, mixed, gain), part["out"], part["out_lanes"],
        [pltpu.VMEM((rows, width), BF16)], 2 * rows * width * width,
    )


def open_back(grad, dn, second, gain, part):
    rows, width = grad.shape
    shapes = [
        jax.ShapeDtypeStruct((rows, width), F32),
        jax.ShapeDtypeStruct((rows, width), BF16),
        jax.ShapeDtypeStruct((rows, width), BF16),
        jax.ShapeDtypeStruct((1, width), F32),
    ]
    return whole_call(
        open_back_kernel, shapes, part["starts"], (grad, dn, second, gain), part["out"],
        part["out_lanes"], flops=2 * rows * width * width,
    )


def project_back(dq, dkv, x, gain, dsecond, part, ready):
    rows, width = x.shape
    shapes = [jax.ShapeDtypeStruct((rows, width), BF16), jax.ShapeDtypeStruct((1, width), F32)]
    return whole_call(
        project_back_kernel, shapes, part["starts"], (dq, dkv, x, gain, dsecond), part["qkv"],
        (0, 512), [pltpu.VMEM((rows, width), F32)], 4 * rows * width * width, ready,
    )


def weight_back(normed, dq, dkv, mixed, dbranch, part, ready=()):
    rows, width = normed.shape
    nblocks = len(part["qkv"])
    nrow, cut = part["qkv"][0].shape[:2]
    shapes = [jax.ShapeDtypeStruct((nrow, cut, 512), BF16)] * nblocks
    shapes += [jax.ShapeDtypeStruct((nrow, 256, width // nrow), BF16)] * nblocks
    operands = (normed, dq, dkv, mixed, dbranch)
    grads = pl.pallas_call(
        behind(functools.partial(weight_back_kernel, nblocks), len(ready)),
        in_specs=[pl.BlockSpec(memory_space=pl.ANY)] * len(ready)
        + [pl.BlockSpec(memory_space=pltpu.SMEM)]
        + [pl.BlockSpec(memory_space=pltpu.VMEM)] * len(operands),
        out_specs=[pl.BlockSpec(memory_space=pltpu.VMEM)] * len(shapes),
        out_shape=shapes,
        compiler_params=pltpu.CompilerParams(vmem_limit_bytes=VMEM_LIMIT),
        cost_estimate=pl.CostEstimate(
            flops=6 * rows * width * width, bytes_accessed=8 * 1024 * 1024, transcendentals=0
        ),
    )(*ready, part["starts_back"], *operands)
    return grads[:nblocks], grads[nblocks:]


def stack_heads(value):
    low = (lax.broadcasted_iota(jnp.int32, (value.shape[0], 128), 1) < HEAD).astype(F32)
    first, second = value[:, :128].astype(F32), value[:, 128:].astype(F32)
    return jnp.concatenate(
        [first * low, second * low, first * (1.0 - low), second * (1.0 - low)], axis=0
    )


def unstack_heads(value):
    rows = value.shape[0] // 4
    low = lax.broadcasted_iota(jnp.int32, (rows, 128), 1) < HEAD
    first = jnp.where(low, value[:rows], value[2 * rows : 3 * rows])
    second = jnp.where(low, value[rows : 2 * rows], value[3 * rows :])
    return first, second


def attend_kernel(q_ref, k_ref, v_ref, bias_ref, o_ref, lse_ref):
    stacked = (stack_heads(q_ref[0]) * HEAD**-0.5).astype(BF16)
    scores = dot_nt(k_ref[0], stacked) + bias_ref[...]
    top = jnp.max(scores, axis=0, keepdims=True)
    weights = jnp.exp(scores - top)
    total = jnp.sum(weights, axis=0, keepdims=True)
    mixed = dot_tn(v_ref[0], weights.astype(BF16)) / total
    first, second = unstack_heads(mixed.T)
    o_ref[0, :, :128] = first
    o_ref[0, :, 128:] = second
    lse_ref[0, 0] = top + jnp.log(total)


def attend(qkv, kv, bias):
    micro, rows, _ = qkv.shape
    keys, width = kv.shape[1], kv.shape[2]
    groups = width // 256
    return pl.pallas_call(
        attend_kernel,
        grid=(micro, groups),
        in_specs=[
            pl.BlockSpec((1, rows, 256), lambda m, g: (m, 0, g)),
            pl.BlockSpec((1, keys, 128), lambda m, g: (m, 0, 2 * g)),
            pl.BlockSpec((1, keys, 128), lambda m, g: (m, 0, 2 * g + 1)),
            pl.BlockSpec((keys, 4 * rows), lambda m, g: (0, 0)),
        ],
        out_specs=[
            pl.BlockSpec((1, rows, 256), lambda m, g: (m, 0, g)),
            pl.BlockSpec((1, 1, 1, 4 * rows), lambda m, g: (m, g, 0, 0)),
        ],
        out_shape=[
            jax.ShapeDtypeStruct((micro, rows, groups * 256), F32),
            jax.ShapeDtypeStruct((micro, groups, 1, 4 * rows), F32),
        ],
        compiler_params=pltpu.CompilerParams(vmem_limit_bytes=VMEM_LIMIT),
        cost_estimate=pl.CostEstimate(
            flops=micro * groups * 4 * rows * keys * 128 * 4,
            bytes_accessed=2 * micro * keys * width + 4 * keys * 4 * rows,
            transcendentals=micro * groups * 4 * rows * keys,
        ),
    )(qkv, kv, kv, bias)


def attend_back_kernel(
    q_ref, k_ref, v_ref, bias_ref, do_ref, o_ref, lse_ref, cos_ref, sin_ref, kcos_ref, ksin_ref,
    dq_ref, dkv_ref,
):
    scale = HEAD**-0.5
    queries = (stack_heads(q_ref[0]) * scale).astype(BF16)
    grads_wide = stack_heads(do_ref[0])
    product = grads_wide * stack_heads(o_ref[0])
    delta = jnp.sum(product.T, axis=0, keepdims=True)
    grads = grads_wide.astype(BF16)
    keys, values = k_ref[0], v_ref[0]
    probs = jnp.exp(dot_nt(keys, queries) + bias_ref[...] - lse_ref[0, 0])
    dvalues = dot_nn(probs.astype(BF16), grads)
    dscores = (probs * (dot_nt(values, grads) - delta)).astype(BF16)
    dkeys = dot_nn(dscores, queries)
    dqueries = dot_tn(keys, dscores) * scale
    first, second = unstack_heads(dqueries.T)
    cos, sin = cos_ref[...], sin_ref[...]
    dq_ref[0, :, :128] = (first * cos - swap_halves(first) * sin).astype(BF16)
    dq_ref[0, :, 128:] = (second * cos - swap_halves(second) * sin).astype(BF16)
    dkv_ref[0, :, :128] = (dkeys * kcos_ref[...] - swap_halves(dkeys) * ksin_ref[...]).astype(BF16)
    dkv_ref[0, :, 128:] = dvalues.astype(BF16)


def attend_back(qkv, kv, bias, grad, o, lse, cos, sin, kcos, ksin):
    micro, rows, _ = qkv.shape
    keys, width = kv.shape[1], kv.shape[2]
    groups = width // 256
    mine = pl.BlockSpec((1, rows, 256), lambda m, g: (m, 0, g))
    return pl.pallas_call(
        attend_back_kernel,
        grid=(micro, groups),
        in_specs=[
            mine,
            pl.BlockSpec((1, keys, 128), lambda m, g: (m, 0, 2 * g)),
            pl.BlockSpec((1, keys, 128), lambda m, g: (m, 0, 2 * g + 1)),
            pl.BlockSpec((keys, 4 * rows), lambda m, g: (0, 0)),
            mine,
            mine,
            pl.BlockSpec((1, 1, 1, 4 * rows), lambda m, g: (m, g, 0, 0)),
            pl.BlockSpec((rows, 128), lambda m, g: (0, 0)),
            pl.BlockSpec((rows, 128), lambda m, g: (0, 0)),
            pl.BlockSpec((keys, 128), lambda m, g: (0, 0)),
            pl.BlockSpec((keys, 128), lambda m, g: (0, 0)),
        ],
        out_specs=[mine, pl.BlockSpec((1, keys, 256), lambda m, g: (m, 0, g))],
        out_shape=[
            jax.ShapeDtypeStruct((micro, rows, groups * 256), BF16),
            jax.ShapeDtypeStruct((micro, keys, width), BF16),
        ],
        compiler_params=pltpu.CompilerParams(vmem_limit_bytes=VMEM_LIMIT),
        cost_estimate=pl.CostEstimate(
            flops=micro * groups * 4 * rows * keys * 128 * 10,
            bytes_accessed=4 * micro * keys * width + 4 * keys * 4 * rows,
            transcendentals=micro * groups * 4 * rows * keys,
        ),
    )(qkv, kv, kv, bias, grad, o, lse, cos, sin, kcos, ksin)


def chosen_rows(place_ref, m, cap, tokens):
    slots = lax.broadcasted_iota(jnp.int32, (cap, tokens), 0)
    return jnp.where(slots == place_ref[0, m : m + 1, :], 1.0, 0.0).astype(BF16)


def slot_weights(pick, weight_ref, m):
    return jnp.sum(pick.astype(F32) * weight_ref[0, m : m + 1, :], axis=1, keepdims=True)


def load_tokens(pieces, scratch):
    for at, piece in enumerate(pieces):
        rows = piece.shape[1]
        scratch[:, at * rows : (at + 1) * rows, :] = piece[...]


def store_tokens(out_ref, total):
    blocks, _, rows, _ = out_ref.shape
    for at in range(blocks):
        out_ref[at] = total[:, at * rows : (at + 1) * rows, :].astype(BF16)


def by_load(counts_ref, body, empty=None):
    e = pl.program_id(0)
    most = jnp.maximum(counts_ref[2 * e], counts_ref[2 * e + 1])
    below = 0
    for cap in (CAP // 3, 2 * CAP // 3, CAP):
        pl.when((most > below) & (most <= cap))(functools.partial(body, cap))
        below = cap
    if empty is not None:
        pl.when(most == 0)(empty)


def expert_call(kernel, local, operands, specs, outs, scratch, flops, moved, ready=()):
    def spec(shape, own):
        zeros = (0,) * (len(shape) - 1)
        if own is not False:
            return pl.BlockSpec((1, *shape[1:]), lambda e: (e + int(own) - 1, *zeros))
        return pl.BlockSpec(shape, lambda e: (0, *zeros))

    return pl.pallas_call(
        behind(kernel, len(ready)),
        grid=(local,),
        in_specs=[pl.BlockSpec(memory_space=pl.ANY) for _ in ready]
        + [
            pl.BlockSpec(memory_space=pltpu.SMEM) if own is None else spec(o.shape, own)
            for o, own in zip(operands, specs)
        ],
        out_specs=[spec(shape, own) for shape, own in outs],
        out_shape=[jax.ShapeDtypeStruct(shape, BF16) for shape, _ in outs],
        scratch_shapes=scratch,
        compiler_params=pltpu.CompilerParams(vmem_limit_bytes=VMEM_LIMIT),
        cost_estimate=pl.CostEstimate(flops=flops, bytes_accessed=moved, transcendentals=0),
    )(*ready, *operands)


def expert_hidden_kernel(ncol, counts_ref, place_ref, *refs):
    pieces, refs = refs[:ncol], refs[ncol:]
    gate_ref, up_ref, chosen_ref, hidden_ref, active_ref, tokens_ref, rows_ref = refs
    micro, tokens, _ = tokens_ref.shape
    hidden = gate_ref.shape[2]

    @pl.when(pl.program_id(0) == 0)
    def _():
        load_tokens(pieces, tokens_ref)

    def body(cap):
        for m in range(micro):
            chosen = dot_nn(chosen_rows(place_ref, m, cap, tokens), tokens_ref[m]).astype(BF16)
            rows_ref[m * cap : (m + 1) * cap, :] = chosen
            chosen_ref[0, m, :cap, :] = chosen
        gate = dot_nn(rows_ref[: micro * cap, :], gate_ref[0])
        up = dot_nn(rows_ref[: micro * cap, :], up_ref[0])
        active = (gate * jax.nn.sigmoid(gate) * up).astype(BF16)
        for m in range(micro):
            slots = slice(m * cap, (m + 1) * cap)
            hidden_ref[0, m, :cap, :hidden] = gate[slots].astype(BF16)
            hidden_ref[0, m, :cap, hidden:] = up[slots].astype(BF16)
            active_ref[0, m, :cap, :] = active[slots]

    by_load(counts_ref, body)


def expert_out_kernel(counts_ref, place_ref, weight_ref, active_ref, down_ref, y_ref, total_ref):
    micro, tokens, _ = total_ref.shape

    @pl.when(pl.program_id(0) == 0)
    def _():
        total_ref[...] = jnp.zeros_like(total_ref)

    def body(cap):
        active = jnp.concatenate([active_ref[0, m, :cap, :] for m in range(micro)], axis=0)
        out = dot_nn(active, down_ref[0])
        for m in range(micro):
            pick = chosen_rows(place_ref, m, cap, tokens)
            scaled = (out[m * cap : (m + 1) * cap] * slot_weights(pick, weight_ref, m)).astype(BF16)
            total_ref[m] += dot_tn(pick, scaled)

    by_load(counts_ref, body)

    @pl.when(pl.program_id(0) == pl.num_programs(0) - 1)
    def _():
        store_tokens(y_ref, total_ref)


def gate_and_up(weights, local):
    gate, up = weights[0], weights[-2]
    return gate, up, True, (local + 1 if len(weights) == 2 else True)


def experts(counts, place, weight, pieces, weights):
    micro, rows, width = pieces[0].shape
    local, hidden = place.shape[0], weights[0].shape[2]
    gate, up, at_gate, at_up = gate_and_up(weights, local)
    down = weights[-1]
    ncol = len(pieces)
    tokens = ncol * rows
    slots = local * micro * 256
    chosen, hid, active = expert_call(
        functools.partial(expert_hidden_kernel, ncol),
        local,
        (counts, place, *pieces, gate, up),
        (None, True, *[False] * ncol, at_gate, at_up),
        [
            ((local, micro, CAP, width), True),
            ((local, micro, CAP, 2 * hidden), True),
            ((local, micro, CAP, hidden), True),
        ],
        [pltpu.VMEM((micro, tokens, width), BF16), pltpu.VMEM((micro * CAP, width), BF16)],
        slots * width * (4 * hidden + 2 * tokens),
        local * width * (4 * hidden + 4 * micro * CAP),
    )
    (y,) = expert_call(
        expert_out_kernel,
        local,
        (counts, place, weight, active, down),
        (None, True, True, True, True),
        [((ncol, micro, rows, width), False)],
        [pltpu.VMEM((micro, tokens, width), F32)],
        slots * width * (2 * hidden + 2 * tokens),
        local * width * 2 * hidden + 4 * micro * tokens * width,
    )
    return y, chosen, hid


def expert_back_kernel(ncol, counts_ref, place_ref, weight_ref, *refs):
    pieces, refs = refs[:ncol], refs[ncol:]
    gate_ref, up_ref, down_ref, hidden_ref, dx_ref, dhidden_ref, ddown_ref, *refs = refs
    tokens_ref, total_ref, rows_ref = refs
    micro, tokens, _ = tokens_ref.shape
    hidden = down_ref.shape[1]

    @pl.when(pl.program_id(0) == 0)
    def _():
        load_tokens(pieces, tokens_ref)
        total_ref[...] = jnp.zeros_like(total_ref)

    def body(cap):
        picks = [chosen_rows(place_ref, m, cap, tokens) for m in range(micro)]
        for m in range(micro):
            grads = dot_nn(picks[m], tokens_ref[m]) * slot_weights(picks[m], weight_ref, m)
            rows_ref[m * cap : (m + 1) * cap, :] = grads.astype(BF16)
        used = micro * cap
        dactive = dot_nt(rows_ref[:used, :], down_ref[0])
        both = jnp.concatenate([hidden_ref[0, m, :cap, :] for m in range(micro)], axis=0)
        gate, up = both[:, :hidden].astype(F32), both[:, hidden:].astype(F32)
        sigmoid = jax.nn.sigmoid(gate)
        silu = gate * sigmoid
        dgate = (dactive * up * sigmoid * (1.0 + gate * (1.0 - sigmoid))).astype(BF16)
        dup = (dactive * silu).astype(BF16)
        for m in range(micro):
            dhidden_ref[0, m, :cap, :hidden] = dgate[m * cap : (m + 1) * cap]
            dhidden_ref[0, m, :cap, hidden:] = dup[m * cap : (m + 1) * cap]
        ddown_ref[0] = dot_tn((silu * up).astype(BF16), rows_ref[:used, :]).astype(BF16)
        out = (dot_nt(dgate, gate_ref[0]) + dot_nt(dup, up_ref[0])).astype(BF16)
        for m in range(micro):
            total_ref[m] += dot_tn(picks[m], out[m * cap : (m + 1) * cap])

    def empty():
        ddown_ref[...] = jnp.zeros_like(ddown_ref)

    by_load(counts_ref, body, empty)

    @pl.when(pl.program_id(0) == pl.num_programs(0) - 1)
    def _():
        store_tokens(dx_ref, total_ref)


def expert_weight_back_kernel(counts_ref, chosen_ref, dhidden_ref, dgate_ref, dup_ref):
    micro = chosen_ref.shape[1]
    hidden = dgate_ref.shape[2]
    outs = dgate_ref, dup_ref

    def body(cap):
        rows = jnp.concatenate([chosen_ref[0, m, :cap, :] for m in range(micro)], axis=0)
        both = jnp.concatenate([dhidden_ref[0, m, :cap, :] for m in range(micro)], axis=0)
        grads = dot_tn(rows, both).astype(BF16)
        dgate_ref[0] = grads[:, :hidden]
        dup_ref[0] = grads[:, hidden:]

    def empty():
        for out in outs:
            out[...] = jnp.zeros_like(out)

    by_load(counts_ref, body, empty)


def experts_back(counts, place, weight, pieces, weights, hid):
    micro, rows, width = pieces[0].shape
    local, hidden = place.shape[0], weights[0].shape[2]
    gate, up, at_gate, at_up = gate_and_up(weights, local)
    down = weights[-1]
    ncol = len(pieces)
    tokens = ncol * rows
    slots = local * micro * 256
    dx, dhid, ddown = expert_call(
        functools.partial(expert_back_kernel, ncol),
        local,
        (counts, place, weight, *pieces, gate, up, down, hid),
        (None, True, True, *[False] * ncol, at_gate, at_up, True, True),
        [
            ((ncol, micro, rows, width), False),
            ((local, micro, CAP, 2 * hidden), True),
            (down.shape, True),
        ],
        [
            pltpu.VMEM((micro, tokens, width), BF16),
            pltpu.VMEM((micro, tokens, width), F32),
            pltpu.VMEM((micro * CAP, width), BF16),
        ],
        slots * width * (8 * hidden + 4 * tokens),
        local * width * (8 * hidden + 2 * micro * CAP),
    )
    return dx, dhid, ddown


def expert_weights_back(counts, chosen, dhid, weights, ready):
    local, micro = chosen.shape[:2]
    width, hidden = weights[0].shape[1:]
    shapes = [(local, width, hidden)] * 2
    return expert_call(
        expert_weight_back_kernel,
        local,
        (counts, chosen, dhid),
        (None, True, True),
        [(shape, True) for shape in shapes],
        [],
        local * micro * 256 * width * 4 * hidden,
        local * width * (4 * hidden + 4 * micro * CAP),
        ready,
    )


def spread_rows(value):
    both = jnp.stack([value, exchange(value)])
    return gather_col(both)


def collect_rows(partial, begun=None):
    blocks = [partial[k] for k in range(partial.shape[0])]
    theirs = exchange(scatter_col([b[1] for b in blocks], begun).astype(BF16))
    return scatter_col([b[0] for b in blocks]) + theirs.astype(F32)


def forward_layer(layer_in, env, part):
    rows, width = layer_in.shape
    prompt = env["prompt"]
    normed, qkv = project(layer_in, part["gain_first"], env["cos"], env["sin"], part)
    own = qkv[:, width:]
    near = gather_col(own)
    far = gather_col(jnp.concatenate(gather_row(own[:prompt])[1:], axis=0))
    kv = jnp.concatenate([b for pair in zip(near, far) for b in pair], axis=0)
    mixed, lse = attend(qkv[None], kv[None], env["bias"])
    second, normed_second = close_attention(layer_in, mixed[0], part["gain_second"], part)
    pieces = spread_rows(normed_second)
    partial, chosen, hid = experts(*part["slots"], pieces, part["experts"])
    result = second + collect_rows(partial)
    keep = {
        "layer_in": layer_in,
        "normed": normed,
        "qkv": qkv,
        "kv": kv,
        "mixed": mixed,
        "lse": lse,
        "second": second,
        "chosen": chosen,
        "hid": hid,
    }
    return result, keep


def backward_layer(grad_result, pieces, keep, env, part, before_projections=None):
    rows, _ = grad_result.shape
    prompt = env["prompt"]
    ncol, nrow = lax.axis_size("col"), lax.axis_size("row")
    partial, dhid, ddown = experts_back(*part["slots"], pieces, part["experts"], keep["hid"])
    begun = []
    dn2 = collect_rows(partial, begun)
    dhidden = expert_weights_back(part["slots"][0], keep["chosen"], dhid, part["experts"], begun)
    dsecond, dbranch, dmixed, gain_second = open_back(
        grad_result, dn2, keep["second"], part["gain_second"], part
    )
    dq, dkv = attend_back(
        keep["qkv"][None], keep["kv"][None], env["bias"], dmixed[None], keep["mixed"],
        keep["lse"], env["cos"], env["sin"], env["kcos"], env["ksin"],
    )
    span = dkv.shape[1] // ncol
    own = scatter_col([dkv[0, k * span : (k + 1) * span] for k in range(ncol)])
    parts = [own[:prompt]]
    for j in range(1, nrow):
        at = rows + (j - 1) * prompt
        parts.append(own[at : at + prompt].astype(BF16))
    own = jnp.concatenate([scatter_row(parts), own[prompt:rows]], axis=0).astype(BF16)
    small = keep["normed"], dq[0], own, keep["mixed"][0], dbranch, part
    ready = ()
    if before_projections is not None:
        small = weight_back(*small)
        ready = (*before_projections, small[0][0])
    grad_in, gain_first = project_back(
        dq[0], own, keep["layer_in"], part["gain_first"], dsecond, part, ready
    )
    return grad_in, {
        "small": small,
        "experts": (*dhidden, ddown),
        "gain_first": gain_first[0],
        "gain_second": gain_second[0],
    }


def own_rows(value, prompt_rows):
    micro, _, shard = value.shape
    ncol = lax.axis_size("col")
    return jnp.concatenate(
        [
            value[:, :prompt_rows].reshape(micro, ncol, -1, shard),
            value[:, prompt_rows:].reshape(micro, ncol, -1, shard),
        ],
        axis=2,
    )


def to_rows(value, prompt_rows):
    split = own_rows(value, prompt_rows)
    return lax.all_to_all(split, "col", 1, 3, tiled=True)[:, 0]


def to_columns(value, prompt):
    micro, _, width = value.shape
    ncol, col = lax.axis_size("col"), lax.axis_index("col")
    shard = width // ncol
    blocks = []
    for k in range(ncol):
        block = lax.dynamic_slice_in_dim(value, (col ^ k) * shard, shard, 2)
        blocks.append(flip(block, k) if k else block)
    blocks = jnp.stack(blocks)
    blocks = [lax.dynamic_index_in_dim(blocks, col ^ c, 0, False) for c in range(ncol)]
    parts = [b[:, :prompt] for b in blocks] + [b[:, prompt:] for b in blocks]
    return jnp.concatenate(parts, axis=1)


def turn_tables(positions):
    half = HEAD // 2
    freqs = THETA ** (-(jnp.arange(half).astype(F32) * 2.0) / HEAD)
    angles = positions.astype(F32)[:, None] * freqs[None, :]
    cos, sin = jnp.cos(angles), jnp.sin(angles)
    return (
        jnp.concatenate([cos, cos, cos, cos], axis=1),
        jnp.concatenate([-sin, sin, -sin, sin], axis=1),
    )


def small_weights(rows, w_rows):
    nrow, cut = rows.shape[:2]
    ncol, row, col = lax.axis_size("col"), lax.axis_index("row"), lax.axis_index("col")
    index = jnp.arange(nrow, dtype=jnp.int32)
    blocks = gather_col(rows)

    def result(qkv, out, lanes, order):
        return {
            "starts": jnp.concatenate([index * cut, order]),
            "starts_back": jnp.concatenate([((row - index) % nrow) * cut, order]),
            "qkv": qkv,
            "out": out,
            "out_lanes": lanes,
        }

    if w_rows == 256:
        order = (col ^ jnp.arange(ncol, dtype=jnp.int32)) * 256
        return result(blocks, blocks, (512, 256), order)
    blocks = jnp.stack(blocks)
    whole = [lax.dynamic_index_in_dim(blocks, col ^ c, 0, False) for c in range(ncol)]
    qkv, out = [], []
    for a, b in zip(whole[::2], whole[1::2]):
        heads = [a[..., :64], b[..., :64], a[..., 64:128], b[..., 64:128]]
        others = [a[..., 128:192], b[..., 128:192], a[..., 192:256], b[..., 192:256]]
        qkv.append(jnp.concatenate(heads + others, axis=2))
        a, b = a[..., 256:], b[..., 256:]
        out.append(jnp.concatenate([a[:, :64], b[:, :64], a[:, 64:], b[:, 64:]], axis=1))
    return result(qkv, out, (0, cut), jnp.arange(len(qkv), dtype=jnp.int32) * 256)


def pack_weights(w_query, w_key, w_value, w_out):
    if w_out.shape[0] == 256:
        heads = lambda v: [v[..., :64], v[..., 128:192], v[..., 64:128], v[..., 192:]]
        rows = [w_out[:64], w_out[128:192], w_out[64:128], w_out[192:]]
        w_out = jnp.concatenate(rows, axis=0)
        w_query = jnp.concatenate(heads(w_query), axis=1)
    return jnp.concatenate([w_query, w_key, w_value, w_out], axis=1)


def col_gradients(qkv, out, w_rows, begun=None):
    ncol, col = lax.axis_size("col"), lax.axis_index("col")
    if w_rows == 256:
        blocks = [jnp.concatenate([a, b], axis=2) for a, b in zip(qkv, out)]
    else:
        whole = []
        for a, b in zip(qkv, out):
            for c in (0, 1):
                at = lambda i: a[..., 64 * i : 64 * i + 64]
                heads = [at(c), at(2 + c), at(4 + c), at(6 + c)]
                rows = jnp.concatenate(
                    [b[:, 64 * c : 64 * c + 64], b[:, 128 + 64 * c : 192 + 64 * c]], axis=1
                )
                whole.append(jnp.concatenate([*heads, rows], axis=2))
        whole = jnp.stack(whole)
        blocks = [lax.dynamic_index_in_dim(whole, col ^ k, 0, False) for k in range(ncol)]
    return scatter_col(blocks, begun).astype(BF16)


def routing(ids, scale, prompt_rows, first, local):
    ncol, col = lax.axis_size("col"), lax.axis_index("col")

    def mine(value):
        blocks = own_rows(value, prompt_rows)
        order = [lax.dynamic_index_in_dim(blocks, col ^ k, 1, False) for k in range(ncol)]
        return jnp.concatenate(order, axis=1).transpose(0, 2, 1)

    ids, scale = mine(ids), mine(scale)
    names = first + jnp.arange(local, dtype=jnp.int32)
    match = ids[None] == names[:, None, None, None]
    member = jnp.any(match, axis=2)
    weight = jnp.sum(jnp.where(match, scale[None], 0.0), axis=2)
    tokens = member.shape[2]
    order = jnp.arange(tokens, dtype=jnp.int32)
    earlier = (order[:, None] <= order[None, :]).astype(BF16)
    seen = dot_nn(member.astype(BF16).reshape(-1, tokens), earlier).astype(jnp.int32)
    seen = seen.reshape(member.shape)
    return seen[:, :, -1].reshape(-1), jnp.where(member, seen - 1, -1), weight


def on_device(
    x_in,
    targets,
    w_query,
    w_key,
    w_value,
    w_out,
    w_gate,
    w_up,
    w_down,
    gain_attn,
    gain_ffn,
    expert_ids,
    gates,
    lengths,
):
    section, row, col = (lax.axis_index(name) for name in ("section", "row", "col"))
    nrow, ncol = lax.axis_size("row"), lax.axis_size("col")
    micro, _, tokens, shard = x_in.shape
    width = shard * ncol
    prompt_rows = tokens - CONT_LEN
    prompt_len = prompt_rows * nrow
    prompt, cont = prompt_rows // ncol, CONT_LEN // ncol
    local = w_gate.shape[1]
    half = local // 2
    columns, kcols = w_query.shape[2], w_key.shape[2]
    home = [section == 0, section == 1]

    def by_layer(value):
        other = exchange(value)
        return [jnp.where(is_home, value, other) for is_home in home]

    w_rows = w_out.shape[1]
    packed = by_layer(pack_weights(w_query[0], w_key[0], w_value[0], w_out[0]))
    big = [w[0] for w in (w_gate, w_up, w_down)]
    over_row = lambda v: lax.all_gather(v, "row", axis=0)
    small_first = over_row(packed[0])
    crossed = [exchange(after(big[0][half:], packed[0]))]
    for w in big[1:]:
        crossed.append(exchange(after(w[half:], crossed[-1])))
    shards = [
        [jnp.where(is_home, w[:half], c) for w, c in zip(big, crossed)] for is_home in home
    ]
    gate, up, down = shards[1]
    shards[1] = [jnp.concatenate([gate, up], axis=0), down]
    ids_layer, gates_layer = by_layer(expert_ids[0, :, 0]), by_layer(gates[0, :, 0])
    gains = by_layer(jnp.concatenate([gain_attn, gain_ffn]).astype(F32))

    def whole(pieces):
        axes = (1,) * (len(pieces) - 1) + (2,)
        return [lax.all_gather(w, "row", axis=axis, tiled=True) for w, axis in zip(pieces, axes)]

    def layer_part(layer, held):
        own_first = lambda v: jnp.where(home[0], v, v[::-1])
        first = col * local + jnp.where(home[layer], 0, half)
        ids, scale = own_first(ids_layer[layer]), own_first(gates_layer[layer])
        return {
            "experts": held,
            "gain_first": gains[layer][:1],
            "gain_second": gains[layer][1:],
            "slots": routing(ids, scale, prompt_rows, first, half),
        }

    shards[0] = [after(w, small_first) for w in shards[0]]
    parts = [layer_part(0, whole(shards[0]))]
    parts[0].update(small_weights(small_first, w_rows))
    held = parts[0]["experts"]
    small_later = over_row(after(packed[1], held[0]))
    parts.append(layer_part(1, whole(lax.optimization_barrier((shards[1], held[2]))[0])))
    parts[1].update(small_weights(small_later, w_rows))

    def prompt_positions(row_index, col_index):
        return row_index * prompt_rows + col_index * prompt + jnp.arange(prompt, dtype=jnp.int32)

    def cont_positions(col_index):
        return prompt_len + col_index * cont + jnp.arange(cont, dtype=jnp.int32)

    positions = jnp.concatenate([prompt_positions(row, col), cont_positions(col)])
    key_positions = []
    for k in range(ncol):
        key_positions += [prompt_positions(row, col ^ k), cont_positions(col ^ k)]
        key_positions += [prompt_positions((row - j) % nrow, col ^ k) for j in range(1, nrow)]
    key_positions = jnp.concatenate(key_positions)
    bias = jnp.where(key_positions[:, None] <= jnp.tile(positions, GROUP)[None, :], 0.0, NEG)
    cos, sin = turn_tables(positions)
    kcos, ksin = turn_tables(key_positions)
    env = {"prompt": prompt, "cos": cos, "sin": sin, "kcos": kcos, "ksin": ksin, "bias": bias}

    mine = lambda v: lax.dynamic_index_in_dim(v, section, 0, keepdims=True)
    first_in = to_rows(mine(x_in[:, 0]), prompt_rows)[0]
    goal = to_rows(mine(targets[:, 0]), prompt_rows)[0].astype(F32)

    result, keep_first = forward_layer(first_in, env, parts[0])
    mid = result.astype(BF16)
    final, keep_last = forward_layer(mid, env, parts[1])

    count = (micro * prompt_len + jnp.sum(lengths)).astype(F32)
    length = lengths[section, row]
    valid = (positions - prompt_len < length).astype(F32)[:, None]
    diff = (final - goal) * valid
    loss = jnp.sum(diff * diff) / count
    dfinal = (2.0 / count) * diff

    def both_micros(first, last):
        received = exchange(jnp.where(home[0], last, first))
        pair = jnp.where(home[0], jnp.stack([first, received]), jnp.stack([received, last]))
        return to_columns(pair, prompt)

    outputs = both_micros(mid, final.astype(BF16))
    dfinal_pieces = spread_rows(dfinal.astype(BF16))
    dmid, last_grads = backward_layer(dfinal, dfinal_pieces, keep_last, env, parts[1])
    dmid_pieces = spread_rows(dmid)
    small_last = col_gradients(*weight_back(*last_grads["small"], dmid_pieces[-1:]), w_rows)
    small_last = small_last, shift(small_last, "section", [(0, 1)])
    dx, first_grads = backward_layer(dmid, dmid_pieces, keep_first, env, parts[0], small_last)

    layer_grads = [first_grads, last_grads]

    def over_rows(j, layer, *earlier):
        grad = after(layer_grads[layer]["experts"][j], *earlier)
        return lax.psum_scatter(grad, "row", scatter_dimension=(1, 1, 2)[j], tiled=True)

    order = (2, 0, 1)
    sums_last = [over_rows(j, 1) for j in order]
    back_last = [shift(g, "section", [(0, 1)]) for g in sums_last]
    sums_first = [over_rows(j, 0, back) for j, back in zip(order, back_last)]
    back_first = [shift(g, "section", [(1, 0)]) for g in sums_first[:2]]
    small_first = col_gradients(*first_grads["small"], w_rows)
    small = [None] * nrow
    for j in (*range(1, nrow), 0):
        pair = small_first[j], shift(small_first[j], "section", [(1, 0)])
        first, last = (a.astype(F32) + b.astype(F32) for a, b in (pair, (small_last[0][j], small_last[1][j])))
        small[j] = jnp.where(home[0], first, last).astype(BF16)
    small[0] = needing(small[0], back_first[0])
    small = scatter_row(small)
    back_first.append(shift(needing(sums_first[2], small), "section", [(1, 0)]))

    def expert_gradient(j):
        at = order.index(j)
        own = jnp.where(home[0], sums_first[at], sums_last[at])
        other = jnp.where(home[0], back_first[at], back_last[at])
        return jnp.concatenate([own, other], axis=0).astype(F32)

    grad_gate, grad_up, grad_down = (expert_gradient(j) for j in range(3))
    grad_query, grad_out = small[:, :columns], small[:, columns + 2 * kcols :]
    if w_rows == 256:
        heads = lambda v: [v[:, :64], v[:, 128:192], v[:, 64:128], v[:, 192:]]
        grad_query = jnp.concatenate(heads(grad_query), axis=1)
        grad_out = jnp.concatenate(
            [grad_out[:64], grad_out[128:192], grad_out[64:128], grad_out[192:]], axis=0
        )
    tally = jnp.concatenate(
        [g[name] for g in layer_grads for name in ("gain_first", "gain_second")]
        + [jnp.broadcast_to(loss, (128,))]
    )
    tally = total_everywhere(tally)
    loss = tally[4 * width]
    gains = tally[: 4 * width].reshape(2, 2, width)
    gains = jnp.where(home[0], gains[0], gains[1])
    gains = lax.dynamic_slice_in_dim(gains, col * shard, shard, 1)

    input_grads = both_micros(dx, dmid)
    return (
        outputs[None, :, None],
        loss,
        input_grads[None, :, None],
        grad_query[None],
        small[None, :, columns : columns + kcols],
        small[None, :, columns + kcols : columns + 2 * kcols],
        grad_out[None],
        grad_gate[None],
        grad_up[None],
        grad_down[None],
        gains[:1],
        gains[1:],
    )


def solution(mesh):
    in_specs = (
        P(None, "row", None, "col"),
        P(None, "row", None, "col"),
        P("section", "row", "col"),
        P("section", "row", "col"),
        P("section", "row", "col"),
        P("section", "col", "row"),
        P("section", "col", "row", None),
        P("section", "col", "row", None),
        P("section", "col", None, "row"),
        P("section", None),
        P("section", None),
        P("section", None, "row", None, None),
        P("section", None, "row", None, None),
        P(),
    )
    out_specs = (
        P("section", None, "row", None, "col"),
        P(),
        P("section", None, "row", None, "col"),
        P("section", "row", "col"),
        P("section", "row", "col"),
        P("section", "row", "col"),
        P("section", "col", "row"),
        P("section", "col", "row", None),
        P("section", "col", "row", None),
        P("section", "col", None, "row"),
        P("section", "col"),
        P("section", "col"),
    )
    return jax.shard_map(
        on_device, mesh=mesh, in_specs=in_specs, out_specs=out_specs, check_vma=False
    )
```

```python
import functools

import jax
import jax.numpy as jnp
from jax import lax
from jax.experimental import pallas as pl
from jax.experimental.pallas import tpu as pltpu
from jax.sharding import PartitionSpec as P

HEAD = 64
HIDDEN_SIZE = 512
CONT_LEN = 512
CAP = 384
GROUP = 4

EPS = 1e-06
THETA = 10000.0
NEG = -1e30
BF16 = jnp.bfloat16
F32 = jnp.float32
VMEM_LIMIT = 60 * 1024 * 1024


def shift(value, axis, pairs):
    return lax.ppermute(value, axis, pairs)


def flip(value, bit):
    count = lax.axis_size("col")
    return shift(value, "col", [(i, i ^ bit) for i in range(count)])


def col_bits():
    count = lax.axis_size("col")
    bits = [1]
    while bits[-1] * 2 < count:
        bits.append(bits[-1] * 2)
    return bits


def gather_col(value):
    blocks = {0: value}
    for bit in reversed(col_bits()):
        for k in list(blocks):
            blocks[k ^ bit] = flip(blocks[k], bit)
    return [blocks[k] for k in range(lax.axis_size("col"))]


def scatter_col(blocks, begun=None):
    blocks = dict(enumerate(blocks))
    total = None
    for bit in col_bits():
        keep = [k for k in blocks if not k & bit]
        total = {k: blocks[k].astype(F32) + flip(blocks[k ^ bit], bit).astype(F32) for k in keep}
        blocks = {k: total[k].astype(BF16) for k in keep}
        if begun is not None and bit == 1:
            begun.append(blocks[0])
    return total[0]


def exchange(value):
    return shift(value, "section", [(0, 1), (1, 0)])


def ring(value):
    count = lax.axis_size("row")
    return shift(value, "row", [(i, (i + 1) % count) for i in range(count)])


def gather_row(value):
    count = lax.axis_size("row")
    pieces = [value]
    for k in range(1, count):
        pieces.append(shift(value, "row", [(i, (i + k) % count) for i in range(count)]))
    return pieces


def scatter_row(parts):
    count = len(parts)
    total = parts[0].astype(F32)
    for k in range(1, count):
        pairs = [(i, (i - k) % count) for i in range(count)]
        total = total + shift(parts[k], "row", pairs).astype(F32)
    return total


def total_everywhere(value):
    for bit in col_bits():
        value = value + flip(value, bit)
    count, bit = lax.axis_size("row"), 1
    while bit < count:
        value = value + shift(value, "row", [(i, i ^ bit) for i in range(count)])
        bit *= 2
    return value + exchange(value)


def after(value, *others):
    return lax.optimization_barrier((value, *others))[0]


def needing(value, other):
    return value + (other.reshape(-1)[0] * 0.0).astype(value.dtype)


def behind(kernel, count):
    return lambda *refs: kernel(*refs[count:])


def dot_nn(left, right):
    return lax.dot_general(left, right, (((1,), (0,)), ((), ())), preferred_element_type=F32)


def dot_nt(left, right):
    return lax.dot_general(left, right, (((1,), (1,)), ((), ())), preferred_element_type=F32)


def dot_tn(left, right):
    return lax.dot_general(left, right, (((0,), (0,)), ((), ())), preferred_element_type=F32)


def swap_halves(value):
    lanes = value.shape[1]
    lane = lax.broadcasted_iota(jnp.int32, value.shape, 1)
    half = HEAD // 2
    ahead = pltpu.roll(value, lanes - half, 1)
    behind = pltpu.roll(value, half, 1)
    return jnp.where(lane % HEAD < half, ahead, behind)


def ordered(value, starts_ref, first, count, cut):
    picks = []
    for k in range(count):
        start = pl.multiple_of(starts_ref[first + k], cut)
        picks.append(value[:, pl.ds(start, cut)])
    return jnp.concatenate(picks, axis=1)


def flat(ref):
    return ref[...].reshape(ref.shape[0] * ref.shape[1], ref.shape[2])


def normalised(value):
    return lax.rsqrt(jnp.mean(value * value, axis=1, keepdims=True) + EPS)


def project_kernel(nblocks, starts_ref, x_ref, gain_ref, cos_ref, sin_ref, *refs):
    blocks, (n_ref, out_ref) = refs[:nblocks], refs[nblocks:]
    nrow, cut = blocks[0].shape[0], blocks[0].shape[1]
    width = x_ref.shape[1]
    x = x_ref[...].astype(F32)
    n_ref[...] = (x * normalised(x) * gain_ref[...]).astype(BF16)
    normed = ordered(n_ref, starts_ref, 0, nrow, cut)
    cos, sin = cos_ref[...], sin_ref[...]
    turn = lambda v: (v * cos + swap_halves(v) * sin).astype(BF16)
    for k, block in enumerate(blocks):
        raw = dot_nn(normed, flat(block))
        start = pl.multiple_of(starts_ref[nrow + k], 256)
        out_ref[:, pl.ds(start, 256)] = jnp.concatenate(
            [turn(raw[:, :128]), turn(raw[:, 128:256])], axis=1
        )
        start = pl.multiple_of(starts_ref[nrow + k] + width, 256)
        out_ref[:, pl.ds(start, 256)] = jnp.concatenate(
            [turn(raw[:, 256:384]), raw[:, 384:].astype(BF16)], axis=1
        )


def close_kernel(nblocks, starts_ref, x_ref, mixed_ref, gain_ref, *refs):
    blocks, (second_ref, n_ref, wide_ref) = refs[:nblocks], refs[nblocks:]
    nrow, cut = blocks[0].shape[0], blocks[0].shape[2]
    wide_ref[...] = mixed_ref[...].astype(BF16)
    mixed = ordered(wide_ref, starts_ref, nrow, nblocks, 256)
    for j in range(nrow):
        weight = jnp.concatenate([block[j] for block in blocks], axis=0)
        lanes = pl.ds(pl.multiple_of(starts_ref[j], cut), cut)
        second_ref[:, lanes] = x_ref[:, lanes].astype(F32) + dot_nn(mixed, weight)
    second = second_ref[...].astype(BF16).astype(F32)
    n_ref[...] = (second * normalised(second) * gain_ref[...]).astype(BF16)


def norm_back(grad, value, gain):
    rho = normalised(value)
    scaled = grad * gain
    inner = jnp.sum(scaled * value, axis=1, keepdims=True)
    out = rho * scaled - value * (rho * rho * rho) * (inner / value.shape[1])
    return out, jnp.sum(grad * value * rho, axis=0, keepdims=True)


def open_back_kernel(nblocks, starts_ref, grad_ref, dn_ref, second_ref, gain_ref, *refs):
    blocks, (dsecond_ref, dbranch_ref, dmixed_ref, dgain_ref) = refs[:nblocks], refs[nblocks:]
    nrow, cut = blocks[0].shape[0], blocks[0].shape[2]
    second = second_ref[...].astype(BF16).astype(F32)
    dnorm, dgain_ref[...] = norm_back(dn_ref[...], second, gain_ref[...])
    dsecond = grad_ref[...].astype(F32) + dnorm
    dsecond_ref[...] = dsecond
    dbranch_ref[...] = dsecond.astype(BF16)
    for k, block in enumerate(blocks):
        total = None
        for j in range(nrow):
            lanes = pl.ds(pl.multiple_of(starts_ref[j], cut), cut)
            term = dot_nt(dbranch_ref[:, lanes], block[j])
            total = term if total is None else total + term
        start = pl.multiple_of(starts_ref[nrow + k], 256)
        dmixed_ref[:, pl.ds(start, 256)] = total.astype(BF16)


def project_back_kernel(nblocks, starts_ref, dq_ref, dkv_ref, x_ref, gain_ref, dsecond_ref, *refs):
    blocks, (dx_ref, dgain_ref, wide_ref) = refs[:nblocks], refs[nblocks:]
    nrow, cut = blocks[0].shape[0], blocks[0].shape[1]
    total = None
    for k, block in enumerate(blocks):
        lanes = pl.ds(pl.multiple_of(starts_ref[nrow + k], 256), 256)
        grad = jnp.concatenate([dq_ref[:, lanes], dkv_ref[:, lanes]], axis=1)
        term = dot_nt(grad, flat(block))
        total = term if total is None else total + term
    for j in range(nrow):
        lanes = pl.ds(pl.multiple_of(starts_ref[j], cut), cut)
        wide_ref[:, lanes] = total[:, j * cut : (j + 1) * cut]
    dnorm, dgain_ref[...] = norm_back(wide_ref[...], x_ref[...].astype(F32), gain_ref[...])
    dx_ref[...] = (dsecond_ref[...] + dnorm).astype(BF16)


def weight_back_kernel(nblocks, starts_ref, n_ref, dq_ref, dkv_ref, mixed_ref, dbranch_ref, *refs):
    qkvs, outs = refs[:nblocks], refs[nblocks : 2 * nblocks]
    nrow, cut = qkvs[0].shape[0], qkvs[0].shape[1]
    normed = ordered(n_ref, starts_ref, 0, nrow, cut)
    for k in range(nblocks):
        lanes = pl.ds(pl.multiple_of(starts_ref[nrow + k], 256), 256)
        grad = jnp.concatenate([dq_ref[:, lanes], dkv_ref[:, lanes]], axis=1)
        qkvs[k][...] = dot_tn(normed, grad).astype(BF16).reshape(qkvs[k].shape)
        mixed = mixed_ref[:, lanes].astype(BF16)
        for j in range(nrow):
            there = pl.ds(pl.multiple_of(starts_ref[j], cut), cut)
            outs[k][j] = dot_tn(mixed, dbranch_ref[:, there]).astype(BF16)


def whole_call(kernel, out_shape, starts, operands, blocks, lanes, scratch=(), flops=0, ready=()):
    start, count = lanes
    specs = [pl.BlockSpec(memory_space=pltpu.SMEM)]
    specs += [pl.BlockSpec(memory_space=pltpu.VMEM) for _ in operands]
    specs += [
        pl.BlockSpec((*b.shape[:2], count), lambda i: (0, 0, start // count)) for b in blocks
    ]
    specs[1 : 1 + len(operands)] = [
        pl.BlockSpec(o.shape, lambda i, n=o.ndim: (0,) * n) for o in operands
    ]
    specs = [pl.BlockSpec(memory_space=pl.ANY) for _ in ready] + specs
    return pl.pallas_call(
        behind(functools.partial(kernel, len(blocks)), len(ready)),
        grid=(1,),
        in_specs=specs,
        out_specs=[pl.BlockSpec(o.shape, lambda i, n=len(o.shape): (0,) * n) for o in out_shape],
        out_shape=out_shape,
        scratch_shapes=scratch,
        compiler_params=pltpu.CompilerParams(vmem_limit_bytes=VMEM_LIMIT),
        cost_estimate=pl.CostEstimate(
            flops=flops,
            bytes_accessed=8 * 1024 * 1024,
            transcendentals=0,
        ),
    )(*ready, starts, *operands, *blocks)


def project(x, gain, cos, sin, part):
    rows, width = x.shape
    shapes = [
        jax.ShapeDtypeStruct((rows, width), BF16),
        jax.ShapeDtypeStruct((rows, 2 * width), BF16),
    ]
    return whole_call(
        project_kernel, shapes, part["starts"], (x, gain, cos, sin), part["qkv"], (0, 512),
        flops=4 * rows * width * width,
    )


def close_attention(x, mixed, gain, part):
    rows, width = x.shape
    shapes = [jax.ShapeDtypeStruct((rows, width), F32), jax.ShapeDtypeStruct((rows, width), BF16)]
    return whole_call(
        close_kernel, shapes, part["starts"], (x, mixed, gain), part["out"], part["out_lanes"],
        [pltpu.VMEM((rows, width), BF16)], 2 * rows * width * width,
    )


def open_back(grad, dn, second, gain, part):
    rows, width = grad.shape
    shapes = [
        jax.ShapeDtypeStruct((rows, width), F32),
        jax.ShapeDtypeStruct((rows, width), BF16),
        jax.ShapeDtypeStruct((rows, width), BF16),
        jax.ShapeDtypeStruct((1, width), F32),
    ]
    return whole_call(
        open_back_kernel, shapes, part["starts"], (grad, dn, second, gain), part["out"],
        part["out_lanes"], flops=2 * rows * width * width,
    )


def project_back(dq, dkv, x, gain, dsecond, part, ready):
    rows, width = x.shape
    shapes = [jax.ShapeDtypeStruct((rows, width), BF16), jax.ShapeDtypeStruct((1, width), F32)]
    return whole_call(
        project_back_kernel, shapes, part["starts"], (dq, dkv, x, gain, dsecond), part["qkv"],
        (0, 512), [pltpu.VMEM((rows, width), F32)], 4 * rows * width * width, ready,
    )


def weight_back(normed, dq, dkv, mixed, dbranch, part, ready=()):
    rows, width = normed.shape
    nblocks = len(part["qkv"])
    nrow, cut = part["qkv"][0].shape[:2]
    shapes = [jax.ShapeDtypeStruct((nrow, cut, 512), BF16)] * nblocks
    shapes += [jax.ShapeDtypeStruct((nrow, 256, width // nrow), BF16)] * nblocks
    operands = (normed, dq, dkv, mixed, dbranch)
    grads = pl.pallas_call(
        behind(functools.partial(weight_back_kernel, nblocks), len(ready)),
        in_specs=[pl.BlockSpec(memory_space=pl.ANY)] * len(ready)
        + [pl.BlockSpec(memory_space=pltpu.SMEM)]
        + [pl.BlockSpec(memory_space=pltpu.VMEM)] * len(operands),
        out_specs=[pl.BlockSpec(memory_space=pltpu.VMEM)] * len(shapes),
        out_shape=shapes,
        compiler_params=pltpu.CompilerParams(vmem_limit_bytes=VMEM_LIMIT),
        cost_estimate=pl.CostEstimate(
            flops=6 * rows * width * width, bytes_accessed=8 * 1024 * 1024, transcendentals=0
        ),
    )(*ready, part["starts_back"], *operands)
    return grads[:nblocks], grads[nblocks:]


def stack_heads(value):
    low = (lax.broadcasted_iota(jnp.int32, (value.shape[0], 128), 1) < HEAD).astype(F32)
    first, second = value[:, :128].astype(F32), value[:, 128:].astype(F32)
    return jnp.concatenate(
        [first * low, second * low, first * (1.0 - low), second * (1.0 - low)], axis=0
    )


def unstack_heads(value):
    rows = value.shape[0] // 4
    low = lax.broadcasted_iota(jnp.int32, (rows, 128), 1) < HEAD
    first = jnp.where(low, value[:rows], value[2 * rows : 3 * rows])
    second = jnp.where(low, value[rows : 2 * rows], value[3 * rows :])
    return first, second


def attend_kernel(q_ref, k_ref, v_ref, bias_ref, o_ref, lse_ref):
    stacked = (stack_heads(q_ref[0]) * HEAD**-0.5).astype(BF16)
    scores = dot_nt(k_ref[0], stacked) + bias_ref[...]
    top = jnp.max(scores, axis=0, keepdims=True)
    weights = jnp.exp(scores - top)
    total = jnp.sum(weights, axis=0, keepdims=True)
    mixed = dot_tn(v_ref[0], weights.astype(BF16)) / total
    first, second = unstack_heads(mixed.T)
    o_ref[0, :, :128] = first
    o_ref[0, :, 128:] = second
    lse_ref[0, 0] = top + jnp.log(total)


def attend(qkv, kv, bias):
    micro, rows, _ = qkv.shape
    keys, width = kv.shape[1], kv.shape[2]
    groups = width // 256
    return pl.pallas_call(
        attend_kernel,
        grid=(micro, groups),
        in_specs=[
            pl.BlockSpec((1, rows, 256), lambda m, g: (m, 0, g)),
            pl.BlockSpec((1, keys, 128), lambda m, g: (m, 0, 2 * g)),
            pl.BlockSpec((1, keys, 128), lambda m, g: (m, 0, 2 * g + 1)),
            pl.BlockSpec((keys, 4 * rows), lambda m, g: (0, 0)),
        ],
        out_specs=[
            pl.BlockSpec((1, rows, 256), lambda m, g: (m, 0, g)),
            pl.BlockSpec((1, 1, 1, 4 * rows), lambda m, g: (m, g, 0, 0)),
        ],
        out_shape=[
            jax.ShapeDtypeStruct((micro, rows, groups * 256), F32),
            jax.ShapeDtypeStruct((micro, groups, 1, 4 * rows), F32),
        ],
        compiler_params=pltpu.CompilerParams(vmem_limit_bytes=VMEM_LIMIT),
        cost_estimate=pl.CostEstimate(
            flops=micro * groups * 4 * rows * keys * 128 * 4,
            bytes_accessed=2 * micro * keys * width + 4 * keys * 4 * rows,
            transcendentals=micro * groups * 4 * rows * keys,
        ),
    )(qkv, kv, kv, bias)


def attend_back_kernel(
    q_ref, k_ref, v_ref, bias_ref, do_ref, o_ref, lse_ref, cos_ref, sin_ref, kcos_ref, ksin_ref,
    dq_ref, dkv_ref,
):
    scale = HEAD**-0.5
    queries = (stack_heads(q_ref[0]) * scale).astype(BF16)
    grads_wide = stack_heads(do_ref[0])
    product = grads_wide * stack_heads(o_ref[0])
    delta = jnp.sum(product.T, axis=0, keepdims=True)
    grads = grads_wide.astype(BF16)
    keys, values = k_ref[0], v_ref[0]
    probs = jnp.exp(dot_nt(keys, queries) + bias_ref[...] - lse_ref[0, 0])
    dvalues = dot_nn(probs.astype(BF16), grads)
    dscores = (probs * (dot_nt(values, grads) - delta)).astype(BF16)
    dkeys = dot_nn(dscores, queries)
    dqueries = dot_tn(keys, dscores) * scale
    first, second = unstack_heads(dqueries.T)
    cos, sin = cos_ref[...], sin_ref[...]
    dq_ref[0, :, :128] = (first * cos - swap_halves(first) * sin).astype(BF16)
    dq_ref[0, :, 128:] = (second * cos - swap_halves(second) * sin).astype(BF16)
    dkv_ref[0, :, :128] = (dkeys * kcos_ref[...] - swap_halves(dkeys) * ksin_ref[...]).astype(BF16)
    dkv_ref[0, :, 128:] = dvalues.astype(BF16)


def attend_back(qkv, kv, bias, grad, o, lse, cos, sin, kcos, ksin):
    micro, rows, _ = qkv.shape
    keys, width = kv.shape[1], kv.shape[2]
    groups = width // 256
    mine = pl.BlockSpec((1, rows, 256), lambda m, g: (m, 0, g))
    return pl.pallas_call(
        attend_back_kernel,
        grid=(micro, groups),
        in_specs=[
            mine,
            pl.BlockSpec((1, keys, 128), lambda m, g: (m, 0, 2 * g)),
            pl.BlockSpec((1, keys, 128), lambda m, g: (m, 0, 2 * g + 1)),
            pl.BlockSpec((keys, 4 * rows), lambda m, g: (0, 0)),
            mine,
            mine,
            pl.BlockSpec((1, 1, 1, 4 * rows), lambda m, g: (m, g, 0, 0)),
            pl.BlockSpec((rows, 128), lambda m, g: (0, 0)),
            pl.BlockSpec((rows, 128), lambda m, g: (0, 0)),
            pl.BlockSpec((keys, 128), lambda m, g: (0, 0)),
            pl.BlockSpec((keys, 128), lambda m, g: (0, 0)),
        ],
        out_specs=[mine, pl.BlockSpec((1, keys, 256), lambda m, g: (m, 0, g))],
        out_shape=[
            jax.ShapeDtypeStruct((micro, rows, groups * 256), BF16),
            jax.ShapeDtypeStruct((micro, keys, width), BF16),
        ],
        compiler_params=pltpu.CompilerParams(vmem_limit_bytes=VMEM_LIMIT),
        cost_estimate=pl.CostEstimate(
            flops=micro * groups * 4 * rows * keys * 128 * 10,
            bytes_accessed=4 * micro * keys * width + 4 * keys * 4 * rows,
            transcendentals=micro * groups * 4 * rows * keys,
        ),
    )(qkv, kv, kv, bias, grad, o, lse, cos, sin, kcos, ksin)


def chosen_rows(place_ref, m, cap, tokens):
    slots = lax.broadcasted_iota(jnp.int32, (cap, tokens), 0)
    return jnp.where(slots == place_ref[0, m : m + 1, :], 1.0, 0.0).astype(BF16)


def slot_weights(pick, weight_ref, m):
    return jnp.sum(pick.astype(F32) * weight_ref[0, m : m + 1, :], axis=1, keepdims=True)


def load_tokens(pieces, scratch):
    for at, piece in enumerate(pieces):
        rows = piece.shape[1]
        scratch[:, at * rows : (at + 1) * rows, :] = piece[...]


def store_tokens(out_ref, total):
    blocks, _, rows, _ = out_ref.shape
    for at in range(blocks):
        out_ref[at] = total[:, at * rows : (at + 1) * rows, :].astype(BF16)


def by_load(counts_ref, body, empty=None):
    e = pl.program_id(0)
    most = jnp.maximum(counts_ref[2 * e], counts_ref[2 * e + 1])
    below = 0
    for cap in (CAP // 3, 2 * CAP // 3, CAP):
        pl.when((most > below) & (most <= cap))(functools.partial(body, cap))
        below = cap
    if empty is not None:
        pl.when(most == 0)(empty)


def expert_call(kernel, local, operands, specs, outs, scratch, flops, moved, ready=()):
    def spec(shape, own):
        zeros = (0,) * (len(shape) - 1)
        if own is not False:
            return pl.BlockSpec((1, *shape[1:]), lambda e: (e + int(own) - 1, *zeros))
        return pl.BlockSpec(shape, lambda e: (0, *zeros))

    return pl.pallas_call(
        behind(kernel, len(ready)),
        grid=(local,),
        in_specs=[pl.BlockSpec(memory_space=pl.ANY) for _ in ready]
        + [
            pl.BlockSpec(memory_space=pltpu.SMEM) if own is None else spec(o.shape, own)
            for o, own in zip(operands, specs)
        ],
        out_specs=[spec(shape, own) for shape, own in outs],
        out_shape=[jax.ShapeDtypeStruct(shape, BF16) for shape, _ in outs],
        scratch_shapes=scratch,
        compiler_params=pltpu.CompilerParams(vmem_limit_bytes=VMEM_LIMIT),
        cost_estimate=pl.CostEstimate(flops=flops, bytes_accessed=moved, transcendentals=0),
    )(*ready, *operands)


def expert_hidden_kernel(ncol, counts_ref, place_ref, *refs):
    pieces, refs = refs[:ncol], refs[ncol:]
    gate_ref, up_ref, chosen_ref, hidden_ref, active_ref, tokens_ref, rows_ref = refs
    micro, tokens, _ = tokens_ref.shape
    hidden = gate_ref.shape[2]

    @pl.when(pl.program_id(0) == 0)
    def _():
        load_tokens(pieces, tokens_ref)

    def body(cap):
        for m in range(micro):
            chosen = dot_nn(chosen_rows(place_ref, m, cap, tokens), tokens_ref[m]).astype(BF16)
            rows_ref[m * cap : (m + 1) * cap, :] = chosen
            chosen_ref[0, m, :cap, :] = chosen
        gate = dot_nn(rows_ref[: micro * cap, :], gate_ref[0])
        up = dot_nn(rows_ref[: micro * cap, :], up_ref[0])
        active = (gate * jax.nn.sigmoid(gate) * up).astype(BF16)
        for m in range(micro):
            slots = slice(m * cap, (m + 1) * cap)
            hidden_ref[0, m, :cap, :hidden] = gate[slots].astype(BF16)
            hidden_ref[0, m, :cap, hidden:] = up[slots].astype(BF16)
            active_ref[0, m, :cap, :] = active[slots]

    by_load(counts_ref, body)


def expert_out_kernel(counts_ref, place_ref, weight_ref, active_ref, down_ref, y_ref, total_ref):
    micro, tokens, _ = total_ref.shape

    @pl.when(pl.program_id(0) == 0)
    def _():
        total_ref[...] = jnp.zeros_like(total_ref)

    def body(cap):
        active = jnp.concatenate([active_ref[0, m, :cap, :] for m in range(micro)], axis=0)
        out = dot_nn(active, down_ref[0])
        for m in range(micro):
            pick = chosen_rows(place_ref, m, cap, tokens)
            scaled = (out[m * cap : (m + 1) * cap] * slot_weights(pick, weight_ref, m)).astype(BF16)
            total_ref[m] += dot_tn(pick, scaled)

    by_load(counts_ref, body)

    @pl.when(pl.program_id(0) == pl.num_programs(0) - 1)
    def _():
        store_tokens(y_ref, total_ref)


def gate_and_up(weights, local):
    gate, up = weights[0], weights[-2]
    return gate, up, True, (local + 1 if len(weights) == 2 else True)


def experts(counts, place, weight, pieces, weights):
    micro, rows, width = pieces[0].shape
    local, hidden = place.shape[0], weights[0].shape[2]
    gate, up, at_gate, at_up = gate_and_up(weights, local)
    down = weights[-1]
    ncol = len(pieces)
    tokens = ncol * rows
    slots = local * micro * 256
    chosen, hid, active = expert_call(
        functools.partial(expert_hidden_kernel, ncol),
        local,
        (counts, place, *pieces, gate, up),
        (None, True, *[False] * ncol, at_gate, at_up),
        [
            ((local, micro, CAP, width), True),
            ((local, micro, CAP, 2 * hidden), True),
            ((local, micro, CAP, hidden), True),
        ],
        [pltpu.VMEM((micro, tokens, width), BF16), pltpu.VMEM((micro * CAP, width), BF16)],
        slots * width * (4 * hidden + 2 * tokens),
        local * width * (4 * hidden + 4 * micro * CAP),
    )
    (y,) = expert_call(
        expert_out_kernel,
        local,
        (counts, place, weight, active, down),
        (None, True, True, True, True),
        [((ncol, micro, rows, width), False)],
        [pltpu.VMEM((micro, tokens, width), F32)],
        slots * width * (2 * hidden + 2 * tokens),
        local * width * 2 * hidden + 4 * micro * tokens * width,
    )
    return y, chosen, hid


def expert_back_kernel(ncol, counts_ref, place_ref, weight_ref, *refs):
    pieces, refs = refs[:ncol], refs[ncol:]
    gate_ref, up_ref, down_ref, hidden_ref, dx_ref, dhidden_ref, ddown_ref, *refs = refs
    tokens_ref, total_ref, rows_ref = refs
    micro, tokens, _ = tokens_ref.shape
    hidden = down_ref.shape[1]

    @pl.when(pl.program_id(0) == 0)
    def _():
        load_tokens(pieces, tokens_ref)
        total_ref[...] = jnp.zeros_like(total_ref)

    def body(cap):
        picks = [chosen_rows(place_ref, m, cap, tokens) for m in range(micro)]
        for m in range(micro):
            grads = dot_nn(picks[m], tokens_ref[m]) * slot_weights(picks[m], weight_ref, m)
            rows_ref[m * cap : (m + 1) * cap, :] = grads.astype(BF16)
        used = micro * cap
        dactive = dot_nt(rows_ref[:used, :], down_ref[0])
        both = jnp.concatenate([hidden_ref[0, m, :cap, :] for m in range(micro)], axis=0)
        gate, up = both[:, :hidden].astype(F32), both[:, hidden:].astype(F32)
        sigmoid = jax.nn.sigmoid(gate)
        silu = gate * sigmoid
        dgate = (dactive * up * sigmoid * (1.0 + gate * (1.0 - sigmoid))).astype(BF16)
        dup = (dactive * silu).astype(BF16)
        for m in range(micro):
            dhidden_ref[0, m, :cap, :hidden] = dgate[m * cap : (m + 1) * cap]
            dhidden_ref[0, m, :cap, hidden:] = dup[m * cap : (m + 1) * cap]
        ddown_ref[0] = dot_tn((silu * up).astype(BF16), rows_ref[:used, :]).astype(BF16)
        out = (dot_nt(dgate, gate_ref[0]) + dot_nt(dup, up_ref[0])).astype(BF16)
        for m in range(micro):
            total_ref[m] += dot_tn(picks[m], out[m * cap : (m + 1) * cap])

    def empty():
        ddown_ref[...] = jnp.zeros_like(ddown_ref)

    by_load(counts_ref, body, empty)

    @pl.when(pl.program_id(0) == pl.num_programs(0) - 1)
    def _():
        store_tokens(dx_ref, total_ref)


def expert_weight_back_kernel(counts_ref, chosen_ref, dhidden_ref, dgate_ref, dup_ref):
    micro = chosen_ref.shape[1]
    hidden = dgate_ref.shape[2]
    outs = dgate_ref, dup_ref

    def body(cap):
        rows = jnp.concatenate([chosen_ref[0, m, :cap, :] for m in range(micro)], axis=0)
        both = jnp.concatenate([dhidden_ref[0, m, :cap, :] for m in range(micro)], axis=0)
        grads = dot_tn(rows, both).astype(BF16)
        dgate_ref[0] = grads[:, :hidden]
        dup_ref[0] = grads[:, hidden:]

    def empty():
        for out in outs:
            out[...] = jnp.zeros_like(out)

    by_load(counts_ref, body, empty)


def experts_back(counts, place, weight, pieces, weights, hid):
    micro, rows, width = pieces[0].shape
    local, hidden = place.shape[0], weights[0].shape[2]
    gate, up, at_gate, at_up = gate_and_up(weights, local)
    down = weights[-1]
    ncol = len(pieces)
    tokens = ncol * rows
    slots = local * micro * 256
    dx, dhid, ddown = expert_call(
        functools.partial(expert_back_kernel, ncol),
        local,
        (counts, place, weight, *pieces, gate, up, down, hid),
        (None, True, True, *[False] * ncol, at_gate, at_up, True, True),
        [
            ((ncol, micro, rows, width), False),
            ((local, micro, CAP, 2 * hidden), True),
            (down.shape, True),
        ],
        [
            pltpu.VMEM((micro, tokens, width), BF16),
            pltpu.VMEM((micro, tokens, width), F32),
            pltpu.VMEM((micro * CAP, width), BF16),
        ],
        slots * width * (8 * hidden + 4 * tokens),
        local * width * (8 * hidden + 2 * micro * CAP),
    )
    return dx, dhid, ddown


def expert_weights_back(counts, chosen, dhid, weights, ready):
    local, micro = chosen.shape[:2]
    width, hidden = weights[0].shape[1:]
    shapes = [(local, width, hidden)] * 2
    return expert_call(
        expert_weight_back_kernel,
        local,
        (counts, chosen, dhid),
        (None, True, True),
        [(shape, True) for shape in shapes],
        [],
        local * micro * 256 * width * 4 * hidden,
        local * width * (4 * hidden + 4 * micro * CAP),
        ready,
    )


def spread_rows(value):
    both = jnp.stack([value, exchange(value)])
    return gather_col(both)


def collect_rows(partial, begun=None):
    blocks = [partial[k] for k in range(partial.shape[0])]
    theirs = exchange(scatter_col([b[1] for b in blocks], begun).astype(BF16))
    return scatter_col([b[0] for b in blocks]) + theirs.astype(F32)


def forward_layer(layer_in, env, part):
    rows, width = layer_in.shape
    prompt = env["prompt"]
    normed, qkv = project(layer_in, part["gain_first"], env["cos"], env["sin"], part)
    own = qkv[:, width:]
    near = gather_col(own)
    far = gather_col(jnp.concatenate(gather_row(own[:prompt])[1:], axis=0))
    kv = jnp.concatenate([b for pair in zip(near, far) for b in pair], axis=0)
    mixed, lse = attend(qkv[None], kv[None], env["bias"])
    second, normed_second = close_attention(layer_in, mixed[0], part["gain_second"], part)
    pieces = spread_rows(normed_second)
    partial, chosen, hid = experts(*part["slots"], pieces, part["experts"])
    result = second + collect_rows(partial)
    keep = {
        "layer_in": layer_in,
        "normed": normed,
        "qkv": qkv,
        "kv": kv,
        "mixed": mixed,
        "lse": lse,
        "second": second,
        "chosen": chosen,
        "hid": hid,
    }
    return result, keep


def backward_layer(grad_result, pieces, keep, env, part, before_projections=None):
    rows, _ = grad_result.shape
    prompt = env["prompt"]
    ncol, nrow = lax.axis_size("col"), lax.axis_size("row")
    partial, dhid, ddown = experts_back(*part["slots"], pieces, part["experts"], keep["hid"])
    begun = []
    dn2 = collect_rows(partial, begun)
    dhidden = expert_weights_back(part["slots"][0], keep["chosen"], dhid, part["experts"], begun)
    dsecond, dbranch, dmixed, gain_second = open_back(
        grad_result, dn2, keep["second"], part["gain_second"], part
    )
    dq, dkv = attend_back(
        keep["qkv"][None], keep["kv"][None], env["bias"], dmixed[None], keep["mixed"],
        keep["lse"], env["cos"], env["sin"], env["kcos"], env["ksin"],
    )
    span = dkv.shape[1] // ncol
    own = scatter_col([dkv[0, k * span : (k + 1) * span] for k in range(ncol)])
    parts = [own[:prompt]]
    for j in range(1, nrow):
        at = rows + (j - 1) * prompt
        parts.append(own[at : at + prompt].astype(BF16))
    own = jnp.concatenate([scatter_row(parts), own[prompt:rows]], axis=0).astype(BF16)
    small = keep["normed"], dq[0], own, keep["mixed"][0], dbranch, part
    ready = ()
    if before_projections is not None:
        small = weight_back(*small)
        ready = (*before_projections, small[0][0])
    grad_in, gain_first = project_back(
        dq[0], own, keep["layer_in"], part["gain_first"], dsecond, part, ready
    )
    return grad_in, {
        "small": small,
        "experts": (*dhidden, ddown),
        "gain_first": gain_first[0],
        "gain_second": gain_second[0],
    }


def own_rows(value, prompt_rows):
    micro, _, shard = value.shape
    ncol = lax.axis_size("col")
    return jnp.concatenate(
        [
            value[:, :prompt_rows].reshape(micro, ncol, -1, shard),
            value[:, prompt_rows:].reshape(micro, ncol, -1, shard),
        ],
        axis=2,
    )


def to_rows(value, prompt_rows):
    split = own_rows(value, prompt_rows)
    return lax.all_to_all(split, "col", 1, 3, tiled=True)[:, 0]


def to_columns(value, prompt):
    micro, _, width = value.shape
    ncol, col = lax.axis_size("col"), lax.axis_index("col")
    shard = width // ncol
    blocks = []
    for k in range(ncol):
        block = lax.dynamic_slice_in_dim(value, (col ^ k) * shard, shard, 2)
        blocks.append(flip(block, k) if k else block)
    blocks = jnp.stack(blocks)
    blocks = [lax.dynamic_index_in_dim(blocks, col ^ c, 0, False) for c in range(ncol)]
    parts = [b[:, :prompt] for b in blocks] + [b[:, prompt:] for b in blocks]
    return jnp.concatenate(parts, axis=1)


def turn_tables(positions):
    half = HEAD // 2
    freqs = THETA ** (-(jnp.arange(half).astype(F32) * 2.0) / HEAD)
    angles = positions.astype(F32)[:, None] * freqs[None, :]
    cos, sin = jnp.cos(angles), jnp.sin(angles)
    return (
        jnp.concatenate([cos, cos, cos, cos], axis=1),
        jnp.concatenate([-sin, sin, -sin, sin], axis=1),
    )


def small_weights(rows, w_rows):
    nrow, cut = rows.shape[:2]
    ncol, row, col = lax.axis_size("col"), lax.axis_index("row"), lax.axis_index("col")
    index = jnp.arange(nrow, dtype=jnp.int32)
    blocks = gather_col(rows)

    def result(qkv, out, lanes, order):
        return {
            "starts": jnp.concatenate([index * cut, order]),
            "starts_back": jnp.concatenate([((row - index) % nrow) * cut, order]),
            "qkv": qkv,
            "out": out,
            "out_lanes": lanes,
        }

    if w_rows == 256:
        order = (col ^ jnp.arange(ncol, dtype=jnp.int32)) * 256
        return result(blocks, blocks, (512, 256), order)
    blocks = jnp.stack(blocks)
    whole = [lax.dynamic_index_in_dim(blocks, col ^ c, 0, False) for c in range(ncol)]
    qkv, out = [], []
    for a, b in zip(whole[::2], whole[1::2]):
        heads = [a[..., :64], b[..., :64], a[..., 64:128], b[..., 64:128]]
        others = [a[..., 128:192], b[..., 128:192], a[..., 192:256], b[..., 192:256]]
        qkv.append(jnp.concatenate(heads + others, axis=2))
        a, b = a[..., 256:], b[..., 256:]
        out.append(jnp.concatenate([a[:, :64], b[:, :64], a[:, 64:], b[:, 64:]], axis=1))
    return result(qkv, out, (0, cut), jnp.arange(len(qkv), dtype=jnp.int32) * 256)


def pack_weights(w_query, w_key, w_value, w_out):
    if w_out.shape[0] == 256:
        heads = lambda v: [v[..., :64], v[..., 128:192], v[..., 64:128], v[..., 192:]]
        rows = [w_out[:64], w_out[128:192], w_out[64:128], w_out[192:]]
        w_out = jnp.concatenate(rows, axis=0)
        w_query = jnp.concatenate(heads(w_query), axis=1)
    return jnp.concatenate([w_query, w_key, w_value, w_out], axis=1)


def col_gradients(qkv, out, w_rows, begun=None):
    ncol, col = lax.axis_size("col"), lax.axis_index("col")
    if w_rows == 256:
        blocks = [jnp.concatenate([a, b], axis=2) for a, b in zip(qkv, out)]
    else:
        whole = []
        for a, b in zip(qkv, out):
            for c in (0, 1):
                at = lambda i: a[..., 64 * i : 64 * i + 64]
                heads = [at(c), at(2 + c), at(4 + c), at(6 + c)]
                rows = jnp.concatenate(
                    [b[:, 64 * c : 64 * c + 64], b[:, 128 + 64 * c : 192 + 64 * c]], axis=1
                )
                whole.append(jnp.concatenate([*heads, rows], axis=2))
        whole = jnp.stack(whole)
        blocks = [lax.dynamic_index_in_dim(whole, col ^ k, 0, False) for k in range(ncol)]
    return scatter_col(blocks, begun).astype(BF16)


def routing(ids, scale, prompt_rows, first, local):
    ncol, col = lax.axis_size("col"), lax.axis_index("col")

    def mine(value):
        blocks = own_rows(value, prompt_rows)
        order = [lax.dynamic_index_in_dim(blocks, col ^ k, 1, False) for k in range(ncol)]
        return jnp.concatenate(order, axis=1).transpose(0, 2, 1)

    ids, scale = mine(ids), mine(scale)
    names = first + jnp.arange(local, dtype=jnp.int32)
    match = ids[None] == names[:, None, None, None]
    member = jnp.any(match, axis=2)
    weight = jnp.sum(jnp.where(match, scale[None], 0.0), axis=2)
    tokens = member.shape[2]
    order = jnp.arange(tokens, dtype=jnp.int32)
    earlier = (order[:, None] <= order[None, :]).astype(BF16)
    seen = dot_nn(member.astype(BF16).reshape(-1, tokens), earlier).astype(jnp.int32)
    seen = seen.reshape(member.shape)
    return seen[:, :, -1].reshape(-1), jnp.where(member, seen - 1, -1), weight


def on_device(
    x_in,
    targets,
    w_query,
    w_key,
    w_value,
    w_out,
    w_gate,
    w_up,
    w_down,
    gain_attn,
    gain_ffn,
    expert_ids,
    gates,
    lengths,
):
    section, row, col = (lax.axis_index(name) for name in ("section", "row", "col"))
    nrow, ncol = lax.axis_size("row"), lax.axis_size("col")
    micro, _, tokens, shard = x_in.shape
    width = shard * ncol
    prompt_rows = tokens - CONT_LEN
    prompt_len = prompt_rows * nrow
    prompt, cont = prompt_rows // ncol, CONT_LEN // ncol
    local = w_gate.shape[1]
    half = local // 2
    columns, kcols = w_query.shape[2], w_key.shape[2]
    home = [section == 0, section == 1]

    def by_layer(value):
        other = exchange(value)
        return [jnp.where(is_home, value, other) for is_home in home]

    w_rows = w_out.shape[1]
    packed = by_layer(pack_weights(w_query[0], w_key[0], w_value[0], w_out[0]))
    big = [w[0] for w in (w_gate, w_up, w_down)]
    over_row = lambda v: lax.all_gather(v, "row", axis=0)
    small_first = over_row(packed[0])
    crossed = [exchange(after(big[0][half:], packed[0]))]
    for w in big[1:]:
        crossed.append(exchange(after(w[half:], crossed[-1])))
    shards = [
        [jnp.where(is_home, w[:half], c) for w, c in zip(big, crossed)] for is_home in home
    ]
    gate, up, down = shards[1]
    shards[1] = [jnp.concatenate([gate, up], axis=0), down]
    ids_layer, gates_layer = by_layer(expert_ids[0, :, 0]), by_layer(gates[0, :, 0])
    gains = by_layer(jnp.concatenate([gain_attn, gain_ffn]).astype(F32))

    def whole(pieces):
        axes = (1,) * (len(pieces) - 1) + (2,)
        return [lax.all_gather(w, "row", axis=axis, tiled=True) for w, axis in zip(pieces, axes)]

    def layer_part(layer, held):
        own_first = lambda v: jnp.where(home[0], v, v[::-1])
        first = col * local + jnp.where(home[layer], 0, half)
        ids, scale = own_first(ids_layer[layer]), own_first(gates_layer[layer])
        return {
            "experts": held,
            "gain_first": gains[layer][:1],
            "gain_second": gains[layer][1:],
            "slots": routing(ids, scale, prompt_rows, first, half),
        }

    shards[0] = [after(w, small_first) for w in shards[0]]
    parts = [layer_part(0, whole(shards[0]))]
    parts[0].update(small_weights(small_first, w_rows))
    held = parts[0]["experts"]
    small_later = over_row(after(packed[1], held[0]))
    parts.append(layer_part(1, whole(lax.optimization_barrier((shards[1], held[2]))[0])))
    parts[1].update(small_weights(small_later, w_rows))

    def prompt_positions(row_index, col_index):
        return row_index * prompt_rows + col_index * prompt + jnp.arange(prompt, dtype=jnp.int32)

    def cont_positions(col_index):
        return prompt_len + col_index * cont + jnp.arange(cont, dtype=jnp.int32)

    positions = jnp.concatenate([prompt_positions(row, col), cont_positions(col)])
    key_positions = []
    for k in range(ncol):
        key_positions += [prompt_positions(row, col ^ k), cont_positions(col ^ k)]
        key_positions += [prompt_positions((row - j) % nrow, col ^ k) for j in range(1, nrow)]
    key_positions = jnp.concatenate(key_positions)
    bias = jnp.where(key_positions[:, None] <= jnp.tile(positions, GROUP)[None, :], 0.0, NEG)
    cos, sin = turn_tables(positions)
    kcos, ksin = turn_tables(key_positions)
    env = {"prompt": prompt, "cos": cos, "sin": sin, "kcos": kcos, "ksin": ksin, "bias": bias}

    mine = lambda v: lax.dynamic_index_in_dim(v, section, 0, keepdims=True)
    first_in = to_rows(mine(x_in[:, 0]), prompt_rows)[0]
    goal = to_rows(mine(targets[:, 0]), prompt_rows)[0].astype(F32)

    result, keep_first = forward_layer(first_in, env, parts[0])
    mid = result.astype(BF16)
    final, keep_last = forward_layer(mid, env, parts[1])

    count = (micro * prompt_len + jnp.sum(lengths)).astype(F32)
    length = lengths[section, row]
    valid = (positions - prompt_len < length).astype(F32)[:, None]
    diff = (final - goal) * valid
    loss = jnp.sum(diff * diff) / count
    dfinal = (2.0 / count) * diff

    def both_micros(first, last):
        received = exchange(jnp.where(home[0], last, first))
        pair = jnp.where(home[0], jnp.stack([first, received]), jnp.stack([received, last]))
        return to_columns(pair, prompt)

    outputs = both_micros(mid, final.astype(BF16))
    dfinal_pieces = spread_rows(dfinal.astype(BF16))
    dmid, last_grads = backward_layer(dfinal, dfinal_pieces, keep_last, env, parts[1])
    dmid_pieces = spread_rows(dmid)
    small_last = col_gradients(*weight_back(*last_grads["small"], dmid_pieces[-1:]), w_rows)
    small_last = small_last, shift(small_last, "section", [(0, 1)])
    dx, first_grads = backward_layer(dmid, dmid_pieces, keep_first, env, parts[0], small_last)

    layer_grads = [first_grads, last_grads]

    def over_rows(j, layer, *earlier):
        grad = after(layer_grads[layer]["experts"][j], *earlier)
        return lax.psum_scatter(grad, "row", scatter_dimension=(1, 1, 2)[j], tiled=True)

    order = (2, 0, 1)
    sums_last = [over_rows(j, 1) for j in order]
    back_last = [shift(g, "section", [(0, 1)]) for g in sums_last]
    sums_first = [over_rows(j, 0, back) for j, back in zip(order, back_last)]
    back_first = [shift(g, "section", [(1, 0)]) for g in sums_first[:2]]
    small_first = col_gradients(*first_grads["small"], w_rows)
    small = [None] * nrow
    for j in (*range(1, nrow), 0):
        pair = small_first[j], shift(small_first[j], "section", [(1, 0)])
        first, last = (a.astype(F32) + b.astype(F32) for a, b in (pair, (small_last[0][j], small_last[1][j])))
        small[j] = jnp.where(home[0], first, last).astype(BF16)
    small[0] = needing(small[0], back_first[0])
    small = scatter_row(small)
    back_first.append(shift(sums_first[2], "section", [(1, 0)]))

    def expert_gradient(j):
        at = order.index(j)
        own = jnp.where(home[0], sums_first[at], sums_last[at])
        other = jnp.where(home[0], back_first[at], back_last[at])
        return jnp.concatenate([own, other], axis=0).astype(F32)

    grad_gate, grad_up, grad_down = (expert_gradient(j) for j in range(3))
    grad_query, grad_out = small[:, :columns], small[:, columns + 2 * kcols :]
    if w_rows == 256:
        heads = lambda v: [v[:, :64], v[:, 128:192], v[:, 64:128], v[:, 192:]]
        grad_query = jnp.concatenate(heads(grad_query), axis=1)
        grad_out = jnp.concatenate(
            [grad_out[:64], grad_out[128:192], grad_out[64:128], grad_out[192:]], axis=0
        )
    tally = jnp.concatenate(
        [g[name] for g in layer_grads for name in ("gain_first", "gain_second")]
        + [jnp.broadcast_to(loss, (128,))]
    )
    tally = total_everywhere(tally)
    loss = tally[4 * width]
    gains = tally[: 4 * width].reshape(2, 2, width)
    gains = jnp.where(home[0], gains[0], gains[1])
    gains = lax.dynamic_slice_in_dim(gains, col * shard, shard, 1)

    input_grads = both_micros(dx, dmid)
    return (
        outputs[None, :, None],
        loss,
        input_grads[None, :, None],
        grad_query[None],
        small[None, :, columns : columns + kcols],
        small[None, :, columns + kcols : columns + 2 * kcols],
        grad_out[None],
        grad_gate[None],
        grad_up[None],
        grad_down[None],
        gains[:1],
        gains[1:],
    )


def solution(mesh):
    in_specs = (
        P(None, "row", None, "col"),
        P(None, "row", None, "col"),
        P("section", "row", "col"),
        P("section", "row", "col"),
        P("section", "row", "col"),
        P("section", "col", "row"),
        P("section", "col", "row", None),
        P("section", "col", "row", None),
        P("section", "col", None, "row"),
        P("section", None),
        P("section", None),
        P("section", None, "row", None, None),
        P("section", None, "row", None, None),
        P(),
    )
    out_specs = (
        P("section", None, "row", None, "col"),
        P(),
        P("section", None, "row", None, "col"),
        P("section", "row", "col"),
        P("section", "row", "col"),
        P("section", "row", "col"),
        P("section", "col", "row"),
        P("section", "col", "row", None),
        P("section", "col", "row", None),
        P("section", "col", None, "row"),
        P("section", "col"),
        P("section", "col"),
    )
    return jax.shard_map(
        on_device, mesh=mesh, in_specs=in_specs, out_specs=out_specs, check_vma=False
    )
```
